128 devices in a mesh: row: 32 (over x, z_lo, y), col: 4 (over z_hi, core).
Axes of the slice: x: 4, y: 4, z: 4 (z_hi: 2, z_lo: 2; z = z_hi * 2 + z_lo), core: 2. Of those that a mesh axis runs over, the one named last changes fastest.
Arguments:
- vectors: float32 [2, 131072, 1024], P(None, ('row', 'col')), may hold values from -6 to 6
- panel_store: float32 [2, 2, 131072, 256], P(None, None, ('row', 'col')), may hold values from -0.015625 to 0.015625
- block_ids: int32 [2, 16384], P(None, ('row', 'col')), may hold values from 0 to 16383, as said below
- offsets: int32 [2], replicated, may hold values from 0 to 16383
- tri_factors: float32 [2, 2, 256, 256], replicated, may hold values from -6 to 6
Outputs:
- transformed: float32 [2, 131072, 1024], P(None, ('row', 'col'))
The draws below stay inside these ranges and needn't reach their ends.
Inputs may be any that keep to these rules, and one draw needn't show every extreme that they name: `block_ids`: for each panel the ids are a permutation of the 16384 row blocks; list slot t of the shard held by any device (t counted within that shard, 0 to 127) holds a block of strip t, that is an id g with g // 128 equal to t.
All inputs are finite; a program needn't handle non-finite values.
Results may differ from the reference program's by a relative error of at most 0.0003.
Values sent between devices are 32-bit elements; how exact they have to be, the bound alone decides.
A program may use at most 192 MiB of HBM per device.

```python
import jax
import jax.numpy as jnp
from jax import lax

N = 131072
W = 256
K = 1024
BR = 8
PANELS = 2
STRIPS = 128
BLOCKS = 16384
STRIP_BLOCKS = 128


def draw_block_ids(key, part):
    key = jax.random.fold_in(key, 7)
    per_source = STRIP_BLOCKS // STRIPS
    keys = jax.random.split(key, PANELS * STRIPS)
    shuffled = jax.vmap(lambda single: jax.random.permutation(single, STRIP_BLOCKS))(keys)
    shuffled = shuffled.reshape(PANELS, STRIPS, STRIPS, per_source)
    strip_start = (jnp.arange(STRIPS, dtype=jnp.int32) * STRIP_BLOCKS)[None, :, None, None]
    global_ids = shuffled.astype(jnp.int32) + strip_start
    global_ids = jnp.transpose(global_ids, (0, 2, 1, 3))
    return global_ids.reshape(PANELS, BLOCKS).astype(jnp.int32)


def block_levels(stream_key, shape, cuts, least, largest):
    loudness = 1.0
    for dim, parts in cuts:
        draws = jax.random.uniform(jax.random.fold_in(jax.random.fold_in(stream_key, 6), dim), (parts,), jnp.float32, least / len(cuts), largest / len(cuts))
        loudness = loudness * jnp.repeat(jnp.exp(draws), shape[dim] // parts).reshape((-1,) + (1,) * (len(shape) - 1 - dim))
    return loudness


def gaussian(rng, extent, deviation, bound, pieces=(), kind=jnp.bfloat16):
    drawn = deviation * jax.random.normal(rng, extent, jnp.float32)
    if pieces:
        drawn = drawn * block_levels(rng, extent, pieces, -0.22, 0.18)
    return jnp.clip(drawn, -bound, bound).astype(kind)


def setup_inputs(seed: int = 0) -> dict:
    arg_keys = jax.random.split(jax.random.key(seed), 6)
    return {
        "vectors": gaussian(arg_keys[0], (2, N, K), 1.0, 6.0, ((1, 128),), jnp.float32),
        "panel_store": gaussian(arg_keys[1], (PANELS, 2, N, W), N ** -0.5, 0.015625, ((2, 128),), jnp.float32),
        "block_ids": draw_block_ids(jax.random.fold_in(arg_keys[5], 71), 0),
        "offsets": jax.random.randint(arg_keys[3], (PANELS,), 0, N // 8).astype(jnp.int32),
        "tri_factors": gaussian(arg_keys[4], (PANELS, 2, W, W), ((2 * N) ** 0.5 / W), 6.0, (), jnp.float32),
    }


highest = lax.Precision.HIGHEST


def contract(first_op, second_op):
    return lax.dot_general(first_op, second_op, (((0,), (0,)), ((), ())), precision=highest, preferred_element_type=jnp.float32)


def matmul(first_op, second_op):
    return jnp.dot(first_op, second_op, precision=highest, preferred_element_type=jnp.float32)


def adjoint_times(first_op, second_op):
    real_part = contract(first_op[0], second_op[0]) + contract(first_op[1], second_op[1])
    imag_part = contract(first_op[0], second_op[1]) - contract(first_op[1], second_op[0])
    return jnp.stack([real_part, imag_part])


def complex_times(first_op, second_op):
    real_part = matmul(first_op[0], second_op[0]) - matmul(first_op[1], second_op[1])
    imag_part = matmul(first_op[0], second_op[1]) + matmul(first_op[1], second_op[0])
    return jnp.stack([real_part, imag_part])


def adjoint_upper(factor):
    upper_part = jnp.triu(factor)
    return jnp.stack([upper_part[0].T, -upper_part[1].T])


def mask_panel(values, first_row, offset):
    row_count = values.shape[1]
    col_count = values.shape[2]
    row_index = first_row + jnp.arange(row_count, dtype=jnp.int32)[:, None]
    limit = offset + jnp.arange(col_count, dtype=jnp.int32)[None, :]
    below = row_index > limit
    diagonal = row_index == limit
    real_part = jnp.where(below, values[0], jnp.where(diagonal, jnp.ones_like(values[0]), jnp.zeros_like(values[0])))
    imag_part = jnp.where(below, values[1], jnp.zeros_like(values[1]))
    return jnp.stack([real_part, imag_part])


def reference(vectors, panel_store, block_ids, offsets, tri_factors):
    current = vectors
    for panel in range(PANELS):
        blocks = panel_store[panel].reshape(2, BLOCKS, BR, W)
        ordering = jnp.argsort(block_ids[panel])
        placed = blocks[:, ordering].reshape(2, N, W)
        householder = mask_panel(placed, jnp.int32(0), offsets[panel])
        summed = adjoint_times(householder, current)
        update = complex_times(adjoint_upper(tri_factors[panel]), summed)
        current = current - complex_times(householder, update)
    return current
```

```python
import functools

import jax
import jax.numpy as jnp
from jax import lax
from jax.experimental import pallas as pl
from jax.experimental.pallas import tpu as pltpu
from jax.sharding import PartitionSpec as P


MESH = pl.DeviceIdType.MESH


def strip_of(x, y, z, core):
    return ((x * 2 + z % 2) * 4 + y) * 4 + (z // 2) * 2 + core


def exchange_kernel(rows, store_ref, ids_ref, blocks_ref, ids_out_ref, send_sem, recv_sem, id_send_sem, id_recv_sem, own_sem):
    row = lax.axis_index("row")
    col = lax.axis_index("col")
    me = row * 4 + col
    x = row // 8
    y = row % 4
    z = (col // 2) * 2 + (row // 4) % 2
    core = col % 2

    barrier = pltpu.get_barrier_semaphore()

    def greet(step, carry):
        peer = (me + step) % 128
        pl.semaphore_signal(barrier, inc=1, device_id=(peer // 4, peer % 4), device_id_type=MESH)
        return carry

    lax.fori_loop(1, 128, greet, 0)
    own_blocks = pltpu.make_async_copy(
        store_ref.at[:, :, pl.ds(pl.multiple_of(me * rows, rows), rows), :], blocks_ref.at[me], own_sem.at[0]
    )
    own_ids = pltpu.make_async_copy(ids_ref, ids_out_ref.at[me], own_sem.at[1])
    own_blocks.start()
    own_ids.start()
    pl.semaphore_wait(barrier, 127)

    def peer_of(step):
        spread = (step // 2 * 27) % 64
        return strip_of(
            (x + spread % 4) % 4, (y + (spread // 4) % 4) % 4, (z + spread // 16) % 4, (core + step) % 2
        )

    def copies(target, source):
        device = (target // 4, target % 4)
        return (
            pltpu.make_async_remote_copy(
                store_ref.at[:, :, pl.ds(pl.multiple_of(target * rows, rows), rows), :],
                blocks_ref.at[source],
                send_sem.at[target],
                recv_sem.at[source],
                device_id=device,
                device_id_type=MESH,
            ),
            pltpu.make_async_remote_copy(
                ids_ref,
                ids_out_ref.at[source],
                id_send_sem.at[target],
                id_recv_sem.at[source],
                device_id=device,
                device_id_type=MESH,
            ),
        )

    def send(step, carry):
        for copy in copies(peer_of(step), me):
            copy.start()
        return carry

    lax.fori_loop(1, 128, send, 0)
    own_blocks.wait()
    own_ids.wait()

    def finish(step, carry):
        peer = (me + step) % 128
        for copy in copies(peer, peer):
            copy.wait_recv()
            copy.wait_send()
        return carry

    lax.fori_loop(1, 128, finish, 0)


def exchange(panel_store, block_ids):
    panel_count, parts, row_count, col_width = panel_store.shape
    slot_count = block_ids.shape[1]
    rows = row_count // slot_count
    return pl.pallas_call(
        functools.partial(exchange_kernel, rows),
        out_shape=(
            jax.ShapeDtypeStruct((slot_count, panel_count, parts, rows, col_width), jnp.float32),
            jax.ShapeDtypeStruct((slot_count, panel_count, slot_count), jnp.int32),
        ),
        in_specs=[pl.BlockSpec(memory_space=pl.ANY)] * 2,
        out_specs=[pl.BlockSpec(memory_space=pl.ANY)] * 2,
        scratch_shapes=[
            pltpu.SemaphoreType.DMA((128,)),
            pltpu.SemaphoreType.DMA((128,)),
            pltpu.SemaphoreType.DMA((128,)),
            pltpu.SemaphoreType.DMA((128,)),
            pltpu.SemaphoreType.DMA((2,)),
        ],
        compiler_params=pltpu.CompilerParams(collective_id=0, has_side_effects=True),
        name="exchange",
    )(panel_store, block_ids)


VMEM_LIMIT = 60 * 1024 * 1024


def split(value):
    high = value.astype(jnp.bfloat16)
    return high, (value - high.astype(jnp.float32)).astype(jnp.bfloat16)


def dot(first_op, second_op):
    return jnp.dot(first_op, second_op, preferred_element_type=jnp.float32)


def split_dot(first_op, second_op):
    return (
        dot(first_op[0], second_op[0]) + dot(first_op[0], second_op[1]) + dot(first_op[1], second_op[0])
    )


def left_forms(real_part, imag_part):
    return split(real_part + imag_part), split(real_part), split(imag_part)


def right_forms(real_part, imag_part):
    return split(real_part), split(imag_part - real_part), split(real_part + imag_part)


def complex_dot(left, right):
    shared = split_dot(left[0], right[0])
    real_part = shared - split_dot(left[2], right[2])
    imag_part = shared + split_dot(left[1], right[1])
    return real_part, imag_part


def adjoint_upper(tri_ref, panel):
    shape = tri_ref.shape[2:]
    upper = lax.broadcasted_iota(jnp.int32, shape, 0) <= lax.broadcasted_iota(jnp.int32, shape, 1)
    return jnp.where(upper, tri_ref[panel, 0], 0.0).T, -jnp.where(upper, tri_ref[panel, 1], 0.0).T


def product_kernel(
    offsets_ref, ids_ref, blocks_ref, tri_ref, vectors_ref, y_ref, g_ref, x_ref, order_ref, slot_ref, panel_ref, left_ref, sem
):
    @pl.when(pl.program_id(0) == 0)
    def _():
        me = lax.axis_index("row") * 4 + lax.axis_index("col")
        source = lax.broadcasted_iota(jnp.int32, (128, 128), 0)
        lane = lax.broadcasted_iota(jnp.int32, (128, 128), 1)
        for panel in range(2):
            listed = jnp.sum(jnp.where(lane == me, ids_ref[:, panel, :], 0), axis=1, keepdims=True)
            place = listed - me * 128
            order_ref[panel : panel + 1, :] = jnp.sum(
                jnp.where(place == lane, source, 0), axis=0, keepdims=True
            )
        fetch = pltpu.make_async_copy(order_ref, slot_ref, sem)
        fetch.start()
        fetch.wait()

        def place_block(block, carry):
            first = pl.multiple_of(block * 8, 8)
            row_index = me * 1024 + block * 8 + lax.broadcasted_iota(jnp.int32, (8, 256), 0)
            for panel in range(2):
                slot = slot_ref[panel, block]
                limit = offsets_ref[panel] + lax.broadcasted_iota(jnp.int32, (8, 256), 1)
                below = row_index > limit
                diagonal = jnp.where(row_index == limit, 1.0, 0.0)
                panel_ref[0, panel, pl.ds(first, 8), :] = jnp.where(below, blocks_ref[slot, panel, 0], diagonal)
                panel_ref[1, panel, pl.ds(first, 8), :] = jnp.where(below, blocks_ref[slot, panel, 1], 0.0)
            return carry

        lax.fori_loop(0, 128, place_block, 0, unroll=4)

        for panel in range(2):
            for first in range(0, 1024, 256):
                forms = left_forms(
                    panel_ref[0, panel, first : first + 256, :].T, -panel_ref[1, panel, first : first + 256, :].T
                )
                for form in range(3):
                    for piece in range(2):
                        left_ref[form, piece, panel * 256 : (panel + 1) * 256, first : first + 256] = forms[form][piece]

        left = [(left_ref[form, 0, 256:512, :], left_ref[form, 1, 256:512, :]) for form in range(3)]
        real_part, imag_part = complex_dot(left, right_forms(panel_ref[0, 0], panel_ref[1, 0]))
        g_ref[0:256, :] = real_part[:, :128]
        g_ref[256:512, :] = real_part[:, 128:]
        g_ref[512:768, :] = imag_part[:, :128]
        g_ref[768:1024, :] = imag_part[:, 128:]

        for panel in range(2):
            factor = right_forms(*adjoint_upper(tri_ref, panel))

            def scale_rows(step, carry):
                rows = pl.ds(pl.multiple_of(step * 256, 256), 256)
                real_part, imag_part = complex_dot(
                    left_forms(panel_ref[0, panel, rows, :], panel_ref[1, panel, rows, :]), factor
                )
                x_ref[0, rows, panel * 256 : (panel + 1) * 256] = real_part
                x_ref[1, rows, panel * 256 : (panel + 1) * 256] = imag_part
                return carry

            lax.fori_loop(0, 4, scale_rows, 0)

    left = [(left_ref[form, 0], left_ref[form, 1]) for form in range(3)]
    real_part, imag_part = complex_dot(left, right_forms(vectors_ref[0], vectors_ref[1]))
    for tile in range(2):
        y_ref[tile, 0:512, :] = real_part[:, tile * 128 : (tile + 1) * 128]
        y_ref[tile, 512:1024, :] = imag_part[:, tile * 128 : (tile + 1) * 128]


def products(offsets, arrived_ids, arrived, tri_factors, vectors):
    f32 = jnp.float32
    whole = pl.BlockSpec(memory_space=pltpu.VMEM)
    return pl.pallas_call(
        product_kernel,
        grid=(4,),
        out_shape=(
            jax.ShapeDtypeStruct((8, 1024, 128), f32),
            jax.ShapeDtypeStruct((1024, 128), f32),
            jax.ShapeDtypeStruct((2, 1024, 512), f32),
        ),
        in_specs=[
            pl.BlockSpec(memory_space=pltpu.SMEM),
            whole,
            whole,
            whole,
            pl.BlockSpec((2, 1024, 256), lambda step: (0, 0, step)),
        ],
        out_specs=[pl.BlockSpec((2, 1024, 128), lambda step: (step, 0, 0)), whole, whole],
        scratch_shapes=[
            pltpu.VMEM((8, 128), jnp.int32),
            pltpu.SMEM((8, 128), jnp.int32),
            pltpu.VMEM((2, 2, 1024, 256), f32),
            pltpu.VMEM((3, 2, 512, 1024), jnp.bfloat16),
            pltpu.SemaphoreType.DMA,
        ],
        compiler_params=pltpu.CompilerParams(vmem_limit_bytes=VMEM_LIMIT, dimension_semantics=("arbitrary",)),
        name="products",
    )(offsets, arrived_ids, arrived, tri_factors, vectors)


TILES = 9
LINKS = 6


def sum_kernel(y_ref, g_ref, total_ref, held_ref, landed_ref, send_sem, recv_sem):
    row = lax.axis_index("row")
    col = lax.axis_index("col")
    x = row // 8
    y = row % 4
    z = (col // 2) * 2 + (row // 4) % 2
    core = col % 2

    def device(x, y, z, core):
        strip = strip_of(x, y, z, core)
        return (strip // 4, strip % 4)

    near = lambda place: place + 1 - 2 * (place % 2)
    far = lambda place: 3 - place
    near_bit = lambda place: ((place + 1) // 2) % 2
    far_bit = lambda place: place // 2
    links = [
        (device(near(x), y, z, core), near_bit(x)),
        (device(x, near(y), z, core), near_bit(y)),
        (device(x, y, near(z), core), near_bit(z)),
        (device(far(x), y, z, core), far_bit(x)),
        (device(x, far(y), z, core), far_bit(y)),
        (device(x, y, far(z), core), far_bit(z)),
    ]
    sibling = device(x, y, z, 1 - core)

    barrier = pltpu.get_barrier_semaphore()
    for peer in [sibling] + [link[0] for link in links]:
        pl.semaphore_signal(barrier, inc=1, device_id=peer, device_id_type=MESH)
    pl.semaphore_wait(barrier, LINKS + 1)

    def rows(first, count):
        return pl.ds(pl.multiple_of(first, 8), count)

    def given(tile):
        return g_ref if tile == 0 else y_ref.at[tile - 1]

    started = []

    def send(tile, step, source, target, peer):
        copy = pltpu.make_async_remote_copy(
            source,
            target,
            send_sem.at[tile, step],
            recv_sem.at[tile, step],
            device_id=peer,
            device_id_type=MESH,
        )
        copy.start()
        started.append(copy)
        return copy

    base = [0, 512, 768, 896, 960, 992, 1008]
    pending = []
    lows = [0] * TILES
    for tile in range(TILES):
        pending.append(
            send(
                tile,
                0,
                given(tile).at[rows((1 - core) * 512, 512), :],
                landed_ref.at[tile, pl.ds(0, 512), :],
                sibling,
            )
        )
    for step in range(LINKS + 1):
        size = 512 >> step
        for tile in range(TILES):
            pending[tile].wait_recv()
            low = lows[tile]
            arrived = landed_ref[tile, pl.ds(base[step], size), :]
            if step == 0:
                held_ref[tile, :, :] = given(tile)[rows(core * 512, 512), :] + arrived
            elif step < LINKS:
                held_ref[tile, rows(low, size), :] += arrived
            else:
                final = held_ref[tile, rows(low, size), :] + arrived
                total_ref[tile, rows(core * 512 + low, size), :] = final
            if step < LINKS:
                peer, bit = links[(tile + step) % LINKS]
                half = size // 2
                pending[tile] = send(
                    tile,
                    step + 1,
                    held_ref.at[tile, rows(low + (1 - bit) * half, half), :],
                    landed_ref.at[tile, pl.ds(base[step + 1], half), :],
                    peer,
                )
                lows[tile] = low + bit * half
    for step in range(LINKS + 1):
        size = 8 << step
        for tile in range(TILES):
            if step > 0:
                pending[tile].wait_recv()
                bit = links[(tile + LINKS - step) % LINKS][1]
                lows[tile] = lows[tile] - bit * (size // 2)
            peer = links[(tile + LINKS - 1 - step) % LINKS][0] if step < LINKS else sibling
            place = total_ref.at[tile, rows(core * 512 + lows[tile], size), :]
            pending[tile] = send(tile, LINKS + 1 + step, place, place, peer)
    for tile in range(TILES):
        pending[tile].wait_recv()
    for copy in started:
        copy.wait_send()


def sum_products(partial, gram):
    f32 = jnp.float32
    whole = pl.BlockSpec(memory_space=pltpu.VMEM)
    return pl.pallas_call(
        sum_kernel,
        out_shape=jax.ShapeDtypeStruct((TILES, 1024, 128), f32),
        in_specs=[whole, whole],
        out_specs=whole,
        scratch_shapes=[
            pltpu.VMEM((TILES, 512, 128), f32),
            pltpu.VMEM((TILES, 1024, 128), f32),
            pltpu.SemaphoreType.DMA((TILES, 2 * LINKS + 2)),
            pltpu.SemaphoreType.DMA((TILES, 2 * LINKS + 2)),
        ],
        compiler_params=pltpu.CompilerParams(
            vmem_limit_bytes=VMEM_LIMIT, collective_id=1, has_side_effects=True
        ),
        name="sum_products",
    )(partial, gram)


def update_kernel(g_ref, y_ref, x_ref, tri_ref, vectors_ref, out_ref, left_ref):
    @pl.when(pl.program_id(0) == 0)
    def _():
        gram = g_ref[0]
        gram_real = jnp.concatenate([gram[0:256], gram[256:512]], axis=1)
        gram_imag = jnp.concatenate([gram[512:768], gram[768:1024]], axis=1)
        cross = complex_dot(left_forms(gram_real, gram_imag), right_forms(*adjoint_upper(tri_ref, 0)))
        cross = right_forms(*cross)

        def correct_rows(step, carry):
            rows = pl.ds(pl.multiple_of(step * 256, 256), 256)
            second = (x_ref[0, rows, 256:512], x_ref[1, rows, 256:512])
            forms_second = left_forms(*second)
            real_part, imag_part = complex_dot(forms_second, cross)
            forms_first = left_forms(x_ref[0, rows, 0:256] - real_part, x_ref[1, rows, 0:256] - imag_part)
            for form in range(3):
                for piece in range(2):
                    left_ref[form, piece, rows, 0:256] = forms_first[form][piece]
                    left_ref[form, piece, rows, 256:512] = forms_second[form][piece]
            return carry

        lax.fori_loop(0, 4, correct_rows, 0)

    left = [(left_ref[form, 0], left_ref[form, 1]) for form in range(3)]
    summed = jnp.concatenate([y_ref[0], y_ref[1]], axis=1)
    real_part, imag_part = complex_dot(left, right_forms(summed[0:512], summed[512:1024]))
    out_ref[0] = vectors_ref[0] - real_part
    out_ref[1] = vectors_ref[1] - imag_part


def update(total, scaled, tri_factors, vectors):
    whole = pl.BlockSpec(memory_space=pltpu.VMEM)
    columns = pl.BlockSpec((2, 1024, 256), lambda step: (0, 0, step))
    return pl.pallas_call(
        update_kernel,
        grid=(4,),
        out_shape=jax.ShapeDtypeStruct(vectors.shape, jnp.float32),
        in_specs=[
            pl.BlockSpec((1, 1024, 128), lambda step: (0, 0, 0)),
            pl.BlockSpec((pl.Element(2), pl.Element(1024), pl.Element(128)), lambda step: (1 + 2 * step, 0, 0)),
            whole,
            whole,
            columns,
        ],
        out_specs=columns,
        scratch_shapes=[pltpu.VMEM((3, 2, 1024, 512), jnp.bfloat16)],
        compiler_params=pltpu.CompilerParams(vmem_limit_bytes=VMEM_LIMIT, dimension_semantics=("arbitrary",)),
        name="update",
    )(total, total, scaled, tri_factors, vectors)


def per_device(vectors, panel_store, block_ids, offsets, tri_factors):
    arrived, arrived_ids = exchange(panel_store, block_ids)
    partial, gram, scaled = products(offsets, arrived_ids, arrived, tri_factors, vectors)
    total = sum_products(partial, gram)
    return update(total, scaled, tri_factors, vectors)


def solution(mesh):
    placed = (
        P(None, ("row", "col"), None),
        P(None, None, ("row", "col"), None),
        P(None, ("row", "col")),
        P(),
        P(),
    )
    return jax.shard_map(
        per_device,
        mesh=mesh,
        in_specs=placed,
        out_specs=P(None, ("row", "col"), None),
        check_vma=False,
    )
```

```python
import functools

import jax
import jax.numpy as jnp
from jax import lax
from jax.experimental import pallas as pl
from jax.experimental.pallas import tpu as pltpu
from jax.sharding import PartitionSpec as P


MESH = pl.DeviceIdType.MESH


def strip_of(x, y, z, core):
    return ((x * 2 + z % 2) * 4 + y) * 4 + (z // 2) * 2 + core


def exchange_kernel(
    rows,
    store_ref,
    ids_ref,
    blocks_ref,
    ids_out_ref,
    relay_ref,
    send_sem,
    recv_sem,
    id_send_sem,
    id_recv_sem,
    hop_send_sem,
    hop_recv_sem,
    last_send_sem,
    last_recv_sem,
    own_sem,
):
    row = lax.axis_index("row")
    col = lax.axis_index("col")
    me = row * 4 + col
    x = row // 8
    y = row % 4
    z = (col // 2) * 2 + (row // 4) % 2
    core = col % 2

    barrier = pltpu.get_barrier_semaphore()

    def greet(step, carry):
        peer = (me + step) % 128
        pl.semaphore_signal(barrier, inc=1, device_id=(peer // 4, peer % 4), device_id_type=MESH)
        return carry

    lax.fori_loop(1, 128, greet, 0)

    def listed(strip):
        return pl.ds(pl.multiple_of(strip * rows, rows), rows)

    own_blocks = pltpu.make_async_copy(store_ref.at[:, :, listed(me), :], blocks_ref.at[me], own_sem.at[0])
    own_ids = pltpu.make_async_copy(ids_ref, ids_out_ref.at[me], own_sem.at[1])
    own_blocks.start()
    own_ids.start()
    pl.semaphore_wait(barrier, 127)

    def remote(source, target, sent, received, strip):
        return pltpu.make_async_remote_copy(
            source,
            target,
            sent,
            received,
            device_id=(strip // 4, strip % 4),
            device_id_type=MESH,
        )

    def offset(step):
        spread = (step // 2 * 27) % 64
        return spread % 4, (spread // 4) % 4, spread // 16

    def opposite(shift):
        return (shift // 2) * (1 - shift % 2)

    def has_opposite(step):
        dx, dy, dz = offset(step)
        return opposite(dx) + opposite(dy) + opposite(dz) > 0

    def shifted(step, sign, core):
        dx, dy, dz = offset(step)
        return strip_of((x + sign * dx + 4) % 4, (y + sign * dy + 4) % 4, (z + sign * dz + 4) % 4, core)

    def target_of(step):
        return shifted(step, 1, (core + step) % 2)

    def origin_of(step):
        return shifted(step, -1, (core + step) % 2)

    def relay_of(step):
        dx, dy, dz = offset(step)
        return strip_of((x + 4 - opposite(dx)) % 4, (y + 4 - opposite(dy)) % 4, (z + 4 - opposite(dz)) % 4, core)

    def relayed_origin(step):
        dx, dy, dz = offset(step)
        return (x + opposite(dx)) % 4, (y + opposite(dy)) % 4, (z + opposite(dz)) % 4

    def relayed_target(step):
        dx, dy, dz = offset(step)
        from_x, from_y, from_z = relayed_origin(step)
        return strip_of((from_x + dx) % 4, (from_y + dy) % 4, (from_z + dz) % 4, (core + step) % 2)

    def whole_copy(step, strip, source):
        return remote(
            store_ref.at[:, :, listed(strip), :], blocks_ref.at[source], send_sem.at[step], recv_sem.at[step], strip
        )

    def first_panel_copy(step, strip, source):
        return remote(
            store_ref.at[0, :, listed(strip), :],
            blocks_ref.at[source, 0],
            send_sem.at[step],
            recv_sem.at[step],
            strip,
        )

    def hop_copy(step):
        return remote(
            store_ref.at[1, :, listed(target_of(step)), :],
            relay_ref.at[step],
            hop_send_sem.at[step],
            hop_recv_sem.at[step],
            relay_of(step),
        )

    def last_copy(step, strip, source):
        return remote(
            relay_ref.at[step], blocks_ref.at[source, 1], last_send_sem.at[step], last_recv_sem.at[step], strip
        )

    def id_copy(step, strip, source):
        return remote(ids_ref, ids_out_ref.at[source], id_send_sem.at[step], id_recv_sem.at[step], strip)

    def send_ids(step, carry):
        id_copy(step, target_of(step), me).start()
        return carry

    def send(step, carry):
        opposed = has_opposite(step)

        @pl.when(opposed)
        def _():
            hop_copy(step).start()
            first_panel_copy(step, target_of(step), me).start()

        @pl.when(jnp.logical_not(opposed))
        def _():
            whole_copy(step, target_of(step), me).start()

        return carry

    def forward(step, carry):
        @pl.when(has_opposite(step))
        def _():
            hop_copy(step).wait_recv()
            last_copy(step, relayed_target(step), strip_of(*relayed_origin(step), core)).start()

        return carry

    lead = 24
    lax.fori_loop(1, lead + 1, send, 0)
    lax.fori_loop(1, 128, send_ids, 0)

    def both(step, carry):
        send(step + lead, carry)
        return forward(step, carry)

    lax.fori_loop(1, 128 - lead, both, 0)
    lax.fori_loop(128 - lead, 128, forward, 0)
    own_blocks.wait()
    own_ids.wait()

    def finish(step, carry):
        strip = target_of(step)
        source = origin_of(step)
        id_copy(step, strip, source).wait()
        opposed = has_opposite(step)

        @pl.when(opposed)
        def _():
            first_panel_copy(step, strip, source).wait()
            hop_copy(step).wait_send()
            last_copy(step, strip, source).wait()

        @pl.when(jnp.logical_not(opposed))
        def _():
            whole_copy(step, strip, source).wait()

        return carry

    lax.fori_loop(1, 128, finish, 0)


def exchange(panel_store, block_ids):
    panel_count, parts, row_count, col_width = panel_store.shape
    slot_count = block_ids.shape[1]
    rows = row_count // slot_count
    return pl.pallas_call(
        functools.partial(exchange_kernel, rows),
        out_shape=(
            jax.ShapeDtypeStruct((slot_count, panel_count, parts, rows, col_width), jnp.float32),
            jax.ShapeDtypeStruct((slot_count, panel_count, slot_count), jnp.int32),
        ),
        in_specs=[pl.BlockSpec(memory_space=pl.ANY)] * 2,
        out_specs=[pl.BlockSpec(memory_space=pl.ANY)] * 2,
        scratch_shapes=[pltpu.VMEM((slot_count, parts, rows, col_width), jnp.float32)]
        + [pltpu.SemaphoreType.DMA((128,))] * 8
        + [pltpu.SemaphoreType.DMA((2,))],
        compiler_params=pltpu.CompilerParams(collective_id=0, has_side_effects=True),
        name="exchange",
    )(panel_store, block_ids)


VMEM_LIMIT = 60 * 1024 * 1024


def split(value):
    high = value.astype(jnp.bfloat16)
    return high, (value - high.astype(jnp.float32)).astype(jnp.bfloat16)


def dot(first_op, second_op):
    return jnp.dot(first_op, second_op, preferred_element_type=jnp.float32)


def split_dot(first_op, second_op):
    return (
        dot(first_op[0], second_op[0]) + dot(first_op[0], second_op[1]) + dot(first_op[1], second_op[0])
    )


def left_forms(real_part, imag_part):
    return split(real_part + imag_part), split(real_part), split(imag_part)


def right_forms(real_part, imag_part):
    return split(real_part), split(imag_part - real_part), split(real_part + imag_part)


def complex_dot(left, right):
    shared = split_dot(left[0], right[0])
    real_part = shared - split_dot(left[2], right[2])
    imag_part = shared + split_dot(left[1], right[1])
    return real_part, imag_part


def adjoint_upper(tri_ref, panel):
    shape = tri_ref.shape[2:]
    upper = lax.broadcasted_iota(jnp.int32, shape, 0) <= lax.broadcasted_iota(jnp.int32, shape, 1)
    return jnp.where(upper, tri_ref[panel, 0], 0.0).T, -jnp.where(upper, tri_ref[panel, 1], 0.0).T


def product_kernel(
    offsets_ref, ids_ref, blocks_ref, tri_ref, vectors_ref, y_ref, g_ref, x_ref, order_ref, slot_ref, panel_ref, left_ref, sem
):
    @pl.when(pl.program_id(0) == 0)
    def _():
        me = lax.axis_index("row") * 4 + lax.axis_index("col")
        source = lax.broadcasted_iota(jnp.int32, (128, 128), 0)
        lane = lax.broadcasted_iota(jnp.int32, (128, 128), 1)
        for panel in range(2):
            listed = jnp.sum(jnp.where(lane == me, ids_ref[:, panel, :], 0), axis=1, keepdims=True)
            place = listed - me * 128
            order_ref[panel : panel + 1, :] = jnp.sum(
                jnp.where(place == lane, source, 0), axis=0, keepdims=True
            )
        fetch = pltpu.make_async_copy(order_ref, slot_ref, sem)
        fetch.start()
        fetch.wait()

        def place_block(block, carry):
            first = pl.multiple_of(block * 8, 8)
            row_index = me * 1024 + block * 8 + lax.broadcasted_iota(jnp.int32, (8, 256), 0)
            for panel in range(2):
                slot = slot_ref[panel, block]
                limit = offsets_ref[panel] + lax.broadcasted_iota(jnp.int32, (8, 256), 1)
                below = row_index > limit
                diagonal = jnp.where(row_index == limit, 1.0, 0.0)
                panel_ref[0, panel, pl.ds(first, 8), :] = jnp.where(below, blocks_ref[slot, panel, 0], diagonal)
                panel_ref[1, panel, pl.ds(first, 8), :] = jnp.where(below, blocks_ref[slot, panel, 1], 0.0)
            return carry

        lax.fori_loop(0, 128, place_block, 0, unroll=4)

        for panel in range(2):
            for first in range(0, 1024, 256):
                forms = left_forms(
                    panel_ref[0, panel, first : first + 256, :].T, -panel_ref[1, panel, first : first + 256, :].T
                )
                for form in range(3):
                    for piece in range(2):
                        left_ref[form, piece, panel * 256 : (panel + 1) * 256, first : first + 256] = forms[form][piece]

        left = [(left_ref[form, 0, 256:512, :], left_ref[form, 1, 256:512, :]) for form in range(3)]
        real_part, imag_part = complex_dot(left, right_forms(panel_ref[0, 0], panel_ref[1, 0]))
        g_ref[0:256, :] = real_part[:, :128]
        g_ref[256:512, :] = real_part[:, 128:]
        g_ref[512:768, :] = imag_part[:, :128]
        g_ref[768:1024, :] = imag_part[:, 128:]

        for panel in range(2):
            factor = right_forms(*adjoint_upper(tri_ref, panel))

            def scale_rows(step, carry):
                rows = pl.ds(pl.multiple_of(step * 256, 256), 256)
                real_part, imag_part = complex_dot(
                    left_forms(panel_ref[0, panel, rows, :], panel_ref[1, panel, rows, :]), factor
                )
                x_ref[0, rows, panel * 256 : (panel + 1) * 256] = real_part
                x_ref[1, rows, panel * 256 : (panel + 1) * 256] = imag_part
                return carry

            lax.fori_loop(0, 4, scale_rows, 0)

    left = [(left_ref[form, 0], left_ref[form, 1]) for form in range(3)]
    real_part, imag_part = complex_dot(left, right_forms(vectors_ref[0], vectors_ref[1]))
    for tile in range(2):
        y_ref[tile, 0:512, :] = real_part[:, tile * 128 : (tile + 1) * 128]
        y_ref[tile, 512:1024, :] = imag_part[:, tile * 128 : (tile + 1) * 128]


def products(offsets, arrived_ids, arrived, tri_factors, vectors):
    f32 = jnp.float32
    whole = pl.BlockSpec(memory_space=pltpu.VMEM)
    return pl.pallas_call(
        product_kernel,
        grid=(4,),
        out_shape=(
            jax.ShapeDtypeStruct((8, 1024, 128), f32),
            jax.ShapeDtypeStruct((1024, 128), f32),
            jax.ShapeDtypeStruct((2, 1024, 512), f32),
        ),
        in_specs=[
            pl.BlockSpec(memory_space=pltpu.SMEM),
            whole,
            whole,
            whole,
            pl.BlockSpec((2, 1024, 256), lambda step: (0, 0, step)),
        ],
        out_specs=[pl.BlockSpec((2, 1024, 128), lambda step: (step, 0, 0)), whole, whole],
        scratch_shapes=[
            pltpu.VMEM((8, 128), jnp.int32),
            pltpu.SMEM((8, 128), jnp.int32),
            pltpu.VMEM((2, 2, 1024, 256), f32),
            pltpu.VMEM((3, 2, 512, 1024), jnp.bfloat16),
            pltpu.SemaphoreType.DMA,
        ],
        compiler_params=pltpu.CompilerParams(vmem_limit_bytes=VMEM_LIMIT, dimension_semantics=("arbitrary",)),
        name="products",
    )(offsets, arrived_ids, arrived, tri_factors, vectors)


TILES = 9
STAGES = 10


def arrival_order():
    free = [0.0] * 7
    ready = []
    for tile in range(TILES):
        free[6] += 0.45
        ready.append((free[6] + 1.5, tile, 0))
    order = []
    now = 0.0
    while ready:
        ready.sort()
        arrived, tile, stage = ready.pop(0)
        order.append((tile, stage))
        now = max(now, arrived) + 0.15
        following = stage + 1
        if following == STAGES:
            continue
        if following in (4, 5):
            finish = now + 0.3
        else:
            if following == 9:
                link, cost = 6, 0.45
            elif following < 4:
                link, cost = (tile + following - 1) % 6, 2.7 / 2 ** (following - 1)
            else:
                link, cost = (tile + 8 - following) % 6, 2.7 / 2 ** (8 - following)
            free[link] = max(free[link], now) + cost
            finish = free[link]
        ready.append((finish + 1.5, tile, following))
    return order


def sum_kernel(y_ref, g_ref, total_ref, held_ref, landed_ref, send_sem, recv_sem):
    row = lax.axis_index("row")
    col = lax.axis_index("col")
    here = (row // 8, row % 4, (col // 2) * 2 + (row // 4) % 2)
    core = col % 2

    def device(place, core):
        strip = strip_of(*place, core)
        return (strip // 4, strip % 4)

    near = [place + 1 - 2 * (place % 2) for place in here]
    far = [3 - place for place in here]
    sibling = device(here, 1 - core)
    other = near + far
    bits = [((place + 1) // 2) % 2 for place in here] + [place // 2 for place in here]

    def across(links):
        place = list(here)
        for link in links:
            place[link % 3] = other[link]
        return device(place, core)

    barrier = pltpu.get_barrier_semaphore()
    peers = [sibling]
    for first in (None, 0, 3):
        for second in (None, 1, 4):
            for third in (None, 2, 5):
                chosen = [link for link in (first, second, third) if link is not None]
                if chosen:
                    peers.append(across(chosen))
    for peer in peers:
        pl.semaphore_signal(barrier, inc=1, device_id=peer, device_id_type=MESH)
    pl.semaphore_wait(barrier, len(peers))

    def rows(first, count):
        return pl.ds(pl.multiple_of(first, 8), count)

    def given(tile):
        return g_ref if tile == 0 else y_ref.at[tile - 1]

    def send(tile, stage, source, target, peer):
        pltpu.make_async_remote_copy(
            source,
            target,
            send_sem.at[tile, stage],
            recv_sem.at[tile, stage],
            device_id=peer,
            device_id_type=MESH,
        ).start()

    counts = [512, 256, 128, 64, 56, 56, 64, 128, 256, 512]
    base = [0, 512, 768, 896, 960]

    def wait(tile, stage, sem):
        some = landed_ref.at[tile, pl.ds(0, counts[stage]), :]
        pltpu.make_async_copy(some, some, sem.at[tile, stage]).wait()

    def order_of(tile):
        return [(tile + step) % 6 for step in range(6)]

    def eighth(tile, flips=0):
        index = 0
        for place, link in enumerate(order_of(tile)[3:]):
            bit = 1 - bits[link] if flips & (4 >> place) else bits[link]
            index = index * 2 + bit
        return index

    def flipped(tile, flips):
        return across([link for place, link in enumerate(order_of(tile)[3:]) if flips & (4 >> place)])

    lows = [0] * TILES

    def total_rows(tile, count):
        return total_ref.at[tile, rows(core * 512 + lows[tile], count), :]

    def advance(tile, stage):
        order = order_of(tile)
        low = lows[tile]
        if stage == 0:
            held_ref[tile, :, :] = given(tile)[rows(core * 512, 512), :] + landed_ref[tile, 0:512, :]
        elif stage < 4:
            size = counts[stage]
            held_ref[tile, rows(low, size), :] += landed_ref[tile, base[stage] : base[stage] + size, :]
        elif stage == 4:
            own = rows(low + eighth(tile) * 8, 8)
            final = held_ref[tile, own, :]
            for flips in range(1, 8):
                final += landed_ref[tile, base[4] + flips * 8 - 8 : base[4] + flips * 8, :]
            total_ref[tile, rows(core * 512 + low + eighth(tile) * 8, 8), :] = final
        if stage < 3:
            size = counts[stage + 1]
            link = order[stage]
            keep = bits[link]
            send(
                tile,
                stage + 1,
                held_ref.at[tile, rows(low + (1 - keep) * size, size), :],
                landed_ref.at[tile, pl.ds(base[stage + 1], size), :],
                across([link]),
            )
            lows[tile] = low + keep * size
        elif stage == 3:
            for flips in range(1, 8):
                send(
                    tile,
                    4,
                    held_ref.at[tile, rows(low + eighth(tile, flips) * 8, 8), :],
                    landed_ref.at[tile, pl.ds(base[4] + flips * 8 - 8, 8), :],
                    flipped(tile, flips),
                )
        elif stage == 4:
            place = total_ref.at[tile, rows(core * 512 + low + eighth(tile) * 8, 8), :]
            for flips in range(1, 8):
                send(tile, 5, place, place, flipped(tile, flips))
        elif stage < 8:
            if stage > 5:
                lows[tile] = low - bits[order[8 - stage]] * counts[stage]
            place = total_rows(tile, counts[stage + 1])
            send(tile, stage + 1, place, place, across([order[7 - stage]]))
        elif stage == 8:
            lows[tile] = low - bits[order[0]] * counts[stage]
            place = total_rows(tile, 512)
            send(tile, 9, place, place, sibling)

    for tile in range(TILES):
        send(tile, 0, given(tile).at[rows((1 - core) * 512, 512), :], landed_ref.at[tile, pl.ds(0, 512), :], sibling)
    for tile, stage in arrival_order():
        wait(tile, stage, recv_sem)
        advance(tile, stage)
    for tile in range(TILES):
        for stage in range(STAGES):
            wait(tile, stage, send_sem)


def sum_products(partial, gram):
    f32 = jnp.float32
    whole = pl.BlockSpec(memory_space=pltpu.VMEM)
    return pl.pallas_call(
        sum_kernel,
        out_shape=jax.ShapeDtypeStruct((TILES, 1024, 128), f32),
        in_specs=[whole, whole],
        out_specs=whole,
        scratch_shapes=[
            pltpu.VMEM((TILES, 512, 128), f32),
            pltpu.VMEM((TILES, 1024, 128), f32),
            pltpu.SemaphoreType.DMA((TILES, STAGES)),
            pltpu.SemaphoreType.DMA((TILES, STAGES)),
        ],
        compiler_params=pltpu.CompilerParams(
            vmem_limit_bytes=VMEM_LIMIT, collective_id=1, has_side_effects=True
        ),
        name="sum_products",
    )(partial, gram)


def update_kernel(g_ref, y_ref, x_ref, tri_ref, vectors_ref, out_ref, left_ref):
    @pl.when(pl.program_id(0) == 0)
    def _():
        gram = g_ref[0]
        gram_real = jnp.concatenate([gram[0:256], gram[256:512]], axis=1)
        gram_imag = jnp.concatenate([gram[512:768], gram[768:1024]], axis=1)
        cross = complex_dot(left_forms(gram_real, gram_imag), right_forms(*adjoint_upper(tri_ref, 0)))
        cross = right_forms(*cross)

        def correct_rows(step, carry):
            rows = pl.ds(pl.multiple_of(step * 256, 256), 256)
            second = (x_ref[0, rows, 256:512], x_ref[1, rows, 256:512])
            forms_second = left_forms(*second)
            real_part, imag_part = complex_dot(forms_second, cross)
            forms_first = left_forms(x_ref[0, rows, 0:256] - real_part, x_ref[1, rows, 0:256] - imag_part)
            for form in range(3):
                for piece in range(2):
                    left_ref[form, piece, rows, 0:256] = forms_first[form][piece]
                    left_ref[form, piece, rows, 256:512] = forms_second[form][piece]
            return carry

        lax.fori_loop(0, 4, correct_rows, 0)

    left = [(left_ref[form, 0], left_ref[form, 1]) for form in range(3)]
    summed = jnp.concatenate([y_ref[0], y_ref[1]], axis=1)
    real_part, imag_part = complex_dot(left, right_forms(summed[0:512], summed[512:1024]))
    out_ref[0] = vectors_ref[0] - real_part
    out_ref[1] = vectors_ref[1] - imag_part


def update(total, scaled, tri_factors, vectors):
    whole = pl.BlockSpec(memory_space=pltpu.VMEM)
    columns = pl.BlockSpec((2, 1024, 256), lambda step: (0, 0, step))
    return pl.pallas_call(
        update_kernel,
        grid=(4,),
        out_shape=jax.ShapeDtypeStruct(vectors.shape, jnp.float32),
        in_specs=[
            pl.BlockSpec((1, 1024, 128), lambda step: (0, 0, 0)),
            pl.BlockSpec((pl.Element(2), pl.Element(1024), pl.Element(128)), lambda step: (1 + 2 * step, 0, 0)),
            whole,
            whole,
            columns,
        ],
        out_specs=columns,
        scratch_shapes=[pltpu.VMEM((3, 2, 1024, 512), jnp.bfloat16)],
        compiler_params=pltpu.CompilerParams(vmem_limit_bytes=VMEM_LIMIT, dimension_semantics=("arbitrary",)),
        name="update",
    )(total, total, scaled, tri_factors, vectors)


def per_device(vectors, panel_store, block_ids, offsets, tri_factors):
    arrived, arrived_ids = exchange(panel_store, block_ids)
    partial, gram, scaled = products(offsets, arrived_ids, arrived, tri_factors, vectors)
    total = sum_products(partial, gram)
    return update(total, scaled, tri_factors, vectors)


def solution(mesh):
    placed = (
        P(None, ("row", "col"), None),
        P(None, None, ("row", "col"), None),
        P(None, ("row", "col")),
        P(),
        P(),
    )
    return jax.shard_map(
        per_device,
        mesh=mesh,
        in_specs=placed,
        out_specs=P(None, ("row", "col"), None),
        check_vma=False,
    )
```

```python
import jax
import jax.numpy as jnp
from jax import lax
from jax.experimental import pallas as pl
from jax.experimental.pallas import tpu as pltpu
from jax.sharding import PartitionSpec as P


MESH = pl.DeviceIdType.MESH


def strip_of(x, y, z, core):
    return ((x * 2 + z % 2) * 4 + y) * 4 + (z // 2) * 2 + core


VMEM_LIMIT = 60 * 1024 * 1024


def split(value):
    high = value.astype(jnp.bfloat16)
    return high, (value - high.astype(jnp.float32)).astype(jnp.bfloat16)


def dot(first_op, second_op):
    return jnp.dot(first_op, second_op, preferred_element_type=jnp.float32)


def split_dot(first_op, second_op):
    return (
        dot(first_op[0], second_op[0]) + dot(first_op[0], second_op[1]) + dot(first_op[1], second_op[0])
    )


def left_forms(real_part, imag_part):
    return split(real_part + imag_part), split(real_part), split(imag_part)


def right_forms(real_part, imag_part):
    return split(real_part), split(imag_part - real_part), split(real_part + imag_part)


def complex_dot(left, right):
    shared = split_dot(left[0], right[0])
    real_part = shared - split_dot(left[2], right[2])
    imag_part = shared + split_dot(left[1], right[1])
    return real_part, imag_part


def adjoint_upper(tri_ref, panel):
    shape = tri_ref.shape[2:]
    upper = lax.broadcasted_iota(jnp.int32, shape, 0) <= lax.broadcasted_iota(jnp.int32, shape, 1)
    return jnp.where(upper, tri_ref[panel, 0], 0.0).T, -jnp.where(upper, tri_ref[panel, 1], 0.0).T


TILES = 8
STAGES = 10
COUNTS = [256, 128, 64, 32, 56, 24, 32, 64, 128, 256]
BASES = [0, 256, 384, 448, 480]


def arrival_order(chunk_cost, last_stage):
    free = [0.0] * 7
    ready = []
    order = []
    now = 0.0
    chunk = 0
    while ready or chunk < TILES // 2:
        ready.sort()
        if chunk < TILES // 2 and (not ready or ready[0][0] > now):
            order.append((chunk, None))
            now += chunk_cost
            for tile in (2 * chunk, 2 * chunk + 1):
                free[6] = max(free[6], now) + 0.3
                ready.append((free[6] + 1.6, tile, 0))
            chunk += 1
            continue
        arrived, tile, stage = ready.pop(0)
        order.append((tile, stage))
        now = max(now, arrived) + 0.15
        following = stage + 1
        if following > last_stage:
            continue
        if following in (4, 5):
            finish = now + 0.3
        else:
            if following == 9:
                link, cost = 6, 0.3
            elif following < 4:
                link, cost = (tile + following - 1) % 6, 2.0 / 2 ** (following - 1)
            else:
                link, cost = (tile + 8 - following) % 6, 2.0 / 2 ** (8 - following)
            free[link] = max(free[link], now) + cost
            finish = free[link]
        ready.append((finish + 1.6, tile, following))
    return order


def main_kernel(
    offsets_ref,
    ids_ref,
    store_ref,
    tri_ref,
    vectors_ref,
    y_out_ref,
    x_out_ref,
    z_out_ref,
    z_ref,
    first_blocks_ref,
    second_blocks_ref,
    all_ids_ref,
    order_ref,
    slot_ref,
    panel_ref,
    left_ref,
    x_ref,
    part_ref,
    held_ref,
    landed_ref,
    total_ref,
    block_send_sem,
    block_recv_sem,
    id_send_sem,
    id_recv_sem,
    send_sem,
    recv_sem,
    local_sem,
):
    blocks_refs = (first_blocks_ref, second_blocks_ref)
    row = lax.axis_index("row")
    col = lax.axis_index("col")
    me = row * 4 + col
    x = row // 8
    y = row % 4
    z = (col // 2) * 2 + (row // 4) % 2
    here = (x, y, z)
    core = col % 2

    barrier = pltpu.get_barrier_semaphore()

    def greet(step, carry):
        peer = (me + step) % 128
        pl.semaphore_signal(barrier, inc=1, device_id=(peer // 4, peer % 4), device_id_type=MESH)
        return carry

    lax.fori_loop(1, 128, greet, 0)

    def listed(strip):
        return pl.ds(pl.multiple_of(strip * 8, 8), 8)

    fetch_vectors = pltpu.make_async_copy(vectors_ref, z_ref, local_sem.at[0])
    fetch_blocks = [
        pltpu.make_async_copy(
            store_ref.at[panel, :, listed(me), :], blocks_refs[panel].at[me], local_sem.at[1 + 9 * panel]
        )
        for panel in range(2)
    ]
    fetch_ids = pltpu.make_async_copy(ids_ref, all_ids_ref.at[me], local_sem.at[2])
    fetch_blocks[0].start()
    fetch_blocks[1].start()
    fetch_ids.start()
    pl.semaphore_wait(barrier, 127)

    def strip_at(step, sign):
        spread = (step // 2 * 27) % 64
        return strip_of(
            (x + sign * (spread % 4) + 4) % 4,
            (y + sign * ((spread // 4) % 4) + 4) % 4,
            (z + sign * (spread // 16) + 4) % 4,
            (core + step) % 2,
        )

    def block_copy(panel, step, strip, source):
        return pltpu.make_async_remote_copy(
            store_ref.at[panel, :, listed(strip), :],
            blocks_refs[panel].at[source],
            block_send_sem.at[panel, step],
            block_recv_sem.at[panel, step],
            device_id=(strip // 4, strip % 4),
            device_id_type=MESH,
        )

    def id_copy(step, strip, source):
        return pltpu.make_async_remote_copy(
            ids_ref,
            all_ids_ref.at[source],
            id_send_sem.at[step],
            id_recv_sem.at[step],
            device_id=(strip // 4, strip % 4),
            device_id_type=MESH,
        )

    def send_ids(step, carry):
        id_copy(step, strip_at(step, 1), me).start()
        return carry

    def send_blocks(panel, first, last):
        def body(step, carry):
            block_copy(panel, step, strip_at(step, 1), me).start()
            return carry

        lax.fori_loop(first, last, body, 0)

    def wait_blocks(panel):
        def body(step, carry):
            block_copy(panel, step, strip_at(step, 1), strip_at(step, -1)).wait_recv()
            return carry

        lax.fori_loop(1, 128, body, 0)

    send_blocks(0, 1, 32)
    lax.fori_loop(1, 128, send_ids, 0)
    send_blocks(0, 32, 128)
    fetch_vectors.start()
    send_blocks(1, 1, 24)
    next_block = [24]

    def send_some(count):
        first = next_block[0]
        last = min(first + count, 128)
        if last > first:
            send_blocks(1, first, last)
        next_block[0] = last

    fetch_blocks[0].wait()
    fetch_blocks[1].wait()
    fetch_ids.wait()

    def wait_ids(step, carry):
        id_copy(step, strip_at(step, 1), strip_at(step, -1)).wait_recv()
        return carry

    lax.fori_loop(1, 128, wait_ids, 0)
    source_index = lax.broadcasted_iota(jnp.int32, (128, 128), 0)
    lane = lax.broadcasted_iota(jnp.int32, (128, 128), 1)
    order_ref[...] = jnp.zeros_like(order_ref)
    for panel in range(2):
        own = jnp.sum(jnp.where(lane == me, all_ids_ref[:, panel, :], 0), axis=1, keepdims=True)
        order_ref[panel : panel + 1, :] = jnp.max(
            jnp.where(own - me * 128 == lane, source_index, 0), axis=0, keepdims=True
        )
    fetch_order = pltpu.make_async_copy(order_ref, slot_ref, local_sem.at[3])
    fetch_order.start()
    fetch_order.wait()
    fetch_vectors.wait()

    def place_panel(panel):
        def place_block(block, carry):
            first = pl.multiple_of(block * 8, 8)
            row_index = me * 1024 + block * 8 + lax.broadcasted_iota(jnp.int32, (8, 256), 0)
            slot = slot_ref[panel, block]
            limit = offsets_ref[panel] + lax.broadcasted_iota(jnp.int32, (8, 256), 1)
            below = row_index > limit
            diagonal = jnp.where(row_index == limit, 1.0, 0.0)
            panel_ref[0, pl.ds(first, 8), :] = jnp.where(below, blocks_refs[panel][slot, 0], diagonal)
            panel_ref[1, pl.ds(first, 8), :] = jnp.where(below, blocks_refs[panel][slot, 1], 0.0)
            return carry

        lax.fori_loop(0, 128, place_block, 0, unroll=4)

        def turn(step, carry):
            rows = pl.ds(pl.multiple_of(step * 256, 256), 256)
            forms = left_forms(panel_ref[0, rows, :].T, -panel_ref[1, rows, :].T)
            for form in range(3):
                for piece in range(2):
                    left_ref[form, piece * 256 : (piece + 1) * 256, rows] = forms[form][piece]
            return carry

        lax.fori_loop(0, 4, turn, 0)

    def scale_panel(panel):
        factor = right_forms(*adjoint_upper(tri_ref, panel))

        def scale_rows(step, carry):
            rows = pl.ds(pl.multiple_of(step * 256, 256), 256)
            scaled = complex_dot(left_forms(panel_ref[0, rows, :], panel_ref[1, rows, :]), factor)
            forms = left_forms(*scaled)
            for form in range(3):
                for piece in range(2):
                    x_ref[form, piece, rows, :] = forms[form][piece]
            return carry

        lax.fori_loop(0, 4, scale_rows, 0)

    def chunk_columns(chunk):
        return slice(chunk * 256, (chunk + 1) * 256)

    def form_products(panel, chunk):
        columns = chunk_columns(chunk)
        forms = right_forms(z_ref[0, :, columns], z_ref[1, :, columns])
        sums = []
        for form in range(3):
            high, low = forms[form]
            both = dot(left_ref[form], high)
            sums.append(both[0:256] + both[256:512] + dot(left_ref[form, 0:256, :], low))
        real_part = sums[0] - sums[2]
        imag_part = sums[0] + sums[1]
        for side in range(2):
            part_ref[panel, 2 * chunk + side, 0:256, :] = real_part[:, side * 128 : (side + 1) * 128]
            part_ref[panel, 2 * chunk + side, 256:512, :] = imag_part[:, side * 128 : (side + 1) * 128]

    def apply_first(chunk):
        columns = chunk_columns(chunk)
        summed = jnp.concatenate([total_ref[0, 2 * chunk], total_ref[0, 2 * chunk + 1]], axis=1)
        forms = right_forms(summed[0:256], summed[256:512])

        def apply_rows(step, carry):
            rows = pl.ds(pl.multiple_of(step * 512, 512), 512)
            left = [(x_ref[form, 0, rows, :], x_ref[form, 1, rows, :]) for form in range(3)]
            real_part, imag_part = complex_dot(left, forms)
            z_ref[0, rows, columns] -= real_part
            z_ref[1, rows, columns] -= imag_part
            return carry

        lax.fori_loop(0, 2, apply_rows, 0)
        copy = pltpu.make_async_copy(z_ref.at[:, :, columns], z_out_ref.at[:, :, columns], local_sem.at[4 + chunk])
        copy.start()
        return copy

    def device(place, core):
        strip = strip_of(*place, core)
        return (strip // 4, strip % 4)

    sibling = device(here, 1 - core)
    other = [place + 1 - 2 * (place % 2) for place in here] + [3 - place for place in here]
    bits = [((place + 1) // 2) % 2 for place in here] + [place // 2 for place in here]

    def across(links):
        place = list(here)
        for link in links:
            place[link % 3] = other[link]
        return device(place, core)

    def rows_at(first, count):
        return pl.ds(pl.multiple_of(first, 8), count)

    def send(panel, tile, stage, source, target, peer):
        pltpu.make_async_remote_copy(
            source,
            target,
            send_sem.at[panel, tile, stage],
            recv_sem.at[panel, tile, stage],
            device_id=peer,
            device_id_type=MESH,
        ).start()

    def wait(panel, tile, stage, sem, counts):
        some = landed_ref.at[panel, tile, pl.ds(0, counts[stage]), :]
        pltpu.make_async_copy(some, some, sem.at[panel, tile, stage]).wait()

    def order_of(tile):
        return [(tile + step) % 6 for step in range(6)]

    def quarter(tile, flips=0):
        first, second = order_of(tile)[3:5]
        high = 1 - bits[first] if flips & 4 else bits[first]
        low = 1 - bits[second] if flips & 2 else bits[second]
        return high * 2 + low

    def flipped(tile, flips):
        return across([link for place, link in enumerate(order_of(tile)[3:]) if flips & (4 >> place)])

    lows = [[0] * TILES, [0] * TILES]

    def begin(panel, tile):
        send(
            panel,
            tile,
            0,
            part_ref.at[panel, tile, rows_at((1 - core) * 256, 256), :],
            landed_ref.at[panel, tile, pl.ds(0, 256), :],
            sibling,
        )

    def advance(panel, tile, stage):
        order = order_of(tile)
        low = lows[panel][tile]
        held = held_ref.at[panel, tile]
        landed = landed_ref.at[panel, tile]
        total = total_ref.at[panel, tile]
        wait(panel, tile, stage, recv_sem, COUNTS)
        if stage == 0:
            held[...] = part_ref[panel, tile, rows_at(core * 256, 256), :] + landed[0:256, :]
        elif stage < 4:
            size = COUNTS[stage]
            held[rows_at(low, size), :] += landed[BASES[stage] : BASES[stage] + size, :]
        elif stage == 4:
            final = held[rows_at(low + quarter(tile) * 8, 8), :]
            for flips in range(1, 8):
                final += landed[BASES[4] + flips * 8 - 8 : BASES[4] + flips * 8, :]
            total[rows_at(core * 256 + low + quarter(tile) * 8, 8), :] = final
        if stage < 3:
            size = COUNTS[stage + 1]
            link = order[stage]
            keep = bits[link]
            send(
                panel,
                tile,
                stage + 1,
                held.at[rows_at(low + (1 - keep) * size, size), :],
                landed.at[pl.ds(BASES[stage + 1], size), :],
                across([link]),
            )
            lows[panel][tile] = low + keep * size
        elif stage == 3:
            for flips in range(1, 8):
                send(
                    panel,
                    tile,
                    4,
                    held.at[rows_at(low + quarter(tile, flips) * 8, 8), :],
                    landed.at[pl.ds(BASES[4] + flips * 8 - 8, 8), :],
                    flipped(tile, flips),
                )
        elif stage == 4:
            place = total.at[rows_at(core * 256 + low + quarter(tile) * 8, 8), :]
            for flips in (2, 4, 6):
                send(panel, tile, 5, place, place, flipped(tile, flips))
        elif stage < 9:
            if stage > 5:
                low = low - bits[order[8 - stage]] * COUNTS[stage]
                lows[panel][tile] = low
            place = total.at[rows_at(core * 256 + low, COUNTS[stage + 1]), :]
            send(panel, tile, stage + 1, place, place, across([order[7 - stage]]) if stage < 8 else sibling)

    wait_blocks(0)
    place_panel(0)
    for tile, stage in arrival_order(2.0, 8):
        if stage is None:
            form_products(0, tile)
            begin(0, 2 * tile)
            begin(0, 2 * tile + 1)
            send_some(8)
            if tile == TILES // 2 - 1:
                scale_panel(0)
        else:
            advance(0, tile, stage)
            send_some(2)
    send_some(128)

    wait_blocks(1)
    place_panel(1)
    written = []
    for tile, stage in arrival_order(3.5, 9):
        if stage is None:
            wait(0, 2 * tile, 9, recv_sem, COUNTS)
            wait(0, 2 * tile + 1, 9, recv_sem, COUNTS)
            written.append(apply_first(tile))
            form_products(1, tile)
            begin(1, 2 * tile)
            begin(1, 2 * tile + 1)
            if tile == TILES // 2 - 1:
                scale_panel(1)
                x_copy = pltpu.make_async_copy(x_ref, x_out_ref, local_sem.at[8])
                x_copy.start()
        else:
            advance(1, tile, stage)
    y_copy = pltpu.make_async_copy(total_ref.at[1], y_out_ref, local_sem.at[9])
    y_copy.start()

    def wait_sent(step, carry):
        strip = strip_at(step, 1)
        id_copy(step, strip, me).wait_send()
        for panel in range(2):
            block_copy(panel, step, strip, me).wait_send()
        return carry

    lax.fori_loop(1, 128, wait_sent, 0)
    for panel in range(2):
        for tile in range(TILES):
            for stage in range(STAGES):
                wait(panel, tile, stage, send_sem, COUNTS)
    for copy in written:
        copy.wait()
    x_copy.wait()
    y_copy.wait()


def main(vectors, panel_store, block_ids, offsets, tri_factors):
    f32 = jnp.float32
    bf16 = jnp.bfloat16
    whole = pl.BlockSpec(memory_space=pltpu.VMEM)
    anywhere = pl.BlockSpec(memory_space=pl.ANY)
    dma = pltpu.SemaphoreType.DMA
    return pl.pallas_call(
        main_kernel,
        out_shape=(
            jax.ShapeDtypeStruct((TILES, 512, 128), f32),
            jax.ShapeDtypeStruct((3, 2, 1024, 256), bf16),
            jax.ShapeDtypeStruct((2, 1024, 1024), f32),
        ),
        in_specs=[pl.BlockSpec(memory_space=pltpu.SMEM), whole, anywhere, whole, anywhere],
        out_specs=[anywhere] * 3,
        scratch_shapes=[
            pltpu.VMEM((2, 1024, 1024), f32),
            pltpu.VMEM((128, 2, 8, 256), f32),
            pltpu.VMEM((128, 2, 8, 256), f32),
            pltpu.VMEM((128, 2, 128), jnp.int32),
            pltpu.VMEM((8, 128), jnp.int32),
            pltpu.SMEM((8, 128), jnp.int32),
            pltpu.VMEM((2, 1024, 256), f32),
            pltpu.VMEM((3, 512, 1024), bf16),
            pltpu.VMEM((3, 2, 1024, 256), bf16),
            pltpu.VMEM((2, TILES, 512, 128), f32),
            pltpu.VMEM((2, TILES, 256, 128), f32),
            pltpu.VMEM((2, TILES, 544, 128), f32),
            pltpu.VMEM((2, TILES, 512, 128), f32),
            dma((2, 128)),
            dma((2, 128)),
            dma((128,)),
            dma((128,)),
            dma((2, TILES, STAGES)),
            dma((2, TILES, STAGES)),
            dma((11,)),
        ],
        compiler_params=pltpu.CompilerParams(
            vmem_limit_bytes=VMEM_LIMIT, collective_id=0, has_side_effects=True
        ),
        name="main",
    )(offsets, block_ids, panel_store, tri_factors, vectors)


def update_kernel(y_ref, x_ref, vectors_ref, out_ref):
    left = [(x_ref[form, 0], x_ref[form, 1]) for form in range(3)]
    summed = jnp.concatenate([y_ref[0], y_ref[1]], axis=1)
    real_part, imag_part = complex_dot(left, right_forms(summed[0:256], summed[256:512]))
    out_ref[0] = vectors_ref[0] - real_part
    out_ref[1] = vectors_ref[1] - imag_part


def update(total, scaled, vectors):
    columns = pl.BlockSpec((2, 1024, 256), lambda step: (0, 0, step))
    return pl.pallas_call(
        update_kernel,
        grid=(4,),
        out_shape=jax.ShapeDtypeStruct(vectors.shape, jnp.float32),
        in_specs=[
            pl.BlockSpec((2, 512, 128), lambda step: (step, 0, 0)),
            pl.BlockSpec((3, 2, 1024, 256), lambda step: (0, 0, 0, 0)),
            columns,
        ],
        out_specs=columns,
        compiler_params=pltpu.CompilerParams(vmem_limit_bytes=VMEM_LIMIT, dimension_semantics=("arbitrary",)),
        name="update",
    )(total, scaled, vectors)


def per_device(vectors, panel_store, block_ids, offsets, tri_factors):
    total, scaled, current = main(vectors, panel_store, block_ids, offsets, tri_factors)
    return update(total, scaled, current)


def solution(mesh):
    placed = (
        P(None, ("row", "col"), None),
        P(None, None, ("row", "col"), None),
        P(None, ("row", "col")),
        P(),
        P(),
    )
    return jax.shard_map(
        per_device,
        mesh=mesh,
        in_specs=placed,
        out_specs=P(None, ("row", "col"), None),
        check_vma=False,
    )
```

```python
import jax
import jax.numpy as jnp
from jax import lax
from jax.experimental import pallas as pl
from jax.experimental.pallas import tpu as pltpu
from jax.sharding import PartitionSpec as P


MESH = pl.DeviceIdType.MESH


def strip_of(x, y, z, core):
    return ((x * 2 + z % 2) * 4 + y) * 4 + (z // 2) * 2 + core


VMEM_LIMIT = 60 * 1024 * 1024


def split(value):
    high = value.astype(jnp.bfloat16)
    return high, (value - high.astype(jnp.float32)).astype(jnp.bfloat16)


def dot(first_op, second_op):
    return jnp.dot(first_op, second_op, preferred_element_type=jnp.float32)


def split_dot(first_op, second_op):
    return (
        dot(first_op[0], second_op[0]) + dot(first_op[0], second_op[1]) + dot(first_op[1], second_op[0])
    )


def left_forms(real_part, imag_part):
    return split(real_part + imag_part), split(real_part), split(imag_part)


def right_forms(real_part, imag_part):
    return split(real_part), split(imag_part - real_part), split(real_part + imag_part)


def complex_dot(left, right):
    shared = split_dot(left[0], right[0])
    real_part = shared - split_dot(left[2], right[2])
    imag_part = shared + split_dot(left[1], right[1])
    return real_part, imag_part


def adjoint_upper(tri_ref, panel):
    shape = tri_ref.shape[2:]
    upper = lax.broadcasted_iota(jnp.int32, shape, 0) <= lax.broadcasted_iota(jnp.int32, shape, 1)
    return jnp.where(upper, tri_ref[panel, 0], 0.0).T, -jnp.where(upper, tri_ref[panel, 1], 0.0).T


GROUPS = (
    ((0, 32), (32, 32), (64, 32), (96, 32)),
    ((0, 32), (32, 32), (64, 32), (96, 16), (112, 16)),
)


def product_kernel(
    offsets_ref,
    ids_ref,
    store_ref,
    tri_ref,
    vectors_ref,
    y_out_ref,
    x_out_ref,
    slot_out_ref,
    z_ref,
    first_blocks_ref,
    second_blocks_ref,
    all_ids_ref,
    order_ref,
    slot_ref,
    first_panel_ref,
    second_panel_ref,
    rows_ref,
    match_ref,
    left_ref,
    factor_ref,
    y_ref,
    x_ref,
    block_send_sem,
    block_recv_sem,
    id_send_sem,
    id_recv_sem,
    local_sem,
):
    blocks_refs = (first_blocks_ref, second_blocks_ref)
    panel_refs = (first_panel_ref, second_panel_ref)
    row = lax.axis_index("row")
    col = lax.axis_index("col")
    me = row * 4 + col
    x = row // 8
    y = row % 4
    z = (col // 2) * 2 + (row // 4) % 2
    core = col % 2

    barrier = pltpu.get_barrier_semaphore()

    def greet(step, carry):
        peer = (me + step) % 128
        pl.semaphore_signal(barrier, inc=1, device_id=(peer // 4, peer % 4), device_id_type=MESH)
        return carry

    lax.fori_loop(1, 128, greet, 0)

    def listed(strip):
        return pl.ds(pl.multiple_of(strip * 8, 8), 8)

    own_copies = [
        pltpu.make_async_copy(store_ref.at[panel, :, listed(me), :], blocks_refs[panel].at[0], local_sem.at[panel])
        for panel in range(2)
    ]
    own_copies.append(pltpu.make_async_copy(ids_ref, all_ids_ref.at[0], local_sem.at[2]))
    for copy in own_copies:
        copy.start()
    fetch_vectors = pltpu.make_async_copy(vectors_ref, z_ref, local_sem.at[3])
    fetch_vectors.start()
    pl.semaphore_wait(barrier, 127)

    def strip_at(step, sign):
        spread = (step // 2 * 27) % 64
        return strip_of(
            (x + sign * (spread % 4) + 4) % 4,
            (y + sign * ((spread // 4) % 4) + 4) % 4,
            (z + sign * (spread // 16) + 4) % 4,
            (core + step) % 2,
        )

    def block_copy(panel, step):
        strip = strip_at(step, 1)
        return pltpu.make_async_remote_copy(
            store_ref.at[panel, :, listed(strip), :],
            blocks_refs[panel].at[step],
            block_send_sem.at[panel, step],
            block_recv_sem.at[panel, step],
            device_id=(strip // 4, strip % 4),
            device_id_type=MESH,
        )

    def id_copy(step):
        strip = strip_at(step, 1)
        return pltpu.make_async_remote_copy(
            ids_ref,
            all_ids_ref.at[step],
            id_send_sem.at[step],
            id_recv_sem.at[step],
            device_id=(strip // 4, strip % 4),
            device_id_type=MESH,
        )

    def send_ids(step, carry):
        id_copy(step).start()
        return carry

    def send_blocks(panel, first, last):
        def body(step, carry):
            block_copy(panel, step).start()
            return carry

        lax.fori_loop(first, last, body, 0)

    send_blocks(0, 1, 24)
    lax.fori_loop(1, 128, send_ids, 0)
    send_blocks(0, 24, 128)
    send_blocks(1, 1, 128)

    for panel in range(2):
        forms = right_forms(*adjoint_upper(tri_ref, panel))
        for form in range(3):
            for piece in range(2):
                factor_ref[panel, form, piece] = forms[form][piece]

    for copy in own_copies:
        copy.wait()

    def wait_ids(step, carry):
        id_copy(step).wait_recv()
        return carry

    lax.fori_loop(1, 128, wait_ids, 0)
    down = lax.broadcasted_iota(jnp.int32, (128, 128), 0)
    lane = lax.broadcasted_iota(jnp.int32, (128, 128), 1)
    order_ref[...] = jnp.zeros_like(order_ref)
    places = []
    for panel in range(2):
        own = jnp.sum(jnp.where(lane == me, all_ids_ref[:, panel, :], 0), axis=1, keepdims=True) % 128
        places.append(jnp.sum(jnp.where(down == lane, own, 0), axis=0, keepdims=True))
        order_ref[panel : panel + 1, :] = places[panel]
    slot_of_place = jnp.max(jnp.where(places[0] == down, lane, 0), axis=1, keepdims=True)
    order_ref[2:3, :] = jnp.max(jnp.where(places[1] == down, slot_of_place, 0), axis=0, keepdims=True)
    fetch_order = pltpu.make_async_copy(order_ref, slot_ref, local_sem.at[4])
    fetch_order.start()
    fetch_order.wait()
    write_order = pltpu.make_async_copy(order_ref, slot_out_ref, local_sem.at[5])
    write_order.start()
    fetch_vectors.wait()

    def take_group(panel, first, count):
        size = count * 8
        start = first * 8
        begin = first == 0
        values = panel_refs[panel]

        def wait_block(step, carry):
            block_copy(panel, step).wait_recv()
            return carry

        lax.fori_loop(max(first, 1), first + count, wait_block, 0)

        def take_block(step, carry):
            slot = first + step
            place = slot_ref[panel, slot]
            near = pl.ds(pl.multiple_of(step * 8, 8), 8)
            row_index = me * 1024 + place * 8 + lax.broadcasted_iota(jnp.int32, (8, 256), 0)
            limit = offsets_ref[panel] + lax.broadcasted_iota(jnp.int32, (8, 256), 1)
            below = row_index > limit
            diagonal = jnp.where(row_index == limit, 1.0, 0.0)
            values[0, slot] = jnp.where(below, blocks_refs[panel][slot, 0], diagonal)
            values[1, slot] = jnp.where(below, blocks_refs[panel][slot, 1], 0.0)
            rows_ref[0, near, :] = z_ref[0, place]
            rows_ref[1, near, :] = z_ref[1, place]
            if panel == 1:
                matching = slot_ref[2, slot]
                match_ref[0, near, :] = first_panel_ref[0, matching]
                match_ref[1, near, :] = first_panel_ref[1, matching]
            return carry

        lax.fori_loop(0, count, take_block, 0, unroll=4)

        own = [values[part, first : first + count].reshape(size, 256) for part in range(2)]
        forms = left_forms(own[0].T, -own[1].T)
        for form in range(3):
            for piece in range(2):
                left_ref[form, piece * 256 : (piece + 1) * 256, 0:size] = forms[form][piece]

        def adjoint_products(right):
            sums = []
            for form in range(3):
                high, low = right[form]
                both = dot(left_ref[form, :, 0:size], high)
                sums.append(both[0:256] + both[256:512] + dot(left_ref[form, 0:256, 0:size], low))
            return sums[0] - sums[2], sums[0] + sums[1]

        def add_tiles(tile, parts):
            for part in range(2):
                for side in range(2):
                    value = parts[part][:, side * 128 : (side + 1) * 128]
                    target = y_ref.at[tile + side, part * 256 : (part + 1) * 256, :]
                    if begin:
                        target[...] = value
                    else:
                        target[...] += value

        def take_columns(chunk, carry):
            columns = pl.ds(pl.multiple_of(chunk * 256, 256), 256)
            right = right_forms(rows_ref[0, 0:size, columns], rows_ref[1, 0:size, columns])
            add_tiles(panel * 8 + 2 * chunk, adjoint_products(right))
            return carry

        lax.fori_loop(0, 4, take_columns, 0)

        if panel == 1:
            matched = (match_ref[0, 0:size, :], match_ref[1, 0:size, :])
            add_tiles(16, adjoint_products(right_forms(*matched)))
            for which, source in enumerate((matched, own)):
                factor = [(factor_ref[which, form, 0], factor_ref[which, form, 1]) for form in range(3)]
                scaled = complex_dot(left_forms(*source), factor)
                for part in range(2):
                    x_ref[part, start : start + size, which * 256 : (which + 1) * 256] = scaled[part]

    for panel in range(2):
        for first, count in GROUPS[panel]:
            take_group(panel, first, count)

    y_copy = pltpu.make_async_copy(y_ref, y_out_ref, local_sem.at[6])
    x_copy = pltpu.make_async_copy(x_ref, x_out_ref, local_sem.at[7])
    y_copy.start()
    x_copy.start()

    def wait_sent(step, carry):
        id_copy(step).wait_send()
        block_copy(0, step).wait_send()
        block_copy(1, step).wait_send()
        return carry

    lax.fori_loop(1, 128, wait_sent, 0)
    write_order.wait()
    y_copy.wait()
    x_copy.wait()


def products(vectors, panel_store, block_ids, offsets, tri_factors):
    f32 = jnp.float32
    bf16 = jnp.bfloat16
    whole = pl.BlockSpec(memory_space=pltpu.VMEM)
    anywhere = pl.BlockSpec(memory_space=pl.ANY)
    dma = pltpu.SemaphoreType.DMA
    return pl.pallas_call(
        product_kernel,
        out_shape=(
            jax.ShapeDtypeStruct((TILES, 512, 128), f32),
            jax.ShapeDtypeStruct((2, 1024, 512), f32),
            jax.ShapeDtypeStruct((8, 128), jnp.int32),
        ),
        in_specs=[pl.BlockSpec(memory_space=pltpu.SMEM), whole, anywhere, whole, anywhere],
        out_specs=[anywhere] * 3,
        scratch_shapes=[
            pltpu.VMEM((2, 128, 8, 1024), f32),
            pltpu.VMEM((128, 2, 8, 256), f32),
            pltpu.VMEM((128, 2, 8, 256), f32),
            pltpu.VMEM((128, 2, 128), jnp.int32),
            pltpu.VMEM((8, 128), jnp.int32),
            pltpu.SMEM((8, 128), jnp.int32),
            pltpu.VMEM((2, 128, 8, 256), f32),
            pltpu.VMEM((2, 128, 8, 256), f32),
            pltpu.VMEM((2, 256, 1024), f32),
            pltpu.VMEM((2, 256, 256), f32),
            pltpu.VMEM((3, 512, 256), bf16),
            pltpu.VMEM((2, 3, 2, 256, 256), bf16),
            pltpu.VMEM((TILES, 512, 128), f32),
            pltpu.VMEM((2, 1024, 512), f32),
            dma((2, 128)),
            dma((2, 128)),
            dma((128,)),
            dma((128,)),
            dma((8,)),
        ],
        compiler_params=pltpu.CompilerParams(
            vmem_limit_bytes=VMEM_LIMIT, collective_id=0, has_side_effects=True
        ),
        name="products",
    )(offsets, block_ids, panel_store, tri_factors, vectors.reshape(2, 128, 8, 1024))


TILES = 18
STAGES = 10
COUNTS = [256, 128, 64, 32, 56, 24, 32, 64, 128, 256]
BASES = [0, 256, 384, 448, 480]


def arrival_order():
    free = [0.0] * 7
    ready = []
    for tile in range(TILES):
        free[6] += 0.3
        ready.append((free[6] + 1.6, tile, 0))
    order = []
    now = 0.0
    while ready:
        ready.sort()
        arrived, tile, stage = ready.pop(0)
        order.append((tile, stage))
        now = max(now, arrived) + 0.15
        following = stage + 1
        if following == STAGES:
            continue
        if following in (4, 5):
            finish = now + 0.3
        else:
            if following == 9:
                link, cost = 6, 0.3
            elif following < 4:
                link, cost = (tile + following - 1) % 6, 2.0 / 2 ** (following - 1)
            else:
                link, cost = (tile + 8 - following) % 6, 2.0 / 2 ** (8 - following)
            free[link] = max(free[link], now) + cost
            finish = free[link]
        ready.append((finish + 1.6, tile, following))
    return order


def sum_kernel(part_ref, total_ref, held_ref, landed_ref, send_sem, recv_sem):
    row = lax.axis_index("row")
    col = lax.axis_index("col")
    here = (row // 8, row % 4, (col // 2) * 2 + (row // 4) % 2)
    core = col % 2

    def device(place, core):
        strip = strip_of(*place, core)
        return (strip // 4, strip % 4)

    sibling = device(here, 1 - core)
    other = [place + 1 - 2 * (place % 2) for place in here] + [3 - place for place in here]
    bits = [((place + 1) // 2) % 2 for place in here] + [place // 2 for place in here]

    def across(links):
        place = list(here)
        for link in links:
            place[link % 3] = other[link]
        return device(place, core)

    barrier = pltpu.get_barrier_semaphore()
    peers = [sibling]
    for first in (None, 0, 3):
        for second in (None, 1, 4):
            for third in (None, 2, 5):
                chosen = [link for link in (first, second, third) if link is not None]
                if chosen:
                    peers.append(across(chosen))
    for peer in peers:
        pl.semaphore_signal(barrier, inc=1, device_id=peer, device_id_type=MESH)
    pl.semaphore_wait(barrier, len(peers))

    def rows_at(first, count):
        return pl.ds(pl.multiple_of(first, 8), count)

    def send(tile, stage, source, target, peer):
        pltpu.make_async_remote_copy(
            source,
            target,
            send_sem.at[tile, stage],
            recv_sem.at[tile, stage],
            device_id=peer,
            device_id_type=MESH,
        ).start()

    def wait(tile, stage, sem, counts):
        some = landed_ref.at[tile, pl.ds(0, counts[stage]), :]
        pltpu.make_async_copy(some, some, sem.at[tile, stage]).wait()

    def order_of(tile):
        return [(tile + step) % 6 for step in range(6)]

    def quarter(tile, flips=0):
        first, second = order_of(tile)[3:5]
        high = 1 - bits[first] if flips & 4 else bits[first]
        low = 1 - bits[second] if flips & 2 else bits[second]
        return high * 2 + low

    def flipped(tile, flips):
        return across([link for place, link in enumerate(order_of(tile)[3:]) if flips & (4 >> place)])

    lows = [0] * TILES

    def begin(tile):
        send(
            tile,
            0,
            part_ref.at[tile, rows_at((1 - core) * 256, 256), :],
            landed_ref.at[tile, pl.ds(0, 256), :],
            sibling,
        )

    def advance(tile, stage):
        order = order_of(tile)
        low = lows[tile]
        held = held_ref.at[tile]
        landed = landed_ref.at[tile]
        total = total_ref.at[tile]
        wait(tile, stage, recv_sem, COUNTS)
        if stage == 0:
            held[...] = part_ref[tile, rows_at(core * 256, 256), :] + landed[0:256, :]
        elif stage < 4:
            size = COUNTS[stage]
            held[rows_at(low, size), :] += landed[BASES[stage] : BASES[stage] + size, :]
        elif stage == 4:
            final = held[rows_at(low + quarter(tile) * 8, 8), :]
            for flips in range(1, 8):
                final += landed[BASES[4] + flips * 8 - 8 : BASES[4] + flips * 8, :]
            total[rows_at(core * 256 + low + quarter(tile) * 8, 8), :] = final
        if stage < 3:
            size = COUNTS[stage + 1]
            link = order[stage]
            keep = bits[link]
            send(
                tile,
                stage + 1,
                held.at[rows_at(low + (1 - keep) * size, size), :],
                landed.at[pl.ds(BASES[stage + 1], size), :],
                across([link]),
            )
            lows[tile] = low + keep * size
        elif stage == 3:
            for flips in range(1, 8):
                send(
                    tile,
                    4,
                    held.at[rows_at(low + quarter(tile, flips) * 8, 8), :],
                    landed.at[pl.ds(BASES[4] + flips * 8 - 8, 8), :],
                    flipped(tile, flips),
                )
        elif stage == 4:
            place = total.at[rows_at(core * 256 + low + quarter(tile) * 8, 8), :]
            for flips in (2, 4, 6):
                send(tile, 5, place, place, flipped(tile, flips))
        elif stage < 9:
            if stage > 5:
                low = low - bits[order[8 - stage]] * COUNTS[stage]
                lows[tile] = low
            place = total.at[rows_at(core * 256 + low, COUNTS[stage + 1]), :]
            send(tile, stage + 1, place, place, across([order[7 - stage]]) if stage < 8 else sibling)

    for tile in range(TILES):
        begin(tile)
    for tile, stage in arrival_order():
        advance(tile, stage)
    for tile in range(TILES):
        for stage in range(STAGES):
            wait(tile, stage, send_sem, COUNTS)


def sum_products(partial):
    f32 = jnp.float32
    whole = pl.BlockSpec(memory_space=pltpu.VMEM)
    dma = pltpu.SemaphoreType.DMA
    return pl.pallas_call(
        sum_kernel,
        out_shape=jax.ShapeDtypeStruct((TILES, 512, 128), f32),
        in_specs=[whole],
        out_specs=whole,
        scratch_shapes=[
            pltpu.VMEM((TILES, 256, 128), f32),
            pltpu.VMEM((TILES, 544, 128), f32),
            dma((TILES, STAGES)),
            dma((TILES, STAGES)),
        ],
        compiler_params=pltpu.CompilerParams(
            vmem_limit_bytes=VMEM_LIMIT, collective_id=1, has_side_effects=True
        ),
        name="sum_products",
    )(partial)


def update_kernel(slot_ref, g_ref, first_ref, second_ref, x_ref, tri_ref, vectors_ref, out_ref, left_ref, change_ref):
    def parts(tiles_ref):
        joined = jnp.concatenate([tiles_ref[0], tiles_ref[1]], axis=1)
        return joined[0:256], joined[256:512]

    @pl.when(pl.program_id(0) == 0)
    def _():
        cross = complex_dot(left_forms(*parts(g_ref)), right_forms(*adjoint_upper(tri_ref, 0)))
        cross = right_forms(*cross)

        def correct_rows(step, carry):
            rows = pl.ds(pl.multiple_of(step * 256, 256), 256)
            second = left_forms(x_ref[0, rows, 256:512], x_ref[1, rows, 256:512])
            real_part, imag_part = complex_dot(second, cross)
            first = left_forms(x_ref[0, rows, 0:256] - real_part, x_ref[1, rows, 0:256] - imag_part)
            for form in range(3):
                for piece in range(2):
                    left_ref[form, piece, rows, 0:256] = first[form][piece]
                    left_ref[form, piece, rows, 256:512] = second[form][piece]
            return carry

        lax.fori_loop(0, 4, correct_rows, 0)

    left = [(left_ref[form, 0], left_ref[form, 1]) for form in range(3)]
    first = parts(first_ref)
    second = parts(second_ref)
    summed = [jnp.concatenate([first[part], second[part]], axis=0) for part in range(2)]
    change_ref[0], change_ref[1] = complex_dot(left, right_forms(*summed))

    def put_block(slot, carry):
        rows = pl.ds(pl.multiple_of(slot_ref[1, slot] * 8, 8), 8)
        near = pl.ds(pl.multiple_of(slot * 8, 8), 8)
        for part in range(2):
            out_ref[part, rows, :] = vectors_ref[part, rows, :] - change_ref[part, near, :]
        return carry

    lax.fori_loop(0, 128, put_block, 0, unroll=8)


def update(slots, total, scaled, tri_factors, vectors):
    whole = pl.BlockSpec(memory_space=pltpu.VMEM)
    columns = pl.BlockSpec((2, 1024, 256), lambda step: (0, 0, step))
    return pl.pallas_call(
        update_kernel,
        grid=(4,),
        out_shape=jax.ShapeDtypeStruct(vectors.shape, jnp.float32),
        in_specs=[
            pl.BlockSpec(memory_space=pltpu.SMEM),
            pl.BlockSpec((2, 512, 128), lambda step: (8, 0, 0)),
            pl.BlockSpec((2, 512, 128), lambda step: (step, 0, 0)),
            pl.BlockSpec((2, 512, 128), lambda step: (step + 4, 0, 0)),
            whole,
            whole,
            columns,
        ],
        out_specs=columns,
        scratch_shapes=[pltpu.VMEM((3, 2, 1024, 512), jnp.bfloat16), pltpu.VMEM((2, 1024, 256), jnp.float32)],
        compiler_params=pltpu.CompilerParams(vmem_limit_bytes=VMEM_LIMIT, dimension_semantics=("arbitrary",)),
        name="update",
    )(slots, total, total, total, scaled, tri_factors, vectors)


def per_device(vectors, panel_store, block_ids, offsets, tri_factors):
    partial, scaled, slots = products(vectors, panel_store, block_ids, offsets, tri_factors)
    total = sum_products(partial)
    return update(slots, total, scaled, tri_factors, vectors)


def solution(mesh):
    placed = (
        P(None, ("row", "col"), None),
        P(None, None, ("row", "col"), None),
        P(None, ("row", "col")),
        P(),
        P(),
    )
    return jax.shard_map(
        per_device,
        mesh=mesh,
        in_specs=placed,
        out_specs=P(None, ("row", "col"), None),
        check_vma=False,
    )
```

```python
import jax
import jax.numpy as jnp
from jax import lax
from jax.experimental import pallas as pl
from jax.experimental.pallas import tpu as pltpu
from jax.sharding import PartitionSpec as P


MESH = pl.DeviceIdType.MESH


def strip_of(x, y, z, core):
    return ((x * 2 + z % 2) * 4 + y) * 4 + (z // 2) * 2 + core


VMEM_LIMIT = 60 * 1024 * 1024


def split(value):
    high = value.astype(jnp.bfloat16)
    return high, (value - high.astype(jnp.float32)).astype(jnp.bfloat16)


def dot(first_op, second_op):
    return jnp.dot(first_op, second_op, preferred_element_type=jnp.float32)


def left_pieces(value):
    high, low = split(value)
    return jnp.concatenate([high, high, low], axis=1)


def right_pieces(value):
    high, low = split(value)
    return jnp.concatenate([high, low, high], axis=0)


def left_forms(real_part, imag_part):
    return left_pieces(real_part + imag_part), left_pieces(real_part), left_pieces(imag_part)


def right_forms(real_part, imag_part):
    return right_pieces(real_part), right_pieces(imag_part - real_part), right_pieces(real_part + imag_part)


def complex_dot(left, right):
    shared = dot(left[0], right[0])
    return shared - dot(left[2], right[2]), shared + dot(left[1], right[1])


def adjoint_upper(tri_ref, panel):
    shape = tri_ref.shape[2:]
    upper = lax.broadcasted_iota(jnp.int32, shape, 0) <= lax.broadcasted_iota(jnp.int32, shape, 1)
    return jnp.where(upper, tri_ref[panel, 0], 0.0).T, -jnp.where(upper, tri_ref[panel, 1], 0.0).T


GROUPS = (
    ((0, 64), (64, 64)),
    ((0, 64), (64, 32), (96, 16), (112, 16)),
)


def product_kernel(
    offsets_ref,
    ids_ref,
    store_ref,
    tri_ref,
    vectors_ref,
    y_out_ref,
    x_out_ref,
    slot_out_ref,
    z_ref,
    first_blocks_ref,
    second_blocks_ref,
    all_ids_ref,
    order_ref,
    slot_ref,
    first_panel_ref,
    second_panel_ref,
    rows_ref,
    match_ref,
    left_ref,
    factor_ref,
    y_ref,
    x_ref,
    block_send_sem,
    block_recv_sem,
    id_send_sem,
    id_recv_sem,
    local_sem,
):
    blocks_refs = (first_blocks_ref, second_blocks_ref)
    panel_refs = (first_panel_ref, second_panel_ref)
    row = lax.axis_index("row")
    col = lax.axis_index("col")
    me = row * 4 + col
    x = row // 8
    y = row % 4
    z = (col // 2) * 2 + (row // 4) % 2
    core = col % 2

    barrier = pltpu.get_barrier_semaphore()

    def greet(step, carry):
        peer = (me + step) % 128
        pl.semaphore_signal(barrier, inc=1, device_id=(peer // 4, peer % 4), device_id_type=MESH)
        return carry

    lax.fori_loop(1, 128, greet, 0)

    def listed(strip):
        return pl.ds(pl.multiple_of(strip * 8, 8), 8)

    own_copies = [
        pltpu.make_async_copy(store_ref.at[panel, :, listed(me), :], blocks_refs[panel].at[0], local_sem.at[panel])
        for panel in range(2)
    ]
    own_copies.append(pltpu.make_async_copy(ids_ref, all_ids_ref.at[0], local_sem.at[2]))
    for copy in own_copies:
        copy.start()
    fetch_vectors = pltpu.make_async_copy(vectors_ref, z_ref, local_sem.at[3])
    fetch_vectors.start()
    pl.semaphore_wait(barrier, 127)

    def strip_at(step, sign):
        spread = (step // 2 * 27) % 64
        return strip_of(
            (x + sign * (spread % 4) + 4) % 4,
            (y + sign * ((spread // 4) % 4) + 4) % 4,
            (z + sign * (spread // 16) + 4) % 4,
            (core + step) % 2,
        )

    def block_copy(panel, step):
        strip = strip_at(step, 1)
        return pltpu.make_async_remote_copy(
            store_ref.at[panel, :, listed(strip), :],
            blocks_refs[panel].at[step],
            block_send_sem.at[panel, step],
            block_recv_sem.at[panel, step],
            device_id=(strip // 4, strip % 4),
            device_id_type=MESH,
        )

    def id_copy(step):
        strip = strip_at(step, 1)
        return pltpu.make_async_remote_copy(
            ids_ref,
            all_ids_ref.at[step],
            id_send_sem.at[step],
            id_recv_sem.at[step],
            device_id=(strip // 4, strip % 4),
            device_id_type=MESH,
        )

    def send_ids(step, carry):
        id_copy(step).start()
        return carry

    def send_blocks(panel, first, last):
        def body(step, carry):
            block_copy(panel, step).start()
            return carry

        lax.fori_loop(first, last, body, 0)

    send_blocks(0, 1, 24)
    lax.fori_loop(1, 128, send_ids, 0)
    send_blocks(0, 24, 128)
    send_blocks(1, 1, 128)

    for panel in range(2):
        forms = right_forms(*adjoint_upper(tri_ref, panel))
        for form in range(3):
            factor_ref[panel, form] = forms[form]

    for copy in own_copies:
        copy.wait()

    def wait_ids(step, carry):
        id_copy(step).wait_recv()
        return carry

    lax.fori_loop(1, 128, wait_ids, 0)
    down = lax.broadcasted_iota(jnp.int32, (128, 128), 0)
    lane = lax.broadcasted_iota(jnp.int32, (128, 128), 1)
    order_ref[...] = jnp.zeros_like(order_ref)
    places = []
    for panel in range(2):
        own = jnp.sum(jnp.where(lane == me, all_ids_ref[:, panel, :], 0), axis=1, keepdims=True) % 128
        places.append(jnp.sum(jnp.where(down == lane, own, 0), axis=0, keepdims=True))
        order_ref[panel : panel + 1, :] = places[panel]
    slot_of_place = jnp.max(jnp.where(places[0] == down, lane, 0), axis=1, keepdims=True)
    order_ref[2:3, :] = jnp.max(jnp.where(places[1] == down, slot_of_place, 0), axis=0, keepdims=True)
    fetch_order = pltpu.make_async_copy(order_ref, slot_ref, local_sem.at[4])
    fetch_order.start()
    fetch_order.wait()
    write_order = pltpu.make_async_copy(order_ref, slot_out_ref, local_sem.at[5])
    write_order.start()
    fetch_vectors.wait()

    def take_group(panel, first, count):
        size = count * 8
        start = first * 8
        begin = first == 0
        values = panel_refs[panel]

        def wait_block(step, carry):
            block_copy(panel, step).wait_recv()
            return carry

        lax.fori_loop(max(first, 1), first + count, wait_block, 0)

        def take_block(step, carry):
            slot = first + step
            place = slot_ref[panel, slot]
            near = pl.ds(pl.multiple_of(step * 8, 8), 8)
            row_index = me * 1024 + place * 8 + lax.broadcasted_iota(jnp.int32, (8, 256), 0)
            limit = offsets_ref[panel] + lax.broadcasted_iota(jnp.int32, (8, 256), 1)
            below = row_index > limit
            diagonal = jnp.where(row_index == limit, 1.0, 0.0)
            values[0, slot] = jnp.where(below, blocks_refs[panel][slot, 0], diagonal)
            values[1, slot] = jnp.where(below, blocks_refs[panel][slot, 1], 0.0)
            rows_ref[0, near, :] = z_ref[0, place]
            rows_ref[1, near, :] = z_ref[1, place]
            if panel == 1:
                matching = slot_ref[2, slot]
                match_ref[0, near, :] = first_panel_ref[0, matching]
                match_ref[1, near, :] = first_panel_ref[1, matching]
            return carry

        lax.fori_loop(0, count, take_block, 0, unroll=4)

        own = [values[part, first : first + count].reshape(size, 256) for part in range(2)]
        forms = left_forms(own[0].T, -own[1].T)
        for form in range(3):
            left_ref[form, :, 0 : 3 * size] = forms[form]

        def adjoint_products(right):
            return complex_dot([left_ref[form, :, 0 : 3 * size] for form in range(3)], right)

        def add_tiles(tile, parts):
            for part in range(2):
                for side in range(2):
                    value = parts[part][:, side * 128 : (side + 1) * 128]
                    target = y_ref.at[tile + side, part * 256 : (part + 1) * 256, :]
                    if begin:
                        target[...] = value
                    else:
                        target[...] += value

        def take_columns(chunk, carry):
            columns = pl.ds(pl.multiple_of(chunk * 256, 256), 256)
            right = right_forms(rows_ref[0, 0:size, columns], rows_ref[1, 0:size, columns])
            add_tiles(4 * chunk + 2 * panel, adjoint_products(right))
            return carry

        lax.fori_loop(0, 4, take_columns, 0)

        if panel == 1:
            matched = (match_ref[0, 0:size, :], match_ref[1, 0:size, :])
            add_tiles(16, adjoint_products(right_forms(*matched)))
            for which, source in enumerate((matched, own)):
                scaled = complex_dot(left_forms(*source), [factor_ref[which, form] for form in range(3)])
                for part in range(2):
                    x_ref[part, start : start + size, which * 256 : (which + 1) * 256] = scaled[part]

    for panel in range(2):
        for first, count in GROUPS[panel]:
            take_group(panel, first, count)

    y_copy = pltpu.make_async_copy(y_ref, y_out_ref, local_sem.at[6])
    x_copy = pltpu.make_async_copy(x_ref, x_out_ref, local_sem.at[7])
    y_copy.start()
    x_copy.start()

    def wait_sent(step, carry):
        id_copy(step).wait_send()
        block_copy(0, step).wait_send()
        block_copy(1, step).wait_send()
        return carry

    lax.fori_loop(1, 128, wait_sent, 0)
    write_order.wait()
    y_copy.wait()
    x_copy.wait()


def products(vectors, panel_store, block_ids, offsets, tri_factors):
    f32 = jnp.float32
    bf16 = jnp.bfloat16
    whole = pl.BlockSpec(memory_space=pltpu.VMEM)
    anywhere = pl.BlockSpec(memory_space=pl.ANY)
    dma = pltpu.SemaphoreType.DMA
    return pl.pallas_call(
        product_kernel,
        out_shape=(
            jax.ShapeDtypeStruct((TILES, 512, 128), f32),
            jax.ShapeDtypeStruct((2, 1024, 512), f32),
            jax.ShapeDtypeStruct((8, 128), jnp.int32),
        ),
        in_specs=[pl.BlockSpec(memory_space=pltpu.SMEM), whole, anywhere, whole, anywhere],
        out_specs=[anywhere] * 3,
        scratch_shapes=[
            pltpu.VMEM((2, 128, 8, 1024), f32),
            pltpu.VMEM((128, 2, 8, 256), f32),
            pltpu.VMEM((128, 2, 8, 256), f32),
            pltpu.VMEM((128, 2, 128), jnp.int32),
            pltpu.VMEM((8, 128), jnp.int32),
            pltpu.SMEM((8, 128), jnp.int32),
            pltpu.VMEM((2, 128, 8, 256), f32),
            pltpu.VMEM((2, 128, 8, 256), f32),
            pltpu.VMEM((2, 512, 1024), f32),
            pltpu.VMEM((2, 512, 256), f32),
            pltpu.VMEM((3, 256, 1536), bf16),
            pltpu.VMEM((2, 3, 768, 256), bf16),
            pltpu.VMEM((TILES, 512, 128), f32),
            pltpu.VMEM((2, 1024, 512), f32),
            dma((2, 128)),
            dma((2, 128)),
            dma((128,)),
            dma((128,)),
            dma((8,)),
        ],
        compiler_params=pltpu.CompilerParams(
            vmem_limit_bytes=VMEM_LIMIT, collective_id=0, has_side_effects=True
        ),
        name="products",
    )(offsets, block_ids, panel_store, tri_factors, vectors.reshape(2, 128, 8, 1024))


TILES = 18
STAGES = 10
COUNTS = [256, 128, 64, 32, 56, 24, 32, 64, 128, 256]
BASES = [0, 256, 384, 448, 480]


FIRST_TILES = 9


def step_order():
    sent = 0.0
    free = [0.0] * 7
    now = 0.0
    ready = []
    order = []
    waiting = list(range(TILES - 2, TILES)) + list(range(TILES - 2))

    def send(tile, stage):
        nonlocal sent, now
        size = COUNTS[stage] * 0.512
        now += 0.05 * {4: 7, 5: 3}.get(stage, 1)
        sent = max(sent, now) + size / 230
        arrival = sent
        if stage not in (4, 5):
            link = 6 if stage in (0, 9) else (tile + (stage - 1 if stage < 4 else 8 - stage)) % 6
            free[link] = max(free[link], sent - size / 230) + size / (600 if link == 6 else 50)
            arrival = max(arrival, free[link])
        ready.append((arrival + 1.5, tile, stage))

    def start():
        if waiting:
            tile = waiting.pop(0)
            order.append((tile, 0))
            send(tile, 0)

    for _ in range(FIRST_TILES):
        start()
    while ready:
        ready.sort()
        arrival, tile, stage = ready.pop(0)
        order.append((tile, stage + 1))
        now = max(now, arrival) + 0.12
        if stage < STAGES - 1:
            send(tile, stage + 1)
        if stage == 2:
            start()
    return order


def sum_kernel(part_ref, total_ref, held_ref, landed_ref, send_sem, recv_sem):
    row = lax.axis_index("row")
    col = lax.axis_index("col")
    here = (row // 8, row % 4, (col // 2) * 2 + (row // 4) % 2)
    core = col % 2

    def device(place, core):
        strip = strip_of(*place, core)
        return (strip // 4, strip % 4)

    sibling = device(here, 1 - core)
    other = [place + 1 - 2 * (place % 2) for place in here] + [3 - place for place in here]
    bits = [((place + 1) // 2) % 2 for place in here] + [place // 2 for place in here]

    def across(links):
        place = list(here)
        for link in links:
            place[link % 3] = other[link]
        return device(place, core)

    barrier = pltpu.get_barrier_semaphore()
    peers = [sibling]
    for first in (None, 0, 3):
        for second in (None, 1, 4):
            for third in (None, 2, 5):
                chosen = [link for link in (first, second, third) if link is not None]
                if chosen:
                    peers.append(across(chosen))
    for peer in peers:
        pl.semaphore_signal(barrier, inc=1, device_id=peer, device_id_type=MESH)
    pl.semaphore_wait(barrier, len(peers))

    def rows_at(first, count):
        return pl.ds(pl.multiple_of(first, 8), count)

    def send(tile, stage, source, target, peer):
        pltpu.make_async_remote_copy(
            source,
            target,
            send_sem.at[tile, stage],
            recv_sem.at[tile, stage],
            device_id=peer,
            device_id_type=MESH,
        ).start()

    def wait(tile, stage, sem, counts):
        some = landed_ref.at[tile, pl.ds(0, counts[stage]), :]
        pltpu.make_async_copy(some, some, sem.at[tile, stage]).wait()

    def order_of(tile):
        return [(tile + step) % 6 for step in range(6)]

    def quarter(tile, flips=0):
        first, second = order_of(tile)[3:5]
        high = 1 - bits[first] if flips & 4 else bits[first]
        low = 1 - bits[second] if flips & 2 else bits[second]
        return high * 2 + low

    def flipped(tile, flips):
        return across([link for place, link in enumerate(order_of(tile)[3:]) if flips & (4 >> place)])

    lows = [0] * TILES

    def begin(tile):
        send(
            tile,
            0,
            part_ref.at[tile, rows_at((1 - core) * 256, 256), :],
            landed_ref.at[tile, pl.ds(0, 256), :],
            sibling,
        )

    def advance(tile, stage):
        order = order_of(tile)
        low = lows[tile]
        held = held_ref.at[tile]
        landed = landed_ref.at[tile]
        total = total_ref.at[tile]
        wait(tile, stage, recv_sem, COUNTS)
        if stage == 0:
            held[...] = part_ref[tile, rows_at(core * 256, 256), :] + landed[0:256, :]
        elif stage < 4:
            size = COUNTS[stage]
            held[rows_at(low, size), :] += landed[BASES[stage] : BASES[stage] + size, :]
        elif stage == 4:
            final = held[rows_at(low + quarter(tile) * 8, 8), :]
            for flips in range(1, 8):
                final += landed[BASES[4] + flips * 8 - 8 : BASES[4] + flips * 8, :]
            total[rows_at(core * 256 + low + quarter(tile) * 8, 8), :] = final
        if stage < 3:
            size = COUNTS[stage + 1]
            link = order[stage]
            keep = bits[link]
            send(
                tile,
                stage + 1,
                held.at[rows_at(low + (1 - keep) * size, size), :],
                landed.at[pl.ds(BASES[stage + 1], size), :],
                across([link]),
            )
            lows[tile] = low + keep * size
        elif stage == 3:
            for flips in range(1, 8):
                send(
                    tile,
                    4,
                    held.at[rows_at(low + quarter(tile, flips) * 8, 8), :],
                    landed.at[pl.ds(BASES[4] + flips * 8 - 8, 8), :],
                    flipped(tile, flips),
                )
        elif stage == 4:
            place = total.at[rows_at(core * 256 + low + quarter(tile) * 8, 8), :]
            for flips in (2, 4, 6):
                send(tile, 5, place, place, flipped(tile, flips))
        elif stage < 9:
            if stage > 5:
                low = low - bits[order[8 - stage]] * COUNTS[stage]
                lows[tile] = low
            place = total.at[rows_at(core * 256 + low, COUNTS[stage + 1]), :]
            send(tile, stage + 1, place, place, across([order[7 - stage]]) if stage < 8 else sibling)

    for tile, step in step_order():
        if step == 0:
            begin(tile)
        else:
            advance(tile, step - 1)
    for tile in range(TILES):
        for stage in range(STAGES):
            wait(tile, stage, send_sem, COUNTS)


def sum_products(partial):
    f32 = jnp.float32
    whole = pl.BlockSpec(memory_space=pltpu.VMEM)
    dma = pltpu.SemaphoreType.DMA
    return pl.pallas_call(
        sum_kernel,
        out_shape=jax.ShapeDtypeStruct((TILES, 512, 128), f32),
        in_specs=[whole],
        out_specs=whole,
        scratch_shapes=[
            pltpu.VMEM((TILES, 256, 128), f32),
            pltpu.VMEM((TILES, 544, 128), f32),
            dma((TILES, STAGES)),
            dma((TILES, STAGES)),
        ],
        compiler_params=pltpu.CompilerParams(
            vmem_limit_bytes=VMEM_LIMIT, collective_id=1, has_side_effects=True
        ),
        name="sum_products",
    )(partial)


def update_kernel(slot_ref, g_ref, y_ref, x_ref, tri_ref, vectors_ref, out_ref, left_ref, change_ref):
    def parts(tiles_ref, first):
        joined = jnp.concatenate([tiles_ref[first], tiles_ref[first + 1]], axis=1)
        return joined[0:256], joined[256:512]

    @pl.when(pl.program_id(0) == 0)
    def _():
        cross = complex_dot(left_forms(*parts(g_ref, 0)), right_forms(*adjoint_upper(tri_ref, 0)))
        cross = right_forms(*cross)

        def correct_rows(step, carry):
            rows = pl.ds(pl.multiple_of(step * 256, 256), 256)
            second = left_forms(x_ref[0, rows, 256:512], x_ref[1, rows, 256:512])
            real_part, imag_part = complex_dot(second, cross)
            first = left_forms(x_ref[0, rows, 0:256] - real_part, x_ref[1, rows, 0:256] - imag_part)
            for form in range(3):
                for piece in range(3):
                    start = piece * 512
                    left_ref[form, rows, start : start + 256] = first[form][:, piece * 256 : (piece + 1) * 256]
                    left_ref[form, rows, start + 256 : start + 512] = second[form][:, piece * 256 : (piece + 1) * 256]
            return carry

        lax.fori_loop(0, 4, correct_rows, 0)

    left = [left_ref[form] for form in range(3)]
    first = parts(y_ref, 0)
    second = parts(y_ref, 2)
    summed = [jnp.concatenate([first[part], second[part]], axis=0) for part in range(2)]
    change_ref[0], change_ref[1] = complex_dot(left, right_forms(*summed))

    def put_block(slot, carry):
        rows = pl.ds(pl.multiple_of(slot_ref[1, slot] * 8, 8), 8)
        near = pl.ds(pl.multiple_of(slot * 8, 8), 8)
        for part in range(2):
            out_ref[part, rows, :] = vectors_ref[part, rows, :] - change_ref[part, near, :]
        return carry

    lax.fori_loop(0, 128, put_block, 0, unroll=8)


def update(slots, total, scaled, tri_factors, vectors):
    whole = pl.BlockSpec(memory_space=pltpu.VMEM)
    columns = pl.BlockSpec((2, 1024, 256), lambda step: (0, 0, step))
    return pl.pallas_call(
        update_kernel,
        grid=(4,),
        out_shape=jax.ShapeDtypeStruct(vectors.shape, jnp.float32),
        in_specs=[
            pl.BlockSpec(memory_space=pltpu.SMEM),
            pl.BlockSpec((2, 512, 128), lambda step: (8, 0, 0)),
            pl.BlockSpec((4, 512, 128), lambda step: (step, 0, 0)),
            whole,
            whole,
            columns,
        ],
        out_specs=columns,
        scratch_shapes=[pltpu.VMEM((3, 1024, 1536), jnp.bfloat16), pltpu.VMEM((2, 1024, 256), jnp.float32)],
        compiler_params=pltpu.CompilerParams(vmem_limit_bytes=VMEM_LIMIT, dimension_semantics=("arbitrary",)),
        name="update",
    )(slots, total, total, scaled, tri_factors, vectors)


def per_device(vectors, panel_store, block_ids, offsets, tri_factors):
    partial, scaled, slots = products(vectors, panel_store, block_ids, offsets, tri_factors)
    total = sum_products(partial)
    return update(slots, total, scaled, tri_factors, vectors)


def solution(mesh):
    placed = (
        P(None, ("row", "col"), None),
        P(None, None, ("row", "col"), None),
        P(None, ("row", "col")),
        P(),
        P(),
    )
    return jax.shard_map(
        per_device,
        mesh=mesh,
        in_specs=placed,
        out_specs=P(None, ("row", "col"), None),
        check_vma=False,
    )
```

```python
import jax
import jax.numpy as jnp
from jax import lax
from jax.experimental import pallas as pl
from jax.experimental.pallas import tpu as pltpu
from jax.sharding import PartitionSpec as P


MESH = pl.DeviceIdType.MESH


def strip_of(x, y, z, core):
    return ((x * 2 + z % 2) * 4 + y) * 4 + (z // 2) * 2 + core


VMEM_LIMIT = 60 * 1024 * 1024


def split(value):
    high = value.astype(jnp.bfloat16)
    return high, (value - high.astype(jnp.float32)).astype(jnp.bfloat16)


def dot(first_op, second_op):
    return jnp.dot(first_op, second_op, preferred_element_type=jnp.float32)


def left_pieces(value):
    high, low = split(value)
    return jnp.concatenate([high, high, low], axis=1)


def right_pieces(value):
    high, low = split(value)
    return jnp.concatenate([high, low, high], axis=0)


def left_forms(real_part, imag_part):
    return left_pieces(real_part + imag_part), left_pieces(real_part), left_pieces(imag_part)


def right_forms(real_part, imag_part):
    return right_pieces(real_part), right_pieces(imag_part - real_part), right_pieces(real_part + imag_part)


def complex_dot(left, right):
    shared = dot(left[0], right[0])
    return shared - dot(left[2], right[2]), shared + dot(left[1], right[1])


def adjoint_upper(tri_ref, panel):
    shape = tri_ref.shape[2:]
    upper = lax.broadcasted_iota(jnp.int32, shape, 0) <= lax.broadcasted_iota(jnp.int32, shape, 1)
    return jnp.where(upper, tri_ref[panel, 0], 0.0).T, -jnp.where(upper, tri_ref[panel, 1], 0.0).T


GROUPS = (
    ((0, 64), (64, 64)),
    ((0, 64), (64, 32), (96, 16), (112, 16)),
)


def product_kernel(
    offsets_ref,
    ids_ref,
    store_ref,
    tri_ref,
    vectors_ref,
    y_out_ref,
    x_out_ref,
    slot_out_ref,
    z_ref,
    first_blocks_ref,
    second_blocks_ref,
    relay_ref,
    all_ids_ref,
    order_ref,
    slot_ref,
    first_panel_ref,
    second_panel_ref,
    rows_ref,
    match_ref,
    left_ref,
    factor_ref,
    y_ref,
    x_ref,
    block_send_sem,
    block_recv_sem,
    id_send_sem,
    id_recv_sem,
    hop_send_sem,
    hop_recv_sem,
    last_send_sem,
    local_sem,
):
    blocks_refs = (first_blocks_ref, second_blocks_ref)
    panel_refs = (first_panel_ref, second_panel_ref)
    row = lax.axis_index("row")
    col = lax.axis_index("col")
    me = row * 4 + col
    x = row // 8
    y = row % 4
    z = (col // 2) * 2 + (row // 4) % 2
    core = col % 2

    barrier = pltpu.get_barrier_semaphore()

    def greet(step, carry):
        peer = (me + step) % 128
        pl.semaphore_signal(barrier, inc=1, device_id=(peer // 4, peer % 4), device_id_type=MESH)
        return carry

    lax.fori_loop(1, 128, greet, 0)

    def listed(strip):
        return pl.ds(pl.multiple_of(strip * 8, 8), 8)

    own_copies = [
        pltpu.make_async_copy(store_ref.at[panel, :, listed(me), :], blocks_refs[panel].at[0], local_sem.at[panel])
        for panel in range(2)
    ]
    own_copies.append(pltpu.make_async_copy(ids_ref, all_ids_ref.at[0], local_sem.at[2]))
    for copy in own_copies:
        copy.start()
    fetch_vectors = pltpu.make_async_copy(vectors_ref, z_ref, local_sem.at[3])
    fetch_vectors.start()
    pl.semaphore_wait(barrier, 127)

    def offset(step):
        spread = (step // 2 * 27) % 64
        return spread % 4, (spread // 4) % 4, spread // 16

    def opposite(shift):
        return (shift // 2) * (1 - shift % 2)

    def strip_at(step):
        dx, dy, dz = offset(step)
        return strip_of((x + dx) % 4, (y + dy) % 4, (z + dz) % 4, (core + step) % 2)

    def is_opposite(step):
        dx, dy, dz = offset(step)
        return opposite(dx) + opposite(dy) + opposite(dz) > 0

    def is_relayed(step):
        dx, dy, dz = offset(step)
        return (opposite(dx) + opposite(dy) + opposite(dz)) * (step % 2) > 0

    def relay_of(step):
        dx, dy, dz = offset(step)
        return strip_of((x + opposite(dx)) % 4, (y + opposite(dy)) % 4, (z + opposite(dz)) % 4, core)

    def relayed_target(step):
        dx, dy, dz = offset(step)
        return strip_of(
            (x + 4 - opposite(dx) + dx) % 4,
            (y + 4 - opposite(dy) + dy) % 4,
            (z + 4 - opposite(dz) + dz) % 4,
            (core + step) % 2,
        )

    def remote(source, target, sent, received, strip):
        return pltpu.make_async_remote_copy(
            source,
            target,
            sent,
            received,
            device_id=(strip // 4, strip % 4),
            device_id_type=MESH,
        )

    def block_copy(panel, step):
        strip = strip_at(step)
        return remote(
            store_ref.at[panel, :, listed(strip), :],
            blocks_refs[panel].at[step],
            block_send_sem.at[panel, step],
            block_recv_sem.at[panel, step],
            strip,
        )

    def hop_copy(step):
        return remote(
            store_ref.at[:, :, listed(strip_at(step)), :],
            relay_ref.at[step // 2],
            hop_send_sem.at[step // 2],
            hop_recv_sem.at[step // 2],
            relay_of(step),
        )

    def last_copy(panel, step):
        return remote(
            relay_ref.at[step // 2, panel],
            blocks_refs[panel].at[step],
            last_send_sem.at[panel, step // 2],
            block_recv_sem.at[panel, step],
            relayed_target(step),
        )

    def id_copy(step):
        return remote(ids_ref, all_ids_ref.at[step], id_send_sem.at[step], id_recv_sem.at[step], strip_at(step))

    def send_ids(step, carry):
        id_copy(step).start()
        return carry

    def send_opposite(step, carry):
        @pl.when(is_relayed(step))
        def _():
            hop_copy(step).start()
            block_copy(0, step - 1).start()

        return carry

    def send_first(step, carry):
        @pl.when(jnp.logical_not(is_opposite(step)))
        def _():
            block_copy(0, step).start()

        return carry

    def send_second(step, carry):
        @pl.when(jnp.logical_not(is_relayed(step)))
        def _():
            block_copy(1, step).start()

        return carry

    def forward_first(step, carry):
        @pl.when(is_relayed(step))
        def _():
            hop_copy(step).wait_recv()
            last_copy(0, step).start()

        return carry

    def forward_second(step, carry):
        @pl.when(is_relayed(step))
        def _():
            last_copy(1, step).start()

        return carry

    lax.fori_loop(1, 128, send_opposite, 0)
    lax.fori_loop(1, 128, send_ids, 0)
    lax.fori_loop(1, 128, send_first, 0)

    for panel in range(2):
        forms = right_forms(*adjoint_upper(tri_ref, panel))
        for form in range(3):
            factor_ref[panel, form] = forms[form]

    for copy in own_copies:
        copy.wait()

    def wait_ids(step, carry):
        id_copy(step).wait_recv()
        return carry

    lax.fori_loop(1, 128, wait_ids, 0)
    down = lax.broadcasted_iota(jnp.int32, (128, 128), 0)
    lane = lax.broadcasted_iota(jnp.int32, (128, 128), 1)
    order_ref[...] = jnp.zeros_like(order_ref)
    places = []
    for panel in range(2):
        own = jnp.sum(jnp.where(lane == me, all_ids_ref[:, panel, :], 0), axis=1, keepdims=True) % 128
        places.append(jnp.sum(jnp.where(down == lane, own, 0), axis=0, keepdims=True))
        order_ref[panel : panel + 1, :] = places[panel]
        order_ref[panel + 3 : panel + 4, :] = jnp.max(jnp.where(own == lane, down, 0), axis=0, keepdims=True)
    slot_of_place = jnp.max(jnp.where(places[0] == down, lane, 0), axis=1, keepdims=True)
    order_ref[2:3, :] = jnp.max(jnp.where(places[1] == down, slot_of_place, 0), axis=0, keepdims=True)
    fetch_order = pltpu.make_async_copy(order_ref, slot_ref, local_sem.at[4])
    fetch_order.start()
    fetch_order.wait()
    write_order = pltpu.make_async_copy(order_ref, slot_out_ref, local_sem.at[5])
    write_order.start()
    fetch_vectors.wait()

    def take_group(panel, first, count):
        size = count * 8
        start = first * 8
        begin = first == 0
        values = panel_refs[panel]

        def wait_block(step, carry):
            block_copy(panel, step).wait_recv()
            return carry

        lax.fori_loop(max(first, 1), first + count, wait_block, 0)

        def take_block(step, carry):
            slot = first + step
            place = slot_ref[panel, slot]
            near = pl.ds(pl.multiple_of(step * 8, 8), 8)
            row_index = me * 1024 + place * 8 + lax.broadcasted_iota(jnp.int32, (8, 256), 0)
            limit = offsets_ref[panel] + lax.broadcasted_iota(jnp.int32, (8, 256), 1)
            below = row_index > limit
            diagonal = jnp.where(row_index == limit, 1.0, 0.0)
            values[0, slot] = jnp.where(below, blocks_refs[panel][slot, 0], diagonal)
            values[1, slot] = jnp.where(below, blocks_refs[panel][slot, 1], 0.0)
            rows_ref[0, near, :] = z_ref[0, place]
            rows_ref[1, near, :] = z_ref[1, place]
            if panel == 1:
                matching = slot_ref[2, slot]
                match_ref[0, near, :] = first_panel_ref[0, matching]
                match_ref[1, near, :] = first_panel_ref[1, matching]
            return carry

        lax.fori_loop(0, count, take_block, 0, unroll=4)

        own = [values[part, first : first + count].reshape(size, 256) for part in range(2)]
        forms = left_forms(own[0].T, -own[1].T)
        for form in range(3):
            left_ref[form, :, 0 : 3 * size] = forms[form]

        def adjoint_products(right):
            return complex_dot([left_ref[form, :, 0 : 3 * size] for form in range(3)], right)

        def add_tiles(tile, parts):
            for part in range(2):
                for side in range(2):
                    value = parts[part][:, side * 128 : (side + 1) * 128]
                    target = y_ref.at[tile + side, part * 256 : (part + 1) * 256, :]
                    if begin:
                        target[...] = value
                    else:
                        target[...] += value

        def take_columns(chunk, carry):
            columns = pl.ds(pl.multiple_of(chunk * 256, 256), 256)
            right = right_forms(rows_ref[0, 0:size, columns], rows_ref[1, 0:size, columns])
            add_tiles(4 * chunk + 2 * panel, adjoint_products(right))
            return carry

        lax.fori_loop(0, 4, take_columns, 0)

        if panel == 1:
            matched = (match_ref[0, 0:size, :], match_ref[1, 0:size, :])
            add_tiles(16, adjoint_products(right_forms(*matched)))
            for which, source in enumerate((matched, own)):
                scaled = complex_dot(left_forms(*source), [factor_ref[which, form] for form in range(3)])
                for part in range(2):
                    x_ref[part, start : start + size, which * 256 : (which + 1) * 256] = scaled[part]

    lax.fori_loop(1, 128, forward_first, 0)
    lax.fori_loop(1, 128, send_second, 0)
    for panel in range(2):
        for first, count in GROUPS[panel]:
            take_group(panel, first, count)
            if panel == 0 and first == 0:
                lax.fori_loop(1, 128, forward_second, 0)

    y_copy = pltpu.make_async_copy(y_ref, y_out_ref, local_sem.at[6])
    x_copy = pltpu.make_async_copy(x_ref, x_out_ref, local_sem.at[7])
    y_copy.start()
    x_copy.start()

    def wait_sent(step, carry):
        id_copy(step).wait_send()
        relayed = is_relayed(step)

        @pl.when(relayed)
        def _():
            hop_copy(step).wait_send()
            last_copy(0, step).wait_send()
            last_copy(1, step).wait_send()

        @pl.when(jnp.logical_not(relayed))
        def _():
            block_copy(0, step).wait_send()
            block_copy(1, step).wait_send()

        return carry

    lax.fori_loop(1, 128, wait_sent, 0)
    write_order.wait()
    y_copy.wait()
    x_copy.wait()


def products(vectors, panel_store, block_ids, offsets, tri_factors):
    f32 = jnp.float32
    bf16 = jnp.bfloat16
    whole = pl.BlockSpec(memory_space=pltpu.VMEM)
    anywhere = pl.BlockSpec(memory_space=pl.ANY)
    dma = pltpu.SemaphoreType.DMA
    return pl.pallas_call(
        product_kernel,
        out_shape=(
            jax.ShapeDtypeStruct((18, 512, 128), f32),
            jax.ShapeDtypeStruct((2, 1024, 512), f32),
            jax.ShapeDtypeStruct((8, 128), jnp.int32),
        ),
        in_specs=[pl.BlockSpec(memory_space=pltpu.SMEM), whole, anywhere, whole, anywhere],
        out_specs=[anywhere] * 3,
        scratch_shapes=[
            pltpu.VMEM((2, 128, 8, 1024), f32),
            pltpu.VMEM((128, 2, 8, 256), f32),
            pltpu.VMEM((128, 2, 8, 256), f32),
            pltpu.VMEM((64, 2, 2, 8, 256), f32),
            pltpu.VMEM((128, 2, 128), jnp.int32),
            pltpu.VMEM((8, 128), jnp.int32),
            pltpu.SMEM((8, 128), jnp.int32),
            pltpu.VMEM((2, 128, 8, 256), f32),
            pltpu.VMEM((2, 128, 8, 256), f32),
            pltpu.VMEM((2, 512, 1024), f32),
            pltpu.VMEM((2, 512, 256), f32),
            pltpu.VMEM((3, 256, 1536), bf16),
            pltpu.VMEM((2, 3, 768, 256), bf16),
            pltpu.VMEM((18, 512, 128), f32),
            pltpu.VMEM((2, 1024, 512), f32),
            dma((2, 128)),
            dma((2, 128)),
            dma((128,)),
            dma((128,)),
            dma((64,)),
            dma((64,)),
            dma((2, 64)),
            dma((8,)),
        ],
        compiler_params=pltpu.CompilerParams(
            vmem_limit_bytes=VMEM_LIMIT, collective_id=0, has_side_effects=True
        ),
        name="products",
    )(offsets, block_ids, panel_store, tri_factors, vectors.reshape(2, 128, 8, 1024))


TILES = 9
LINKS = ((), (0,), (1, 2), (3, 4, 5))
HALF_STAGES = len(LINKS)
STAGES = 2 * HALF_STAGES
SIZES = [1024, 512, 256, 64, 8]
COUNTS = [SIZES[stage] - SIZES[stage + 1] for stage in range(HALF_STAGES)]
BASES = [sum(COUNTS[:stage]) for stage in range(HALF_STAGES)]


def level_of(stage):
    return stage if stage < HALF_STAGES else STAGES - 1 - stage


def step_order():
    free = [0.0] * 7
    now = 0.0
    ready = []
    order = []
    work = []
    finished = set()
    queued = set()

    def send(tile, stage):
        nonlocal now
        level = level_of(stage)
        now += 0.06 * (2 ** len(LINKS[level]) - 1 if level else 1)
        if level == 0:
            free[6] = max(free[6], now) + 512 * 0.512 / 600
            arrival = free[6]
        else:
            arrival = now
            for link in LINKS[level]:
                link = (tile + link) % 6
                free[link] = max(free[link], now) + SIZES[level] / 2 * 0.512 / 50
                arrival = max(arrival, free[link])
        ready.append((arrival + 2.5, tile, stage))

    for tile in [TILES - 1] + list(range(TILES - 1)):
        send(tile, 0)
    while ready or work:
        ready.sort()
        if ready and (ready[0][0] <= now or not work):
            arrival, tile, stage = ready.pop(0)
            order.append((tile, stage))
            now = max(now, arrival) + (0.05 + COUNTS[stage] * 0.0006 if stage < HALF_STAGES else 0.03)
            if stage < STAGES - 1:
                send(tile, stage + 1)
            else:
                finished.add(tile)
            if TILES - 1 in finished:
                if None not in queued:
                    queued.add(None)
                    work += [(None, piece) for piece in range(4)]
                for chunk in range(4):
                    if chunk not in queued and {2 * chunk, 2 * chunk + 1} <= finished:
                        queued.add(chunk)
                        work += [(-1 - chunk, piece) for piece in range(4)]
        else:
            order.append(work.pop(0))
            now += 0.8
    return order


def sum_kernel(
    slot_ref,
    part_ref,
    x_in_ref,
    tri_ref,
    vectors_ref,
    out_ref,
    total_ref,
    held_ref,
    landed_ref,
    x_ref,
    left_ref,
    cross_ref,
    right_ref,
    z_ref,
    change_ref,
    result_ref,
    send_sem,
    recv_sem,
    local_sem,
):
    row = lax.axis_index("row")
    col = lax.axis_index("col")
    here = (row // 8, row % 4, (col // 2) * 2 + (row // 4) % 2)
    core = col % 2

    fetch_x = pltpu.make_async_copy(x_in_ref, x_ref, local_sem.at[0])
    fetch_z = pltpu.make_async_copy(vectors_ref, z_ref, local_sem.at[1])

    def device(place, core):
        strip = strip_of(*place, core)
        return (strip // 4, strip % 4)

    sibling = device(here, 1 - core)
    other = [place + 1 - 2 * (place % 2) for place in here] + [3 - place for place in here]
    bits = [((place + 1) // 2) % 2 for place in here] + [place // 2 for place in here]

    def across(links):
        place = list(here)
        for link in links:
            place[link % 3] = other[link]
        return device(place, core)

    barrier = pltpu.get_barrier_semaphore()
    peers = [sibling]
    for first in (None, 0, 3):
        for second in (None, 1, 4):
            for third in (None, 2, 5):
                chosen = [link for link in (first, second, third) if link is not None]
                if chosen:
                    peers.append(across(chosen))
    for peer in peers:
        pl.semaphore_signal(barrier, inc=1, device_id=peer, device_id_type=MESH)
    pl.semaphore_wait(barrier, len(peers))

    def rows_at(first, count):
        return pl.ds(pl.multiple_of(first, 8), count)

    def send(tile, stage, source, target, peer):
        pltpu.make_async_remote_copy(
            source,
            target,
            send_sem.at[tile, stage],
            recv_sem.at[tile, stage],
            device_id=peer,
            device_id_type=MESH,
        ).start()

    def wait(tile, stage, sem):
        some = landed_ref.at[tile, pl.ds(0, COUNTS[level_of(stage)]), :]
        pltpu.make_async_copy(some, some, sem.at[tile, stage]).wait()

    def links_of(tile, level):
        return [(tile + link) % 6 for link in LINKS[level]]

    def share(tile, level, flips=0):
        index = 0
        for place, link in enumerate(links_of(tile, level)):
            index = index * 2 + (1 - bits[link] if flips >> place & 1 else bits[link])
        return index

    def flipped(tile, level, flips):
        return across([link for place, link in enumerate(links_of(tile, level)) if flips >> place & 1])

    lows = [0] * TILES

    def split_rows(tile, level):
        held = held_ref.at[tile]
        size = SIZES[level + 1]
        for flips in range(1, 2 ** len(LINKS[level])):
            send(
                tile,
                level,
                held.at[rows_at(lows[tile] + share(tile, level, flips) * size, size), :],
                landed_ref.at[tile, pl.ds(BASES[level] + (flips - 1) * size, size), :],
                flipped(tile, level, flips),
            )
        lows[tile] = lows[tile] + share(tile, level) * size

    def return_rows(tile, level):
        size = SIZES[level + 1]
        place = total_ref.at[tile, rows_at(core * 512 + lows[tile], size), :]
        for flips in range(1, 2 ** len(LINKS[level])):
            send(tile, STAGES - 1 - level, place, place, flipped(tile, level, flips))

    def advance(tile, stage):
        level = level_of(stage)
        held = held_ref.at[tile]
        wait(tile, stage, recv_sem)
        if stage == 0:
            held[...] = part_ref[tile, rows_at(core * 512, 512), :] + landed_ref[tile, 0:512, :]
            split_rows(tile, 1)
        elif stage < HALF_STAGES:
            size = SIZES[level + 1]
            value = held[rows_at(lows[tile], size), :]
            for piece in range(2 ** len(LINKS[level]) - 1):
                start = BASES[level] + piece * size
                value += landed_ref[tile, start : start + size, :]
            if stage < HALF_STAGES - 1:
                held[rows_at(lows[tile], size), :] = value
                split_rows(tile, level + 1)
            else:
                total_ref[tile, rows_at(core * 512 + lows[tile], size), :] = value
                return_rows(tile, level)
        elif stage < STAGES - 1:
            lows[tile] = lows[tile] - share(tile, level) * SIZES[level + 1]
            if level > 1:
                return_rows(tile, level - 1)
            else:
                place = total_ref.at[tile, rows_at(core * 512, 512), :]
                send(tile, STAGES - 1, place, place, sibling)

    def parts(tile):
        values = total_ref[tile]
        real_part = jnp.concatenate([values[0:256], values[512:768]], axis=1)
        imag_part = jnp.concatenate([values[256:512], values[768:1024]], axis=1)
        return real_part, imag_part

    def correct(piece):
        if piece == 0:
            fetch_x.wait()
            cross = complex_dot(left_forms(*parts(TILES - 1)), right_forms(*adjoint_upper(tri_ref, 0)))
            cross = right_forms(*cross)
            for form in range(3):
                cross_ref[form] = cross[form]
        rows = slice(piece * 256, (piece + 1) * 256)
        second = left_forms(x_ref[0, rows, 256:512], x_ref[1, rows, 256:512])
        real_part, imag_part = complex_dot(second, [cross_ref[form] for form in range(3)])
        first = left_forms(x_ref[0, rows, 0:256] - real_part, x_ref[1, rows, 0:256] - imag_part)
        for form in range(3):
            for part in range(3):
                start = part * 512
                left_ref[form, rows, start : start + 256] = first[form][:, part * 256 : (part + 1) * 256]
                left_ref[form, rows, start + 256 : start + 512] = second[form][:, part * 256 : (part + 1) * 256]

    written = []

    def apply(chunk, piece):
        if piece == 0:
            first = parts(2 * chunk)
            second = parts(2 * chunk + 1)
            forms = right_forms(*[jnp.concatenate([first[part], second[part]], axis=0) for part in range(2)])
            for form in range(3):
                right_ref[form] = forms[form]
        rows = slice(piece * 256, (piece + 1) * 256)
        change = complex_dot([left_ref[form, rows, :] for form in range(3)], [right_ref[form] for form in range(3)])
        for part in range(2):
            change_ref[part, piece * 32 : (piece + 1) * 32] = change[part].reshape(32, 8, 256)
        if piece < 3:
            return
        if not written:
            fetch_z.wait()
        if len(written) > 1:
            written[-2].wait()
        columns = slice(chunk * 256, (chunk + 1) * 256)
        result = result_ref.at[len(written) % 2]

        def put_block(block, carry):
            slot = slot_ref[4, block]
            rows = pl.ds(pl.multiple_of(block * 8, 8), 8)
            for part in range(2):
                result[part, rows, :] = z_ref[part, rows, columns] - change_ref[part, slot]
            return carry

        lax.fori_loop(0, 128, put_block, 0, unroll=8)
        copy = pltpu.make_async_copy(result, out_ref.at[:, :, columns], local_sem.at[2 + len(written)])
        copy.start()
        written.append(copy)

    for tile in [TILES - 1] + list(range(TILES - 1)):
        send(
            tile,
            0,
            part_ref.at[tile, rows_at((1 - core) * 512, 512), :],
            landed_ref.at[tile, pl.ds(0, 512), :],
            sibling,
        )
    fetch_x.start()
    fetch_z.start()
    for tile, step in step_order():
        if tile is None:
            correct(step)
        elif tile < 0:
            apply(-1 - tile, step)
        else:
            advance(tile, step)
    for tile in range(TILES):
        for stage in range(STAGES):
            wait(tile, stage, send_sem)
    for copy in written[-2:]:
        copy.wait()


def sum_and_update(slots, partial, scaled, tri_factors, vectors):
    f32 = jnp.float32
    bf16 = jnp.bfloat16
    whole = pl.BlockSpec(memory_space=pltpu.VMEM)
    anywhere = pl.BlockSpec(memory_space=pl.ANY)
    dma = pltpu.SemaphoreType.DMA
    return pl.pallas_call(
        sum_kernel,
        out_shape=jax.ShapeDtypeStruct(vectors.shape, f32),
        in_specs=[pl.BlockSpec(memory_space=pltpu.SMEM), whole, anywhere, whole, anywhere],
        out_specs=anywhere,
        scratch_shapes=[
            pltpu.VMEM((TILES, 1024, 128), f32),
            pltpu.VMEM((TILES, 512, 128), f32),
            pltpu.VMEM((TILES, 1024, 128), f32),
            pltpu.VMEM((2, 1024, 512), f32),
            pltpu.VMEM((3, 1024, 1536), bf16),
            pltpu.VMEM((3, 768, 256), bf16),
            pltpu.VMEM((3, 1536, 256), bf16),
            pltpu.VMEM((2, 1024, 1024), f32),
            pltpu.VMEM((2, 128, 8, 256), f32),
            pltpu.VMEM((2, 2, 1024, 256), f32),
            dma((TILES, STAGES)),
            dma((TILES, STAGES)),
            dma((6,)),
        ],
        compiler_params=pltpu.CompilerParams(
            vmem_limit_bytes=VMEM_LIMIT, collective_id=1, has_side_effects=True
        ),
        name="sum_and_update",
    )(slots, partial.reshape(TILES, 1024, 128), scaled, tri_factors, vectors)


def per_device(vectors, panel_store, block_ids, offsets, tri_factors):
    partial, scaled, slots = products(vectors, panel_store, block_ids, offsets, tri_factors)
    return sum_and_update(slots, partial, scaled, tri_factors, vectors)


def solution(mesh):
    placed = (
        P(None, ("row", "col"), None),
        P(None, None, ("row", "col"), None),
        P(None, ("row", "col")),
        P(),
        P(),
    )
    return jax.shard_map(
        per_device,
        mesh=mesh,
        in_specs=placed,
        out_specs=P(None, ("row", "col"), None),
        check_vma=False,
    )
```

```python
import jax
import jax.numpy as jnp
from jax import lax
from jax.experimental import pallas as pl
from jax.experimental.pallas import tpu as pltpu
from jax.sharding import PartitionSpec as P


MESH = pl.DeviceIdType.MESH


def strip_of(x, y, z, core):
    return ((x * 2 + z % 2) * 4 + y) * 4 + (z // 2) * 2 + core


VMEM_LIMIT = 60 * 1024 * 1024


def split(value):
    high = value.astype(jnp.bfloat16)
    return high, (value - high.astype(jnp.float32)).astype(jnp.bfloat16)


def dot(first_op, second_op):
    return jnp.dot(first_op, second_op, preferred_element_type=jnp.float32)


def left_pieces(value):
    high, low = split(value)
    return jnp.concatenate([high, high, low], axis=1)


def right_pieces(value):
    high, low = split(value)
    return jnp.concatenate([high, low, high], axis=0)


def left_forms(real_part, imag_part):
    return left_pieces(real_part + imag_part), left_pieces(real_part), left_pieces(imag_part)


def right_forms(real_part, imag_part):
    return right_pieces(real_part), right_pieces(imag_part - real_part), right_pieces(real_part + imag_part)


def complex_dot(left, right):
    shared = dot(left[0], right[0])
    return shared - dot(left[2], right[2]), shared + dot(left[1], right[1])


def adjoint_upper(tri_ref, panel):
    shape = tri_ref.shape[2:]
    upper = lax.broadcasted_iota(jnp.int32, shape, 0) <= lax.broadcasted_iota(jnp.int32, shape, 1)
    return jnp.where(upper, tri_ref[panel, 0], 0.0).T, -jnp.where(upper, tri_ref[panel, 1], 0.0).T


GROUPS = (
    ((0, 64), (64, 64)),
    ((0, 64), (64, 32), (96, 16), (112, 16)),
)


TILES = 9
LINKS = ((), (0,), (1, 2), (3, 4, 5))
HALF_STAGES = len(LINKS)
STAGES = 2 * HALF_STAGES
SIZES = [1024, 512, 256, 64, 8]
COUNTS = [SIZES[stage] - SIZES[stage + 1] for stage in range(HALF_STAGES)]
BASES = [sum(COUNTS[:stage]) for stage in range(HALF_STAGES)]


def level_of(stage):
    return stage if stage < HALF_STAGES else STAGES - 1 - stage


def step_order():
    free = [0.0] * 7
    now = 0.0
    ready = []
    order = []
    work = []
    finished = set()
    queued = set()

    def send(tile, stage):
        nonlocal now
        level = level_of(stage)
        now += 0.06 * (2 ** len(LINKS[level]) - 1 if level else 1)
        if level == 0:
            free[6] = max(free[6], now) + 512 * 0.512 / 600
            arrival = free[6]
        else:
            arrival = now
            for link in LINKS[level]:
                link = (tile + link) % 6
                free[link] = max(free[link], now) + SIZES[level] / 2 * 0.512 / 50
                arrival = max(arrival, free[link])
        ready.append((arrival + 2.5, tile, stage))

    for tile in range(0, TILES - 1, 2):
        ready.append((0.0, tile, 0))
    for tile in [TILES - 1] + list(range(1, TILES - 1, 2)):
        now += 0.5
        send(tile, 0)
    while ready or work:
        ready.sort()
        if ready and (ready[0][0] <= now or not work):
            arrival, tile, stage = ready.pop(0)
            order.append((tile, stage))
            now = max(now, arrival) + (0.05 + COUNTS[stage] * 0.0006 if stage < HALF_STAGES else 0.03)
            if stage < STAGES - 1:
                send(tile, stage + 1)
            else:
                finished.add(tile)
            if TILES - 1 in finished:
                if None not in queued:
                    queued.add(None)
                    work += [(None, piece) for piece in range(4)]
                for chunk in range(4):
                    if chunk not in queued and {2 * chunk, 2 * chunk + 1} <= finished:
                        queued.add(chunk)
                        work += [(-1 - chunk, piece) for piece in range(4)]
        else:
            order.append(work.pop(0))
            now += 0.8
    return order


def main_kernel(
    offsets_ref,
    ids_ref,
    store_ref,
    tri_ref,
    vectors_ref,
    out_ref,
    z_ref,
    first_blocks_ref,
    second_blocks_ref,
    all_ids_ref,
    order_ref,
    slot_ref,
    first_panel_ref,
    second_panel_ref,
    rows_ref,
    match_ref,
    adjoint_ref,
    factor_ref,
    part_ref,
    x_ref,
    total_ref,
    held_ref,
    landed_ref,
    left_ref,
    cross_ref,
    right_ref,
    block_send_sem,
    block_recv_sem,
    id_sem,
    send_sem,
    recv_sem,
    local_sem,
):
    blocks_refs = (first_blocks_ref, second_blocks_ref)
    panel_refs = (first_panel_ref, second_panel_ref)
    row = lax.axis_index("row")
    col = lax.axis_index("col")
    me = row * 4 + col
    x = row // 8
    y = row % 4
    z = (col // 2) * 2 + (row // 4) % 2
    here = (x, y, z)
    core = col % 2

    barrier = pltpu.get_barrier_semaphore()

    def greet(step, carry):
        peer = (me + step) % 128
        pl.semaphore_signal(barrier, inc=1, device_id=(peer // 4, peer % 4), device_id_type=MESH)
        return carry

    lax.fori_loop(1, 128, greet, 0)

    def listed(strip):
        return pl.ds(pl.multiple_of(strip * 8, 8), 8)

    own_copies = [
        pltpu.make_async_copy(store_ref.at[panel, :, listed(me), :], blocks_refs[panel].at[0], local_sem.at[panel])
        for panel in range(2)
    ]
    own_copies.append(pltpu.make_async_copy(ids_ref, all_ids_ref.at[0], local_sem.at[2]))
    for copy in own_copies:
        copy.start()
    fetch_vectors = pltpu.make_async_copy(vectors_ref, z_ref, local_sem.at[3])
    fetch_vectors.start()

    for panel in range(2):
        forms = right_forms(*adjoint_upper(tri_ref, panel))
        for form in range(3):
            factor_ref[panel, form] = forms[form]

    pl.semaphore_wait(barrier, 127)

    def remote(source, target, sent, received, device):
        return pltpu.make_async_remote_copy(
            source,
            target,
            sent,
            received,
            device_id=device,
            device_id_type=MESH,
        )

    def strip_at(step):
        spread = (step // 2 * 27) % 64
        return strip_of(
            (x + spread % 4) % 4, (y + (spread // 4) % 4) % 4, (z + spread // 16) % 4, (core + step) % 2
        )

    def send_blocks(panel, group, first, last):
        def body(step, carry):
            strip = strip_at(step)
            remote(
                store_ref.at[panel, :, listed(strip), :],
                blocks_refs[panel].at[step],
                block_send_sem.at[panel],
                block_recv_sem.at[panel, group],
                (strip // 4, strip % 4),
            ).start()
            return carry

        lax.fori_loop(first, last, body, 0)

    def send_ids(step, carry):
        strip = strip_at(step)
        remote(ids_ref, all_ids_ref.at[step], id_sem.at[0], id_sem.at[1], (strip // 4, strip % 4)).start()
        return carry

    def await_bytes(some, sem):
        pltpu.make_async_copy(some, some, sem).wait()

    send_blocks(0, 0, 1, 24)
    lax.fori_loop(1, 128, send_ids, 0)
    send_blocks(0, 0, 24, 64)
    for panel in range(2):
        for group, (first, count) in enumerate(GROUPS[panel]):
            if panel + group > 0:
                send_blocks(panel, group, max(first, 1), first + count)

    for copy in own_copies:
        copy.wait()
    await_bytes(all_ids_ref.at[pl.ds(1, 127)], id_sem.at[1])
    down = lax.broadcasted_iota(jnp.int32, (128, 128), 0)
    lane = lax.broadcasted_iota(jnp.int32, (128, 128), 1)
    order_ref[...] = jnp.zeros_like(order_ref)
    places = []
    for panel in range(2):
        own = jnp.sum(jnp.where(lane == me, all_ids_ref[:, panel, :], 0), axis=1, keepdims=True) % 128
        places.append(jnp.sum(jnp.where(down == lane, own, 0), axis=0, keepdims=True))
        order_ref[panel : panel + 1, :] = places[panel]
        order_ref[panel + 3 : panel + 4, :] = jnp.max(jnp.where(own == lane, down, 0), axis=0, keepdims=True)
    slot_of_place = jnp.max(jnp.where(places[0] == down, lane, 0), axis=1, keepdims=True)
    order_ref[2:3, :] = jnp.max(jnp.where(places[1] == down, slot_of_place, 0), axis=0, keepdims=True)
    fetch_order = pltpu.make_async_copy(order_ref, slot_ref, local_sem.at[4])
    fetch_order.start()
    fetch_order.wait()
    fetch_vectors.wait()

    def take_group(panel, group, begin_tile):
        first, count = GROUPS[panel][group]
        size = count * 8
        start = first * 8
        begin = first == 0
        values = panel_refs[panel]

        await_bytes(
            blocks_refs[panel].at[pl.ds(max(first, 1), first + count - max(first, 1))], block_recv_sem.at[panel, group]
        )

        def take_block(step, carry):
            slot = first + step
            place = slot_ref[panel, slot]
            near = pl.ds(pl.multiple_of(step * 8, 8), 8)
            row_index = me * 1024 + place * 8 + lax.broadcasted_iota(jnp.int32, (8, 256), 0)
            limit = offsets_ref[panel] + lax.broadcasted_iota(jnp.int32, (8, 256), 1)
            below = row_index > limit
            diagonal = jnp.where(row_index == limit, 1.0, 0.0)
            values[0, slot] = jnp.where(below, blocks_refs[panel][slot, 0], diagonal)
            values[1, slot] = jnp.where(below, blocks_refs[panel][slot, 1], 0.0)
            for part in range(2):
                wanted = z_ref[part, place]
                for chunk in range(4):
                    at = pl.ds(pl.multiple_of(chunk % 2 * 512 + step * 8, 8), 8)
                    rows_ref[chunk // 2, part, at, :] = wanted[:, chunk * 256 : (chunk + 1) * 256]
            if panel == 1:
                matching = slot_ref[2, slot]
                match_ref[0, near, :] = first_panel_ref[0, matching]
                match_ref[1, near, :] = first_panel_ref[1, matching]
            return carry

        lax.fori_loop(0, count, take_block, 0, unroll=4)

        own = [values[part, first : first + count].reshape(size, 256) for part in range(2)]
        forms = left_forms(own[0].T, -own[1].T)
        for form in range(3):
            adjoint_ref[form, :, 0 : 3 * size] = forms[form]

        def adjoint_products(right):
            return complex_dot([adjoint_ref[form, :, 0 : 3 * size] for form in range(3)], right)

        def add_tile(tile, parts):
            for part in range(2):
                for side in range(2):
                    value = parts[part][:, side * 128 : (side + 1) * 128]
                    start = side * 512 + part * 256
                    target = part_ref.at[tile, start : start + 256, :]
                    if begin:
                        target[...] = value
                    else:
                        target[...] += value

        if panel == 1:
            matched = (match_ref[0, 0:size, :], match_ref[1, 0:size, :])
            add_tile(TILES - 1, adjoint_products(right_forms(*matched)))
            if begin_tile is not None:
                begin_tile(TILES - 1)

        def take_columns(chunk, carry):
            at = pl.ds(pl.multiple_of(chunk % 2 * 512, 512), size)
            right = right_forms(rows_ref[chunk // 2, 0, at, :], rows_ref[chunk // 2, 1, at, :])
            add_tile(2 * chunk + panel, adjoint_products(right))
            return carry

        if begin_tile is None:
            lax.fori_loop(0, 4, take_columns, 0)
        else:
            for chunk in range(4):
                take_columns(chunk, 0)
                begin_tile(2 * chunk + panel)

        if panel == 1:
            for which, source in enumerate((matched, own)):
                scaled = complex_dot(left_forms(*source), [factor_ref[which, form] for form in range(3)])
                for part in range(2):
                    x_ref[part, start : start + size, which * 256 : (which + 1) * 256] = scaled[part]

    def device(place, core):
        strip = strip_of(*place, core)
        return (strip // 4, strip % 4)

    sibling = device(here, 1 - core)
    other = [place + 1 - 2 * (place % 2) for place in here] + [3 - place for place in here]
    bits = [((place + 1) // 2) % 2 for place in here] + [place // 2 for place in here]

    def across(links):
        place = list(here)
        for link in links:
            place[link % 3] = other[link]
        return device(place, core)

    def rows_at(first, count):
        return pl.ds(pl.multiple_of(first, 8), count)

    def send(tile, stage, source, target, peer):
        remote(source, target, send_sem.at[tile, stage], recv_sem.at[tile, stage], peer).start()

    def wait(tile, stage, sem):
        some = landed_ref.at[tile, pl.ds(0, COUNTS[level_of(stage)]), :]
        pltpu.make_async_copy(some, some, sem.at[tile, stage]).wait()

    def links_of(tile, level):
        return [(tile + link) % 6 for link in LINKS[level]]

    def share(tile, level, flips=0):
        index = 0
        for place, link in enumerate(links_of(tile, level)):
            index = index * 2 + (1 - bits[link] if flips >> place & 1 else bits[link])
        return index

    def flipped(tile, level, flips):
        return across([link for place, link in enumerate(links_of(tile, level)) if flips >> place & 1])

    lows = [0] * TILES

    def split_rows(tile, level):
        held = held_ref.at[tile]
        size = SIZES[level + 1]
        for flips in range(1, 2 ** len(LINKS[level])):
            send(
                tile,
                level,
                held.at[rows_at(lows[tile] + share(tile, level, flips) * size, size), :],
                landed_ref.at[tile, pl.ds(BASES[level] + (flips - 1) * size, size), :],
                flipped(tile, level, flips),
            )
        lows[tile] = lows[tile] + share(tile, level) * size

    def return_rows(tile, level):
        size = SIZES[level + 1]
        place = total_ref.at[tile, rows_at(core * 512 + lows[tile], size), :]
        for flips in range(1, 2 ** len(LINKS[level])):
            send(tile, STAGES - 1 - level, place, place, flipped(tile, level, flips))

    def advance(tile, stage):
        level = level_of(stage)
        held = held_ref.at[tile]
        wait(tile, stage, recv_sem)
        if stage == 0:
            held[...] = part_ref[tile, rows_at(core * 512, 512), :] + landed_ref[tile, 0:512, :]
            split_rows(tile, 1)
        elif stage < HALF_STAGES:
            size = SIZES[level + 1]
            value = held[rows_at(lows[tile], size), :]
            for piece in range(2 ** len(LINKS[level]) - 1):
                start = BASES[level] + piece * size
                value += landed_ref[tile, start : start + size, :]
            if stage < HALF_STAGES - 1:
                held[rows_at(lows[tile], size), :] = value
                split_rows(tile, level + 1)
            else:
                total_ref[tile, rows_at(core * 512 + lows[tile], size), :] = value
                return_rows(tile, level)
        elif stage < STAGES - 1:
            lows[tile] = lows[tile] - share(tile, level) * SIZES[level + 1]
            if level > 1:
                return_rows(tile, level - 1)
            else:
                place = total_ref.at[tile, rows_at(core * 512, 512), :]
                send(tile, STAGES - 1, place, place, sibling)

    def parts(tile):
        values = total_ref[tile]
        real_part = jnp.concatenate([values[0:256], values[512:768]], axis=1)
        imag_part = jnp.concatenate([values[256:512], values[768:1024]], axis=1)
        return real_part, imag_part

    def correct(piece):
        if piece == 0:
            cross = complex_dot(left_forms(*parts(TILES - 1)), right_forms(*adjoint_upper(tri_ref, 0)))
            cross = right_forms(*cross)
            for form in range(3):
                cross_ref[form] = cross[form]
        rows = slice(piece * 256, (piece + 1) * 256)
        second = left_forms(x_ref[0, rows, 256:512], x_ref[1, rows, 256:512])
        real_part, imag_part = complex_dot(second, [cross_ref[form] for form in range(3)])
        first = left_forms(x_ref[0, rows, 0:256] - real_part, x_ref[1, rows, 0:256] - imag_part)
        for form in range(3):
            for part in range(2):
                source = slice((part + 1) * 256, (part + 2) * 256)
                start = part * 512
                left_ref[form, rows, start : start + 256] = first[form][:, source]
                left_ref[form, rows, start + 256 : start + 512] = second[form][:, source]

    written = []

    def apply(chunk, piece):
        if piece == 0:
            first = parts(2 * chunk)
            second = parts(2 * chunk + 1)
            forms = right_forms(*[jnp.concatenate([first[part], second[part]], axis=0) for part in range(2)])
            for form in range(3):
                right_ref[form, 0:512, :] = forms[form][512:1024]
                right_ref[form, 512:1024, :] = forms[form][0:512]
                right_ref[form, 1024:1536, :] = forms[form][0:512]
        rows = slice(piece * 256, (piece + 1) * 256)
        sums = [
            dot(left_ref[form, rows, 0:512], right_ref[form, 0:512, :])
            + dot(left_ref[form, rows, :], right_ref[form, 512:1536, :])
            for form in range(3)
        ]
        change = (sums[0] - sums[2], sums[0] + sums[1])
        for part in range(2):
            first_blocks_ref[piece * 32 : (piece + 1) * 32, part] = change[part].reshape(32, 8, 256)
        if piece < 3:
            return
        if len(written) > 1:
            written[-2].wait()
        columns = slice(chunk * 256, (chunk + 1) * 256)
        result = rows_ref.at[len(written) % 2]

        def put_block(block, carry):
            slot = slot_ref[4, block]
            rows = pl.ds(pl.multiple_of(block * 8, 8), 8)
            for part in range(2):
                result[part, rows, :] = z_ref[part, block, :, columns] - first_blocks_ref[slot, part]
            return carry

        lax.fori_loop(0, 128, put_block, 0, unroll=8)
        copy = pltpu.make_async_copy(result, out_ref.at[:, :, columns], local_sem.at[5 + len(written)])
        copy.start()
        written.append(copy)

    def begin(tile):
        send(
            tile,
            0,
            part_ref.at[tile, rows_at((1 - core) * 512, 512), :],
            landed_ref.at[tile, pl.ds(0, 512), :],
            sibling,
        )

    for panel in range(2):
        for group in range(len(GROUPS[panel])):
            take_group(panel, group, begin if group == len(GROUPS[panel]) - 1 else None)
    for tile, step in step_order():
        if tile is None:
            correct(step)
        elif tile < 0:
            apply(-1 - tile, step)
        else:
            advance(tile, step)
    await_bytes(all_ids_ref.at[pl.ds(0, 127)], id_sem.at[0])
    for panel in range(2):
        await_bytes(blocks_refs[panel].at[pl.ds(0, 127)], block_send_sem.at[panel])
    for tile in range(TILES):
        for stage in range(STAGES):
            wait(tile, stage, send_sem)
    for copy in written[-2:]:
        copy.wait()


def per_device(vectors, panel_store, block_ids, offsets, tri_factors):
    f32 = jnp.float32
    bf16 = jnp.bfloat16
    whole = pl.BlockSpec(memory_space=pltpu.VMEM)
    anywhere = pl.BlockSpec(memory_space=pl.ANY)
    dma = pltpu.SemaphoreType.DMA
    return pl.pallas_call(
        main_kernel,
        out_shape=jax.ShapeDtypeStruct(vectors.shape, f32),
        in_specs=[pl.BlockSpec(memory_space=pltpu.SMEM), whole, anywhere, whole, anywhere],
        out_specs=anywhere,
        scratch_shapes=[
            pltpu.VMEM((2, 128, 8, 1024), f32),
            pltpu.VMEM((128, 2, 8, 256), f32),
            pltpu.VMEM((128, 2, 8, 256), f32),
            pltpu.VMEM((128, 2, 128), jnp.int32),
            pltpu.VMEM((8, 128), jnp.int32),
            pltpu.SMEM((8, 128), jnp.int32),
            pltpu.VMEM((2, 128, 8, 256), f32),
            pltpu.VMEM((2, 128, 8, 256), f32),
            pltpu.VMEM((2, 2, 1024, 256), f32),
            pltpu.VMEM((2, 512, 256), f32),
            pltpu.VMEM((3, 256, 1536), bf16),
            pltpu.VMEM((2, 3, 768, 256), bf16),
            pltpu.VMEM((TILES, 1024, 128), f32),
            pltpu.VMEM((2, 1024, 512), f32),
            pltpu.VMEM((TILES, 1024, 128), f32),
            pltpu.VMEM((TILES, 512, 128), f32),
            pltpu.VMEM((TILES, 1024, 128), f32),
            pltpu.VMEM((3, 1024, 1024), bf16),
            pltpu.VMEM((3, 768, 256), bf16),
            pltpu.VMEM((3, 1536, 256), bf16),
            dma((2,)),
            dma((2, 4)),
            dma((2,)),
            dma((TILES, STAGES)),
            dma((TILES, STAGES)),
            dma((9,)),
        ],
        compiler_params=pltpu.CompilerParams(
            vmem_limit_bytes=VMEM_LIMIT, collective_id=0, has_side_effects=True
        ),
        name="main",
    )(offsets, block_ids, panel_store, tri_factors, vectors.reshape(2, 128, 8, 1024))


def solution(mesh):
    placed = (
        P(None, ("row", "col"), None),
        P(None, None, ("row", "col"), None),
        P(None, ("row", "col")),
        P(),
        P(),
    )
    return jax.shard_map(
        per_device,
        mesh=mesh,
        in_specs=placed,
        out_specs=P(None, ("row", "col"), None),
        check_vma=False,
    )
```

```python
import jax
import jax.numpy as jnp
from jax import lax
from jax.experimental import pallas as pl
from jax.experimental.pallas import tpu as pltpu
from jax.sharding import PartitionSpec as P


MESH = pl.DeviceIdType.MESH


def strip_of(x, y, z, core):
    return ((x * 2 + z % 2) * 4 + y) * 4 + (z // 2) * 2 + core


VMEM_LIMIT = 60 * 1024 * 1024


def split(value):
    high = value.astype(jnp.bfloat16)
    return high, (value - high.astype(jnp.float32)).astype(jnp.bfloat16)


def dot(first_op, second_op):
    return jnp.dot(first_op, second_op, preferred_element_type=jnp.float32)


def left_pieces(value):
    high, low = split(value)
    return jnp.concatenate([high, high, low], axis=1)


def right_pieces(value):
    high, low = split(value)
    return jnp.concatenate([high, low, high], axis=0)


def left_forms(real_part, imag_part):
    return left_pieces(real_part + imag_part), left_pieces(real_part), left_pieces(imag_part)


def right_forms(real_part, imag_part):
    return right_pieces(real_part), right_pieces(imag_part - real_part), right_pieces(real_part + imag_part)


def complex_dot(left, right):
    shared = dot(left[0], right[0])
    return shared - dot(left[2], right[2]), shared + dot(left[1], right[1])


def adjoint_upper(tri_ref, panel):
    shape = tri_ref.shape[2:]
    upper = lax.broadcasted_iota(jnp.int32, shape, 0) <= lax.broadcasted_iota(jnp.int32, shape, 1)
    return jnp.where(upper, tri_ref[panel, 0], 0.0).T, -jnp.where(upper, tri_ref[panel, 1], 0.0).T


GROUPS = (
    ((0, 64), (64, 64)),
    ((0, 64), (64, 32), (96, 16), (112, 16)),
)


TILES = 9
LINKS = ((), (0,), (1, 2), (3, 4, 5))
HALF_STAGES = len(LINKS)
STAGES = 2 * HALF_STAGES
SIZES = [1024, 512, 256, 64, 8]
COUNTS = [SIZES[stage] - SIZES[stage + 1] for stage in range(HALF_STAGES)]
BASES = [sum(COUNTS[:stage]) for stage in range(HALF_STAGES)]


def level_of(stage):
    return stage if stage < HALF_STAGES else STAGES - 1 - stage


def step_order():
    free = [0.0] * 7
    now = 0.0
    ready = []
    order = []
    work = []
    finished = set()
    queued = set()

    def send(tile, stage):
        nonlocal now
        level = level_of(stage)
        now += 0.06 * (2 ** len(LINKS[level]) - 1 if level else 1)
        if level == 0:
            free[6] = max(free[6], now) + 512 * 0.512 / 600
            arrival = free[6]
        else:
            arrival = now
            for link in LINKS[level]:
                link = (tile + link) % 6
                free[link] = max(free[link], now) + SIZES[level] / 2 * 0.512 / 50
                arrival = max(arrival, free[link])
        ready.append((arrival + 2.5, tile, stage))

    for tile in range(0, TILES - 1, 2):
        ready.append((0.0, tile, 1))
    for tile in [TILES - 1] + list(range(1, TILES - 1, 2)):
        now += 0.5
        send(tile, 0)
    while ready or work:
        ready.sort()
        if ready and (ready[0][0] <= now or not work):
            arrival, tile, stage = ready.pop(0)
            order.append((tile, stage))
            now = max(now, arrival) + (0.05 + COUNTS[stage] * 0.0006 if stage < HALF_STAGES else 0.03)
            if stage < STAGES - 1:
                send(tile, stage + 1)
            else:
                finished.add(tile)
            if TILES - 1 in finished:
                if None not in queued:
                    queued.add(None)
                    work += [(None, piece) for piece in range(4)]
                for chunk in range(4):
                    if chunk not in queued and {2 * chunk, 2 * chunk + 1} <= finished:
                        queued.add(chunk)
                        work += [(-1 - chunk, piece) for piece in range(4)]
        else:
            order.append(work.pop(0))
            now += 0.8
    return order


def main_kernel(
    offsets_ref,
    ids_ref,
    store_ref,
    tri_ref,
    vectors_ref,
    out_ref,
    z_ref,
    first_blocks_ref,
    second_blocks_ref,
    all_ids_ref,
    order_ref,
    slot_ref,
    first_panel_ref,
    second_panel_ref,
    rows_ref,
    match_ref,
    adjoint_ref,
    factor_ref,
    part_ref,
    x_ref,
    total_ref,
    held_ref,
    landed_ref,
    left_ref,
    cross_ref,
    right_ref,
    block_send_sem,
    block_recv_sem,
    id_sem,
    send_sem,
    recv_sem,
    local_sem,
):
    blocks_refs = (first_blocks_ref, second_blocks_ref)
    panel_refs = (first_panel_ref, second_panel_ref)
    row = lax.axis_index("row")
    col = lax.axis_index("col")
    me = row * 4 + col
    x = row // 8
    y = row % 4
    z = (col // 2) * 2 + (row // 4) % 2
    here = (x, y, z)
    core = col % 2

    barrier = pltpu.get_barrier_semaphore()

    def greet(step, carry):
        peer = (me + step) % 128
        pl.semaphore_signal(barrier, inc=1, device_id=(peer // 4, peer % 4), device_id_type=MESH)
        return carry

    lax.fori_loop(1, 128, greet, 0)

    def listed(strip):
        return pl.ds(pl.multiple_of(strip * 8, 8), 8)

    own_copies = [
        pltpu.make_async_copy(store_ref.at[panel, :, listed(me), :], blocks_refs[panel].at[0], local_sem.at[panel])
        for panel in range(2)
    ]
    own_copies.append(pltpu.make_async_copy(ids_ref, all_ids_ref.at[0], local_sem.at[2]))
    for copy in own_copies:
        copy.start()
    fetch_vectors = pltpu.make_async_copy(vectors_ref, z_ref, local_sem.at[3])
    fetch_vectors.start()

    for panel in range(2):
        forms = right_forms(*adjoint_upper(tri_ref, panel))
        for form in range(3):
            factor_ref[panel, form] = forms[form]

    pl.semaphore_wait(barrier, 127)

    def remote(source, target, sent, received, device):
        return pltpu.make_async_remote_copy(
            source,
            target,
            sent,
            received,
            device_id=device,
            device_id_type=MESH,
        )

    def strip_at(step):
        spread = (step // 2 * 27) % 64
        return strip_of(
            (x + spread % 4) % 4, (y + (spread // 4) % 4) % 4, (z + spread // 16) % 4, (core + step) % 2
        )

    def send_blocks(panel, group, first, last):
        def body(step, carry):
            strip = strip_at(step)
            remote(
                store_ref.at[panel, :, listed(strip), :],
                blocks_refs[panel].at[step],
                block_send_sem.at[panel],
                block_recv_sem.at[panel, group],
                (strip // 4, strip % 4),
            ).start()
            return carry

        lax.fori_loop(first, last, body, 0)

    def send_ids(step, carry):
        strip = strip_at(step)
        remote(ids_ref, all_ids_ref.at[step], id_sem.at[0], id_sem.at[1], (strip // 4, strip % 4)).start()
        return carry

    def await_bytes(some, sem):
        pltpu.make_async_copy(some, some, sem).wait()

    send_blocks(0, 0, 1, 48)
    lax.fori_loop(1, 128, send_ids, 0)
    send_blocks(0, 0, 48, 64)
    for panel in range(2):
        for group, (first, count) in enumerate(GROUPS[panel]):
            if panel + group > 0:
                send_blocks(panel, group, max(first, 1), first + count)

    for copy in own_copies:
        copy.wait()
    await_bytes(all_ids_ref.at[pl.ds(1, 127)], id_sem.at[1])
    down = lax.broadcasted_iota(jnp.int32, (128, 128), 0)
    lane = lax.broadcasted_iota(jnp.int32, (128, 128), 1)
    order_ref[...] = jnp.zeros_like(order_ref)
    places = []
    for panel in range(2):
        own = jnp.sum(jnp.where(lane == me, all_ids_ref[:, panel, :], 0), axis=1, keepdims=True) % 128
        places.append(jnp.sum(jnp.where(down == lane, own, 0), axis=0, keepdims=True))
        order_ref[panel : panel + 1, :] = places[panel]
        order_ref[panel + 3 : panel + 4, :] = jnp.max(jnp.where(own == lane, down, 0), axis=0, keepdims=True)
    slot_of_place = jnp.max(jnp.where(places[0] == down, lane, 0), axis=1, keepdims=True)
    order_ref[2:3, :] = jnp.max(jnp.where(places[1] == down, slot_of_place, 0), axis=0, keepdims=True)
    fetch_order = pltpu.make_async_copy(order_ref, slot_ref, local_sem.at[4])
    fetch_order.start()
    fetch_order.wait()
    fetch_vectors.wait()

    def take_group(panel, group, begin_tile):
        first, count = GROUPS[panel][group]
        size = count * 8
        start = first * 8
        begin = first == 0
        values = panel_refs[panel]

        await_bytes(
            blocks_refs[panel].at[pl.ds(max(first, 1), first + count - max(first, 1))], block_recv_sem.at[panel, group]
        )

        def take_block(step, carry):
            slot = first + step
            place = slot_ref[panel, slot]
            near = pl.ds(pl.multiple_of(step * 8, 8), 8)
            row_index = me * 1024 + place * 8 + lax.broadcasted_iota(jnp.int32, (8, 256), 0)
            limit = offsets_ref[panel] + lax.broadcasted_iota(jnp.int32, (8, 256), 1)
            below = row_index > limit
            diagonal = jnp.where(row_index == limit, 1.0, 0.0)
            values[0, slot] = jnp.where(below, blocks_refs[panel][slot, 0], diagonal)
            values[1, slot] = jnp.where(below, blocks_refs[panel][slot, 1], 0.0)
            for part in range(2):
                wanted = z_ref[part, place]
                for chunk in range(4):
                    at = pl.ds(pl.multiple_of(chunk % 2 * 512 + step * 8, 8), 8)
                    rows_ref[chunk // 2, part, at, :] = wanted[:, chunk * 256 : (chunk + 1) * 256]
            if panel == 1:
                matching = slot_ref[2, slot]
                match_ref[0, near, :] = first_panel_ref[0, matching]
                match_ref[1, near, :] = first_panel_ref[1, matching]
            return carry

        lax.fori_loop(0, count, take_block, 0, unroll=4)

        own = [values[part, first : first + count].reshape(size, 256) for part in range(2)]
        forms = left_forms(own[0].T, -own[1].T)
        for form in range(3):
            adjoint_ref[form, :, 0 : 3 * size] = forms[form]

        def adjoint_products(right):
            return complex_dot([adjoint_ref[form, :, 0 : 3 * size] for form in range(3)], right)

        def add_tile(tile, parts):
            for part in range(2):
                for side in range(2):
                    value = parts[part][:, side * 128 : (side + 1) * 128]
                    start = side * 512 + part * 256
                    target = part_ref.at[tile, start : start + 256, :]
                    if begin:
                        target[...] = value
                    else:
                        target[...] += value

        if panel == 1:
            matched = (match_ref[0, 0:size, :], match_ref[1, 0:size, :])
            add_tile(TILES - 1, adjoint_products(right_forms(*matched)))
            if begin_tile is not None:
                begin_tile(TILES - 1)

        def take_columns(chunk, carry):
            at = pl.ds(pl.multiple_of(chunk % 2 * 512, 512), size)
            right = right_forms(rows_ref[chunk // 2, 0, at, :], rows_ref[chunk // 2, 1, at, :])
            add_tile(2 * chunk + panel, adjoint_products(right))
            return carry

        if begin_tile is None:
            lax.fori_loop(0, 4, take_columns, 0)
        else:
            for chunk in range(4):
                take_columns(chunk, 0)
                begin_tile(2 * chunk + panel)

        if panel == 1:
            for which, source in enumerate((matched, own)):
                scaled = complex_dot(left_forms(*source), [factor_ref[which, form] for form in range(3)])
                for part in range(2):
                    x_ref[part, start : start + size, which * 256 : (which + 1) * 256] = scaled[part]

    def device(place, core):
        strip = strip_of(*place, core)
        return (strip // 4, strip % 4)

    sibling = device(here, 1 - core)
    other = [place + 1 - 2 * (place % 2) for place in here] + [3 - place for place in here]
    bits = [((place + 1) // 2) % 2 for place in here] + [place // 2 for place in here]

    def across(links):
        place = list(here)
        for link in links:
            place[link % 3] = other[link]
        return device(place, core)

    def rows_at(first, count):
        return pl.ds(pl.multiple_of(first, 8), count)

    def send(tile, stage, source, target, peer):
        remote(source, target, send_sem.at[tile, stage], recv_sem.at[tile, stage], peer).start()

    def wait(tile, stage, sem):
        some = landed_ref.at[tile, pl.ds(0, COUNTS[level_of(stage)]), :]
        pltpu.make_async_copy(some, some, sem.at[tile, stage]).wait()

    def links_of(tile, level):
        return [(tile + link) % 6 for link in LINKS[level]]

    def share(tile, level, flips=0):
        index = 0
        for place, link in enumerate(links_of(tile, level)):
            index = index * 2 + (1 - bits[link] if flips >> place & 1 else bits[link])
        return index

    def flipped(tile, level, flips):
        return across([link for place, link in enumerate(links_of(tile, level)) if flips >> place & 1])

    lows = [0] * TILES

    def split_rows(tile, level):
        held = held_ref.at[tile]
        size = SIZES[level + 1]
        for flips in range(1, 2 ** len(LINKS[level])):
            send(
                tile,
                level,
                held.at[rows_at(lows[tile] + share(tile, level, flips) * size, size), :],
                landed_ref.at[tile, pl.ds(BASES[level] + (flips - 1) * size, size), :],
                flipped(tile, level, flips),
            )
        lows[tile] = lows[tile] + share(tile, level) * size

    def return_rows(tile, level):
        size = SIZES[level + 1]
        place = total_ref.at[tile, rows_at(core * 512 + lows[tile], size), :]
        for flips in range(1, 2 ** len(LINKS[level])):
            send(tile, STAGES - 1 - level, place, place, flipped(tile, level, flips))

    def advance(tile, stage):
        level = level_of(stage)
        held = held_ref.at[tile]
        wait(tile, stage, recv_sem)
        if stage == 0:
            held[...] = part_ref[tile, rows_at(core * 512, 512), :] + landed_ref[tile, 0:512, :]
            split_rows(tile, 1)
        elif stage < HALF_STAGES:
            size = SIZES[level + 1]
            value = held[rows_at(lows[tile], size), :]
            for piece in range(2 ** len(LINKS[level]) - 1):
                start = BASES[level] + piece * size
                value += landed_ref[tile, start : start + size, :]
            if stage < HALF_STAGES - 1:
                held[rows_at(lows[tile], size), :] = value
                split_rows(tile, level + 1)
            else:
                total_ref[tile, rows_at(core * 512 + lows[tile], size), :] = value
                return_rows(tile, level)
        elif stage < STAGES - 1:
            lows[tile] = lows[tile] - share(tile, level) * SIZES[level + 1]
            if level > 1:
                return_rows(tile, level - 1)
            else:
                place = total_ref.at[tile, rows_at(core * 512, 512), :]
                send(tile, STAGES - 1, place, place, sibling)

    def parts(tile):
        values = total_ref[tile]
        real_part = jnp.concatenate([values[0:256], values[512:768]], axis=1)
        imag_part = jnp.concatenate([values[256:512], values[768:1024]], axis=1)
        return real_part, imag_part

    def correct(piece):
        if piece == 0:
            cross = complex_dot(left_forms(*parts(TILES - 1)), right_forms(*adjoint_upper(tri_ref, 0)))
            cross = right_forms(*cross)
            for form in range(3):
                cross_ref[form] = cross[form]
        rows = slice(piece * 256, (piece + 1) * 256)
        second = left_forms(x_ref[0, rows, 256:512], x_ref[1, rows, 256:512])
        real_part, imag_part = complex_dot(second, [cross_ref[form] for form in range(3)])
        first = left_forms(x_ref[0, rows, 0:256] - real_part, x_ref[1, rows, 0:256] - imag_part)
        for form in range(3):
            for part in range(2):
                source = slice((part + 1) * 256, (part + 2) * 256)
                start = part * 512
                left_ref[form, rows, start : start + 256] = first[form][:, source]
                left_ref[form, rows, start + 256 : start + 512] = second[form][:, source]

    written = []

    def apply(chunk, piece):
        if piece == 0:
            first = parts(2 * chunk)
            second = parts(2 * chunk + 1)
            forms = right_forms(*[jnp.concatenate([first[part], second[part]], axis=0) for part in range(2)])
            for form in range(3):
                right_ref[form, 0:512, :] = forms[form][512:1024]
                right_ref[form, 512:1024, :] = forms[form][0:512]
                right_ref[form, 1024:1536, :] = forms[form][0:512]
        rows = slice(piece * 256, (piece + 1) * 256)
        sums = [
            dot(left_ref[form, rows, 0:512], right_ref[form, 0:512, :])
            + dot(left_ref[form, rows, :], right_ref[form, 512:1536, :])
            for form in range(3)
        ]
        change = (sums[0] - sums[2], sums[0] + sums[1])
        for part in range(2):
            first_blocks_ref[piece * 32 : (piece + 1) * 32, part] = change[part].reshape(32, 8, 256)
        if piece < 3:
            return
        if len(written) > 1:
            written[-2].wait()
        columns = slice(chunk * 256, (chunk + 1) * 256)
        result = rows_ref.at[len(written) % 2]

        def put_block(block, carry):
            slot = slot_ref[4, block]
            rows = pl.ds(pl.multiple_of(block * 8, 8), 8)
            for part in range(2):
                result[part, rows, :] = z_ref[part, block, :, columns] - first_blocks_ref[slot, part]
            return carry

        lax.fori_loop(0, 128, put_block, 0, unroll=8)
        copy = pltpu.make_async_copy(result, out_ref.at[:, :, columns], local_sem.at[5 + len(written)])
        copy.start()
        written.append(copy)

    def begin(tile):
        send(
            tile,
            0,
            part_ref.at[tile, rows_at((1 - core) * 512, 512), :],
            landed_ref.at[tile, pl.ds(0, 512), :],
            sibling,
        )

    for panel in range(2):
        for group in range(len(GROUPS[panel])):
            if panel == 1 and group == 2:
                for tile in range(0, TILES - 1, 2):
                    advance(tile, 0)
            take_group(panel, group, begin if group == len(GROUPS[panel]) - 1 else None)
    for tile, step in step_order():
        if tile is None:
            correct(step)
        elif tile < 0:
            apply(-1 - tile, step)
        else:
            advance(tile, step)
    await_bytes(all_ids_ref.at[pl.ds(0, 127)], id_sem.at[0])
    for panel in range(2):
        await_bytes(blocks_refs[panel].at[pl.ds(0, 127)], block_send_sem.at[panel])
    for tile in range(TILES):
        for stage in range(STAGES):
            wait(tile, stage, send_sem)
    for copy in written[-2:]:
        copy.wait()


def move_kernel(source_ref, target_ref, sem):
    copies = []
    for piece in range(16):
        rows = pl.ds(piece % 8 * 128, 128)
        copies.append(
            pltpu.make_async_copy(
                source_ref.at[piece // 8, rows, :], target_ref.at[piece // 8, rows, :], sem.at[piece]
            )
        )
    for copy in copies:
        copy.start()
    for copy in copies:
        copy.wait()


def per_device(vectors, panel_store, block_ids, offsets, tri_factors):
    f32 = jnp.float32
    bf16 = jnp.bfloat16
    whole = pl.BlockSpec(memory_space=pltpu.VMEM)
    anywhere = pl.BlockSpec(memory_space=pl.ANY)
    dma = pltpu.SemaphoreType.DMA
    result = pl.pallas_call(
        main_kernel,
        out_shape=jax.ShapeDtypeStruct(vectors.shape, f32),
        in_specs=[pl.BlockSpec(memory_space=pltpu.SMEM), whole, anywhere, whole, anywhere],
        out_specs=anywhere,
        scratch_shapes=[
            pltpu.VMEM((2, 128, 8, 1024), f32),
            pltpu.VMEM((128, 2, 8, 256), f32),
            pltpu.VMEM((128, 2, 8, 256), f32),
            pltpu.VMEM((128, 2, 128), jnp.int32),
            pltpu.VMEM((8, 128), jnp.int32),
            pltpu.SMEM((8, 128), jnp.int32),
            pltpu.VMEM((2, 128, 8, 256), f32),
            pltpu.VMEM((2, 128, 8, 256), f32),
            pltpu.VMEM((2, 2, 1024, 256), f32),
            pltpu.VMEM((2, 512, 256), f32),
            pltpu.VMEM((3, 256, 1536), bf16),
            pltpu.VMEM((2, 3, 768, 256), bf16),
            pltpu.VMEM((TILES, 1024, 128), f32),
            pltpu.VMEM((2, 1024, 512), f32),
            pltpu.VMEM((TILES, 1024, 128), f32),
            pltpu.VMEM((TILES, 512, 128), f32),
            pltpu.VMEM((TILES, 1024, 128), f32),
            pltpu.VMEM((3, 1024, 1024), bf16),
            pltpu.VMEM((3, 768, 256), bf16),
            pltpu.VMEM((3, 1536, 256), bf16),
            dma((2,)),
            dma((2, 4)),
            dma((2,)),
            dma((TILES, STAGES)),
            dma((TILES, STAGES)),
            dma((9,)),
        ],
        compiler_params=pltpu.CompilerParams(
            vmem_limit_bytes=VMEM_LIMIT, collective_id=0, has_side_effects=True
        ),
        name="main",
    )(offsets, block_ids, panel_store, tri_factors, vectors.reshape(2, 128, 8, 1024))
    return pl.pallas_call(
        move_kernel,
        out_shape=jax.ShapeDtypeStruct(vectors.shape, f32),
        in_specs=[anywhere],
        out_specs=anywhere,
        scratch_shapes=[dma((16,))],
        name="move",
    )(result)


def solution(mesh):
    placed = (
        P(None, ("row", "col"), None),
        P(None, None, ("row", "col"), None),
        P(None, ("row", "col")),
        P(),
        P(),
    )
    return jax.shard_map(
        per_device,
        mesh=mesh,
        in_specs=placed,
        out_specs=P(None, ("row", "col"), None),
        check_vma=False,
    )
```

```python
import jax
import jax.numpy as jnp
from jax import lax
from jax.experimental import pallas as pl
from jax.experimental.pallas import tpu as pltpu
from jax.sharding import PartitionSpec as P


MESH = pl.DeviceIdType.MESH


def strip_of(x, y, z, core):
    return ((x * 2 + z % 2) * 4 + y) * 4 + (z // 2) * 2 + core


VMEM_LIMIT = 60 * 1024 * 1024


def split(value):
    high = value.astype(jnp.bfloat16)
    return high, (value - high.astype(jnp.float32)).astype(jnp.bfloat16)


def dot(first_op, second_op):
    return jnp.dot(first_op, second_op, preferred_element_type=jnp.float32)


def left_pieces(value):
    high, low = split(value)
    return jnp.concatenate([high, high, low], axis=1)


def right_pieces(value):
    high, low = split(value)
    return jnp.concatenate([high, low, high], axis=0)


def left_forms(real_part, imag_part):
    return left_pieces(real_part + imag_part), left_pieces(real_part), left_pieces(imag_part)


def right_forms(real_part, imag_part):
    return right_pieces(real_part), right_pieces(imag_part - real_part), right_pieces(real_part + imag_part)


def complex_dot(left, right):
    shared = dot(left[0], right[0])
    return shared - dot(left[2], right[2]), shared + dot(left[1], right[1])


def adjoint_upper(tri_ref, panel):
    shape = tri_ref.shape[2:]
    upper = lax.broadcasted_iota(jnp.int32, shape, 0) <= lax.broadcasted_iota(jnp.int32, shape, 1)
    return jnp.where(upper, tri_ref[panel, 0], 0.0).T, -jnp.where(upper, tri_ref[panel, 1], 0.0).T


GROUPS = (
    ((0, 64), (64, 64)),
    ((0, 32), (32, 32), (64, 32), (96, 16), (112, 16)),
)


TILES = 9
LINKS = ((), (0,), (1, 2), (3, 4, 5))
HALF_STAGES = len(LINKS)
STAGES = 2 * HALF_STAGES
SIZES = [1024, 512, 256, 64, 8]
COUNTS = [SIZES[stage] - SIZES[stage + 1] for stage in range(HALF_STAGES)]
BASES = [sum(COUNTS[:stage]) for stage in range(HALF_STAGES)]


def level_of(stage):
    return stage if stage < HALF_STAGES else STAGES - 1 - stage


def step_order():
    free = [0.0] * 7
    now = 0.0
    ready = []
    order = []
    work = []
    finished = set()
    queued = set()

    def send(tile, stage):
        nonlocal now
        level = level_of(stage)
        now += 0.06 * (2 ** len(LINKS[level]) - 1 if level else 1)
        if level == 0:
            free[6] = max(free[6], now) + 512 * 0.512 / 600
            arrival = free[6]
        else:
            arrival = now
            for link in LINKS[level]:
                link = (tile + link) % 6
                free[link] = max(free[link], now) + SIZES[level] / 2 * 0.512 / 50
                arrival = max(arrival, free[link])
        ready.append((arrival + 2.5, tile, stage))

    for tile in range(0, TILES - 1, 2):
        ready.append((0.0, tile, 0))
    for tile in [TILES - 1] + list(range(1, TILES - 1, 2)):
        now += 0.5
        send(tile, 0)
    while ready or work:
        ready.sort()
        if ready and (ready[0][0] <= now or not work):
            arrival, tile, stage = ready.pop(0)
            order.append((tile, stage))
            now = max(now, arrival) + (0.05 + COUNTS[stage] * 0.0006 if stage < HALF_STAGES else 0.03)
            if stage < STAGES - 1:
                send(tile, stage + 1)
            else:
                finished.add(tile)
            if TILES - 1 in finished:
                if None not in queued:
                    queued.add(None)
                    work += [(None, piece) for piece in range(4)]
                for chunk in range(4):
                    if chunk not in queued and {2 * chunk, 2 * chunk + 1} <= finished:
                        queued.add(chunk)
                        work += [(-1 - chunk, piece) for piece in range(4)]
        else:
            order.append(work.pop(0))
            now += 0.8
    return order


def main_kernel(
    offsets_ref,
    ids_ref,
    store_ref,
    tri_ref,
    vectors_ref,
    out_ref,
    listed_ref,
    z_ref,
    first_blocks_ref,
    second_blocks_ref,
    all_ids_ref,
    order_ref,
    slot_ref,
    first_panel_ref,
    second_panel_ref,
    rows_ref,
    match_ref,
    adjoint_ref,
    factor_ref,
    part_ref,
    x_ref,
    total_ref,
    held_ref,
    landed_ref,
    left_ref,
    right_ref,
    block_send_sem,
    block_recv_sem,
    id_sem,
    send_sem,
    recv_sem,
    local_sem,
):
    blocks_refs = (first_blocks_ref, second_blocks_ref)
    panel_refs = (first_panel_ref, second_panel_ref)
    row = lax.axis_index("row")
    col = lax.axis_index("col")
    me = row * 4 + col
    x = row // 8
    y = row % 4
    z = (col // 2) * 2 + (row // 4) % 2
    here = (x, y, z)
    core = col % 2

    barrier = pltpu.get_barrier_semaphore()

    def greet(step, carry):
        peer = (me + step) % 128
        pl.semaphore_signal(barrier, inc=1, device_id=(peer // 4, peer % 4), device_id_type=MESH)
        return carry

    lax.fori_loop(1, 128, greet, 0)

    def listed(strip):
        return pl.ds(pl.multiple_of(strip * 8, 8), 8)

    own_copies = [
        pltpu.make_async_copy(store_ref.at[panel, :, listed(me), :], blocks_refs[panel].at[0], local_sem.at[panel])
        for panel in range(2)
    ]
    own_copies.append(pltpu.make_async_copy(ids_ref, all_ids_ref.at[0], local_sem.at[2]))
    fetch_store = [
        pltpu.make_async_copy(store_ref.at[panel], listed_ref.at[panel], local_sem.at[9 + panel]) for panel in range(2)
    ]
    fetch_store[0].start()
    fetch_store[1].start()
    for copy in own_copies:
        copy.start()
    fetch_vectors = pltpu.make_async_copy(vectors_ref, z_ref, local_sem.at[3])
    fetch_vectors.start()

    for panel in range(2):
        forms = right_forms(*adjoint_upper(tri_ref, panel))
        for form in range(3):
            factor_ref[panel, form] = forms[form]

    pl.semaphore_wait(barrier, 127)

    def remote(source, target, sent, received, device):
        return pltpu.make_async_remote_copy(
            source,
            target,
            sent,
            received,
            device_id=device,
            device_id_type=MESH,
        )

    def strip_at(step):
        spread = (step // 2 * 27) % 64
        return strip_of(
            (x + spread % 4) % 4, (y + (spread // 4) % 4) % 4, (z + spread // 16) % 4, (core + step) % 2
        )

    def send_blocks(panel, group, first, last):
        def body(step, carry):
            strip = strip_at(step)
            remote(
                listed_ref.at[panel, :, listed(strip), :],
                blocks_refs[panel].at[step],
                block_send_sem.at[panel],
                block_recv_sem.at[panel, group],
                (strip // 4, strip % 4),
            ).start()
            return carry

        lax.fori_loop(first, last, body, 0)

    def send_ids(step, carry):
        strip = strip_at(step)
        remote(ids_ref, all_ids_ref.at[step], id_sem.at[0], id_sem.at[1], (strip // 4, strip % 4)).start()
        return carry

    def await_bytes(some, sem):
        pltpu.make_async_copy(some, some, sem).wait()

    fetch_store[0].wait()
    send_blocks(0, 0, 1, 24)
    lax.fori_loop(1, 128, send_ids, 0)
    send_blocks(0, 0, 24, 64)
    fetch_store[1].wait()
    for panel in range(2):
        for group, (first, count) in enumerate(GROUPS[panel]):
            if panel + group > 0:
                send_blocks(panel, group, max(first, 1), first + count)

    for copy in own_copies:
        copy.wait()
    await_bytes(all_ids_ref.at[pl.ds(1, 127)], id_sem.at[1])
    down = lax.broadcasted_iota(jnp.int32, (128, 128), 0)
    lane = lax.broadcasted_iota(jnp.int32, (128, 128), 1)
    order_ref[...] = jnp.zeros_like(order_ref)
    places = []
    for panel in range(2):
        own = jnp.sum(jnp.where(lane == me, all_ids_ref[:, panel, :], 0), axis=1, keepdims=True) % 128
        places.append(jnp.sum(jnp.where(down == lane, own, 0), axis=0, keepdims=True))
        order_ref[panel : panel + 1, :] = places[panel]
        order_ref[panel + 3 : panel + 4, :] = jnp.max(jnp.where(own == lane, down, 0), axis=0, keepdims=True)
    slot_of_place = jnp.max(jnp.where(places[0] == down, lane, 0), axis=1, keepdims=True)
    order_ref[2:3, :] = jnp.max(jnp.where(places[1] == down, slot_of_place, 0), axis=0, keepdims=True)
    fetch_order = pltpu.make_async_copy(order_ref, slot_ref, local_sem.at[4])
    fetch_order.start()
    fetch_order.wait()
    fetch_vectors.wait()

    def take_group(panel, group, begin_tile):
        first, count = GROUPS[panel][group]
        size = count * 8
        start = first * 8
        begin = first == 0
        values = panel_refs[panel]
        kept = first if panel == 0 else 0

        await_bytes(
            blocks_refs[panel].at[pl.ds(max(first, 1), first + count - max(first, 1))], block_recv_sem.at[panel, group]
        )

        def take_block(step, carry):
            slot = first + step
            place = slot_ref[panel, slot]
            near = pl.ds(pl.multiple_of(step * 8, 8), 8)
            row_index = me * 1024 + place * 8 + lax.broadcasted_iota(jnp.int32, (8, 256), 0)
            limit = offsets_ref[panel] + lax.broadcasted_iota(jnp.int32, (8, 256), 1)
            below = row_index > limit
            diagonal = jnp.where(row_index == limit, 1.0, 0.0)
            values[0, kept + step] = jnp.where(below, blocks_refs[panel][slot, 0], diagonal)
            values[1, kept + step] = jnp.where(below, blocks_refs[panel][slot, 1], 0.0)
            for part in range(2):
                wanted = z_ref[part, place]
                for chunk in range(4):
                    at = pl.ds(pl.multiple_of(chunk % 2 * 512 + step * 8, 8), 8)
                    rows_ref[chunk // 2, part, at, :] = wanted[:, chunk * 256 : (chunk + 1) * 256]
            if panel == 1:
                matching = slot_ref[2, slot]
                match_ref[0, near, :] = first_panel_ref[0, matching]
                match_ref[1, near, :] = first_panel_ref[1, matching]
            return carry

        lax.fori_loop(0, count, take_block, 0, unroll=4)

        own = [values[part, kept : kept + count].reshape(size, 256) for part in range(2)]
        forms = left_forms(own[0].T, -own[1].T)
        for form in range(3):
            adjoint_ref[form, :, 0 : 3 * size] = forms[form]

        def adjoint_products(right):
            return complex_dot([adjoint_ref[form, :, 0 : 3 * size] for form in range(3)], right)

        def add_tile(tile, parts):
            for part in range(2):
                for side in range(2):
                    value = parts[part][:, side * 128 : (side + 1) * 128]
                    start = side * 512 + part * 256
                    target = part_ref.at[tile, start : start + 256, :]
                    if begin:
                        target[...] = value
                    else:
                        target[...] += value

        if panel == 1:
            matched = (match_ref[0, 0:size, :], match_ref[1, 0:size, :])
            add_tile(TILES - 1, adjoint_products(right_forms(*matched)))
            if begin_tile is not None:
                begin_tile(TILES - 1)

        def take_columns(chunk, carry):
            at = pl.ds(pl.multiple_of(chunk % 2 * 512, 512), size)
            right = right_forms(rows_ref[chunk // 2, 0, at, :], rows_ref[chunk // 2, 1, at, :])
            add_tile(2 * chunk + panel, adjoint_products(right))
            return carry

        if begin_tile is None:
            lax.fori_loop(0, 4, take_columns, 0)
        else:
            for chunk in range(4):
                take_columns(chunk, 0)
                begin_tile(2 * chunk + panel)

        if panel == 1:
            for which, source in enumerate((matched, own)):
                scaled = complex_dot(left_forms(*source), [factor_ref[which, form] for form in range(3)])
                for part in range(2):
                    x_ref[part, start : start + size, which * 256 : (which + 1) * 256] = scaled[part]

    def device(place, core):
        strip = strip_of(*place, core)
        return (strip // 4, strip % 4)

    sibling = device(here, 1 - core)
    other = [place + 1 - 2 * (place % 2) for place in here] + [3 - place for place in here]
    bits = [((place + 1) // 2) % 2 for place in here] + [place // 2 for place in here]

    def across(links):
        place = list(here)
        for link in links:
            place[link % 3] = other[link]
        return device(place, core)

    def rows_at(first, count):
        return pl.ds(pl.multiple_of(first, 8), count)

    def send(tile, stage, source, target, peer):
        remote(source, target, send_sem.at[tile, stage], recv_sem.at[tile, stage], peer).start()

    def wait(tile, stage, sem):
        some = landed_ref.at[tile, pl.ds(0, COUNTS[level_of(stage)]), :]
        pltpu.make_async_copy(some, some, sem.at[tile, stage]).wait()

    def links_of(tile, level):
        return [(tile + link) % 6 for link in LINKS[level]]

    def share(tile, level, flips=0):
        index = 0
        for place, link in enumerate(links_of(tile, level)):
            index = index * 2 + (1 - bits[link] if flips >> place & 1 else bits[link])
        return index

    def flipped(tile, level, flips):
        return across([link for place, link in enumerate(links_of(tile, level)) if flips >> place & 1])

    lows = [0] * TILES

    def split_rows(tile, level):
        held = held_ref.at[tile]
        size = SIZES[level + 1]
        for flips in range(1, 2 ** len(LINKS[level])):
            send(
                tile,
                level,
                held.at[rows_at(lows[tile] + share(tile, level, flips) * size, size), :],
                landed_ref.at[tile, pl.ds(BASES[level] + (flips - 1) * size, size), :],
                flipped(tile, level, flips),
            )
        lows[tile] = lows[tile] + share(tile, level) * size

    def return_rows(tile, level):
        size = SIZES[level + 1]
        place = total_ref.at[tile, rows_at(core * 512 + lows[tile], size), :]
        for flips in range(1, 2 ** len(LINKS[level])):
            send(tile, STAGES - 1 - level, place, place, flipped(tile, level, flips))

    def advance(tile, stage):
        level = level_of(stage)
        held = held_ref.at[tile]
        wait(tile, stage, recv_sem)
        if stage == 0:
            held[...] = part_ref[tile, rows_at(core * 512, 512), :] + landed_ref[tile, 0:512, :]
            split_rows(tile, 1)
        elif stage < HALF_STAGES:
            size = SIZES[level + 1]
            value = held[rows_at(lows[tile], size), :]
            for piece in range(2 ** len(LINKS[level]) - 1):
                start = BASES[level] + piece * size
                value += landed_ref[tile, start : start + size, :]
            if stage < HALF_STAGES - 1:
                held[rows_at(lows[tile], size), :] = value
                split_rows(tile, level + 1)
            else:
                total_ref[tile, rows_at(core * 512 + lows[tile], size), :] = value
                return_rows(tile, level)
        elif stage < STAGES - 1:
            lows[tile] = lows[tile] - share(tile, level) * SIZES[level + 1]
            if level > 1:
                return_rows(tile, level - 1)
            else:
                place = total_ref.at[tile, rows_at(core * 512, 512), :]
                send(tile, STAGES - 1, place, place, sibling)

    def parts(tile):
        values = total_ref[tile]
        real_part = jnp.concatenate([values[0:256], values[512:768]], axis=1)
        imag_part = jnp.concatenate([values[256:512], values[768:1024]], axis=1)
        return real_part, imag_part

    def correct(piece):
        if piece == 0:
            cross = complex_dot(left_forms(*parts(TILES - 1)), right_forms(*adjoint_upper(tri_ref, 0)))
            cross = right_forms(*cross)
            for form in range(3):
                factor_ref[0, form] = cross[form]
        rows = slice(piece * 256, (piece + 1) * 256)
        second = left_forms(x_ref[0, rows, 256:512], x_ref[1, rows, 256:512])
        real_part, imag_part = complex_dot(second, [factor_ref[0, form] for form in range(3)])
        first = left_forms(x_ref[0, rows, 0:256] - real_part, x_ref[1, rows, 0:256] - imag_part)
        for form in range(3):
            for part in range(2):
                source = slice((part + 1) * 256, (part + 2) * 256)
                start = part * 512
                left_ref[form, rows, start : start + 256] = first[form][:, source]
                left_ref[form, rows, start + 256 : start + 512] = second[form][:, source]

    written = []

    def apply(chunk, piece):
        if piece == 0:
            first = parts(2 * chunk)
            second = parts(2 * chunk + 1)
            forms = right_forms(*[jnp.concatenate([first[part], second[part]], axis=0) for part in range(2)])
            for form in range(3):
                right_ref[form, 0:512, :] = forms[form][512:1024]
                right_ref[form, 512:1024, :] = forms[form][0:512]
                right_ref[form, 1024:1536, :] = forms[form][0:512]
        rows = slice(piece * 256, (piece + 1) * 256)
        sums = [
            dot(left_ref[form, rows, 0:512], right_ref[form, 0:512, :])
            + dot(left_ref[form, rows, :], right_ref[form, 512:1536, :])
            for form in range(3)
        ]
        change = (sums[0] - sums[2], sums[0] + sums[1])
        for part in range(2):
            first_blocks_ref[piece * 32 : (piece + 1) * 32, part] = change[part].reshape(32, 8, 256)
        if piece < 3:
            return
        if len(written) > 1:
            written[-2].wait()
        columns = slice(chunk * 256, (chunk + 1) * 256)
        result = rows_ref.at[len(written) % 2]

        def put_block(block, carry):
            slot = slot_ref[4, block]
            rows = pl.ds(pl.multiple_of(block * 8, 8), 8)
            for part in range(2):
                result[part, rows, :] = z_ref[part, block, :, columns] - first_blocks_ref[slot, part]
            return carry

        lax.fori_loop(0, 128, put_block, 0, unroll=8)
        copy = pltpu.make_async_copy(result, out_ref.at[:, :, columns], local_sem.at[5 + len(written)])
        copy.start()
        written.append(copy)

    def begin(tile):
        send(
            tile,
            0,
            part_ref.at[tile, rows_at((1 - core) * 512, 512), :],
            landed_ref.at[tile, pl.ds(0, 512), :],
            sibling,
        )

    for panel in range(2):
        for group in range(len(GROUPS[panel])):
            take_group(panel, group, begin if group == len(GROUPS[panel]) - 1 else None)
    for tile, step in step_order():
        if tile is None:
            correct(step)
        elif tile < 0:
            apply(-1 - tile, step)
        else:
            advance(tile, step)
    await_bytes(all_ids_ref.at[pl.ds(0, 127)], id_sem.at[0])
    for panel in range(2):
        await_bytes(blocks_refs[panel].at[pl.ds(0, 127)], block_send_sem.at[panel])
    for tile in range(TILES):
        for stage in range(STAGES):
            wait(tile, stage, send_sem)
    for copy in written[-2:]:
        copy.wait()


def move_kernel(source_ref, target_ref, held_ref, in_sem, out_sem):
    into = []
    out_of = []
    for piece in range(16):
        place = (piece // 8, pl.ds(piece % 8 * 128, 128))
        into.append(pltpu.make_async_copy(source_ref.at[place], held_ref.at[place], in_sem.at[piece]))
        out_of.append(pltpu.make_async_copy(held_ref.at[place], target_ref.at[place], out_sem.at[piece]))
    for copy in into:
        copy.start()
    for arriving, leaving in zip(into, out_of):
        arriving.wait()
        leaving.start()
    for copy in out_of:
        copy.wait()


def per_device(vectors, panel_store, block_ids, offsets, tri_factors):
    f32 = jnp.float32
    bf16 = jnp.bfloat16
    whole = pl.BlockSpec(memory_space=pltpu.VMEM)
    anywhere = pl.BlockSpec(memory_space=pl.ANY)
    dma = pltpu.SemaphoreType.DMA
    result = pl.pallas_call(
        main_kernel,
        out_shape=jax.ShapeDtypeStruct(vectors.shape, f32),
        in_specs=[pl.BlockSpec(memory_space=pltpu.SMEM), whole, anywhere, whole, anywhere],
        out_specs=anywhere,
        scratch_shapes=[
            pltpu.VMEM((2, 2, 1024, 256), f32),
            pltpu.VMEM((2, 128, 8, 1024), f32),
            pltpu.VMEM((128, 2, 8, 256), f32),
            pltpu.VMEM((128, 2, 8, 256), f32),
            pltpu.VMEM((128, 2, 128), jnp.int32),
            pltpu.VMEM((8, 128), jnp.int32),
            pltpu.SMEM((8, 128), jnp.int32),
            pltpu.VMEM((2, 128, 8, 256), f32),
            pltpu.VMEM((2, 32, 8, 256), f32),
            pltpu.VMEM((2, 2, 1024, 256), f32),
            pltpu.VMEM((2, 256, 256), f32),
            pltpu.VMEM((3, 256, 1536), bf16),
            pltpu.VMEM((2, 3, 768, 256), bf16),
            pltpu.VMEM((TILES, 1024, 128), f32),
            pltpu.VMEM((2, 1024, 512), f32),
            pltpu.VMEM((TILES, 1024, 128), f32),
            pltpu.VMEM((TILES, 512, 128), f32),
            pltpu.VMEM((TILES, 1024, 128), f32),
            pltpu.VMEM((3, 1024, 1024), bf16),
            pltpu.VMEM((3, 1536, 256), bf16),
            dma((2,)),
            dma((2, 5)),
            dma((2,)),
            dma((TILES, STAGES)),
            dma((TILES, STAGES)),
            dma((11,)),
        ],
        compiler_params=pltpu.CompilerParams(
            vmem_limit_bytes=VMEM_LIMIT, collective_id=0, has_side_effects=True
        ),
        name="main",
    )(offsets, block_ids, panel_store, tri_factors, vectors.reshape(2, 128, 8, 1024))
    return pl.pallas_call(
        move_kernel,
        out_shape=jax.ShapeDtypeStruct(vectors.shape, f32),
        in_specs=[anywhere],
        out_specs=anywhere,
        scratch_shapes=[pltpu.VMEM(vectors.shape, f32), dma((16,)), dma((16,))],
        compiler_params=pltpu.CompilerParams(vmem_limit_bytes=VMEM_LIMIT),
        name="move",
    )(result)


def solution(mesh):
    placed = (
        P(None, ("row", "col"), None),
        P(None, None, ("row", "col"), None),
        P(None, ("row", "col")),
        P(),
        P(),
    )
    return jax.shard_map(
        per_device,
        mesh=mesh,
        in_specs=placed,
        out_specs=P(None, ("row", "col"), None),
        check_vma=False,
    )
```

```python
import jax
import jax.numpy as jnp
from jax import lax
from jax.experimental import pallas as pl
from jax.experimental.pallas import tpu as pltpu
from jax.sharding import PartitionSpec as P


MESH = pl.DeviceIdType.MESH


def strip_of(x, y, z, core):
    return ((x * 2 + z % 2) * 4 + y) * 4 + (z // 2) * 2 + core


VMEM_LIMIT = 60 * 1024 * 1024


def split(value):
    high = value.astype(jnp.bfloat16)
    return high, (value - high.astype(jnp.float32)).astype(jnp.bfloat16)


def dot(first_op, second_op):
    return jnp.dot(first_op, second_op, preferred_element_type=jnp.float32)


def left_pieces(value):
    high, low = split(value)
    return jnp.concatenate([high, high, low], axis=1)


def right_pieces(value):
    high, low = split(value)
    return jnp.concatenate([high, low, high], axis=0)


def left_forms(real_part, imag_part):
    return left_pieces(real_part + imag_part), left_pieces(real_part), left_pieces(imag_part)


def right_forms(real_part, imag_part):
    return right_pieces(real_part), right_pieces(imag_part - real_part), right_pieces(real_part + imag_part)


def complex_dot(left, right):
    shared = dot(left[0], right[0])
    return shared - dot(left[2], right[2]), shared + dot(left[1], right[1])


def adjoint_upper(tri_ref, panel):
    shape = tri_ref.shape[2:]
    upper = lax.broadcasted_iota(jnp.int32, shape, 0) <= lax.broadcasted_iota(jnp.int32, shape, 1)
    return jnp.where(upper, tri_ref[panel, 0], 0.0).T, -jnp.where(upper, tri_ref[panel, 1], 0.0).T


GROUPS = (
    ((0, 64), (64, 64)),
    ((0, 32), (32, 32), (64, 32), (96, 16), (112, 16)),
)


TILES = 9
LINKS = ((), (0, 1), (2, 3), (4, 5))
FIRST_LINKS = (3, 4, 2, 2, 5, 0, 4, 3, 0)
APART = 2.5
HALF_STAGES = len(LINKS)
STAGES = 2 * HALF_STAGES
SIZES = [1024, 512, 128, 32, 8]
COUNTS = [SIZES[stage] - SIZES[stage + 1] for stage in range(HALF_STAGES)]
BASES = [sum(COUNTS[:stage]) for stage in range(HALF_STAGES)]


def level_of(stage):
    return stage if stage < HALF_STAGES else STAGES - 1 - stage


def step_order():
    free = [0.0] * 7
    now = 0.0
    ready = []
    order = []
    work = []
    finished = set()
    queued = set()

    def send(tile, stage):
        nonlocal now
        level = level_of(stage)
        now += 0.06 * (2 ** len(LINKS[level]) - 1 if level else 1)
        if level == 0:
            free[6] = max(free[6], now) + 512 * 0.512 / 600
            arrival = free[6]
        else:
            arrival = now
            for link in LINKS[level]:
                link = (FIRST_LINKS[tile] + link) % 6
                free[link] = max(free[link], now) + SIZES[level] / 2 * 0.512 / 50
                arrival = max(arrival, free[link])
        if stage == 0 and tile < TILES - 1:
            arrival = max(arrival, tile // 2 * APART + 0.5)
        ready.append((arrival + 2.5, tile, stage))

    for tile in range(0, TILES - 1, 2):
        ready.append((tile // 2 * APART, tile, 0))
    for tile in [TILES - 1] + list(range(1, TILES - 1, 2)):
        now += 0.5
        send(tile, 0)
    while ready or work:
        ready.sort()
        if ready and (ready[0][0] <= now or not work):
            arrival, tile, stage = ready.pop(0)
            order.append((tile, stage))
            now = max(now, arrival) + (0.05 + COUNTS[stage] * 0.0006 if stage < HALF_STAGES else 0.03)
            if stage < STAGES - 1:
                send(tile, stage + 1)
            else:
                finished.add(tile)
            if TILES - 1 in finished:
                if None not in queued:
                    queued.add(None)
                    work += [(None, piece) for piece in range(4)]
                for chunk in range(4):
                    if chunk not in queued and {2 * chunk, 2 * chunk + 1} <= finished:
                        queued.add(chunk)
                        work += [(-1 - chunk, piece) for piece in range(4)]
        else:
            order.append(work.pop(0))
            now += 0.8
    return order


def main_kernel(
    offsets_ref,
    ids_ref,
    store_ref,
    tri_ref,
    vectors_ref,
    out_ref,
    listed_ref,
    z_ref,
    first_blocks_ref,
    second_blocks_ref,
    all_ids_ref,
    order_ref,
    slot_ref,
    first_panel_ref,
    second_panel_ref,
    rows_ref,
    match_ref,
    adjoint_ref,
    factor_ref,
    part_ref,
    x_ref,
    total_ref,
    held_ref,
    landed_ref,
    left_ref,
    right_ref,
    block_send_sem,
    block_recv_sem,
    id_sem,
    send_sem,
    recv_sem,
    local_sem,
):
    blocks_refs = (first_blocks_ref, second_blocks_ref)
    panel_refs = (first_panel_ref, second_panel_ref)
    row = lax.axis_index("row")
    col = lax.axis_index("col")
    me = row * 4 + col
    x = row // 8
    y = row % 4
    z = (col // 2) * 2 + (row // 4) % 2
    here = (x, y, z)
    core = col % 2

    barrier = pltpu.get_barrier_semaphore()

    def greet(step, carry):
        peer = (me + step) % 128
        pl.semaphore_signal(barrier, inc=1, device_id=(peer // 4, peer % 4), device_id_type=MESH)
        return carry

    lax.fori_loop(1, 128, greet, 0)

    def listed(strip):
        return pl.ds(pl.multiple_of(strip * 8, 8), 8)

    own_copies = [
        pltpu.make_async_copy(store_ref.at[panel, :, listed(me), :], blocks_refs[panel].at[0], local_sem.at[panel])
        for panel in range(2)
    ]
    own_copies.append(pltpu.make_async_copy(ids_ref, all_ids_ref.at[0], local_sem.at[2]))
    fetch_store = [
        pltpu.make_async_copy(store_ref.at[panel], listed_ref.at[panel], local_sem.at[9 + panel]) for panel in range(2)
    ]
    fetch_store[0].start()
    fetch_store[1].start()
    for copy in own_copies:
        copy.start()
    fetch_vectors = pltpu.make_async_copy(vectors_ref, z_ref, local_sem.at[3])
    fetch_vectors.start()

    for panel in range(2):
        forms = right_forms(*adjoint_upper(tri_ref, panel))
        for form in range(3):
            factor_ref[panel, form] = forms[form]

    pl.semaphore_wait(barrier, 127)

    def remote(source, target, sent, received, device):
        return pltpu.make_async_remote_copy(
            source,
            target,
            sent,
            received,
            device_id=device,
            device_id_type=MESH,
        )

    def strip_at(step):
        spread = (step // 2 * 27) % 64
        return strip_of(
            (x + spread % 4) % 4, (y + (spread // 4) % 4) % 4, (z + spread // 16) % 4, (core + step) % 2
        )

    def send_blocks(panel, group, first, last):
        def body(step, carry):
            strip = strip_at(step)
            remote(
                listed_ref.at[panel, :, listed(strip), :],
                blocks_refs[panel].at[step],
                block_send_sem.at[panel],
                block_recv_sem.at[panel, group],
                (strip // 4, strip % 4),
            ).start()
            return carry

        lax.fori_loop(first, last, body, 0)

    def send_ids(step, carry):
        strip = strip_at(step)
        remote(ids_ref, all_ids_ref.at[step], id_sem.at[0], id_sem.at[1], (strip // 4, strip % 4)).start()
        return carry

    def await_bytes(some, sem):
        pltpu.make_async_copy(some, some, sem).wait()

    fetch_store[0].wait()
    send_blocks(0, 0, 1, 24)
    lax.fori_loop(1, 128, send_ids, 0)
    send_blocks(0, 0, 24, 64)
    fetch_store[1].wait()
    for panel in range(2):
        for group, (first, count) in enumerate(GROUPS[panel]):
            if panel + group > 0:
                send_blocks(panel, group, max(first, 1), first + count)

    for copy in own_copies:
        copy.wait()
    await_bytes(all_ids_ref.at[pl.ds(1, 127)], id_sem.at[1])
    down = lax.broadcasted_iota(jnp.int32, (128, 128), 0)
    lane = lax.broadcasted_iota(jnp.int32, (128, 128), 1)
    order_ref[...] = jnp.zeros_like(order_ref)
    places = []
    for panel in range(2):
        own = jnp.sum(jnp.where(lane == me, all_ids_ref[:, panel, :], 0), axis=1, keepdims=True) % 128
        places.append(jnp.sum(jnp.where(down == lane, own, 0), axis=0, keepdims=True))
        order_ref[panel : panel + 1, :] = places[panel]
        order_ref[panel + 3 : panel + 4, :] = jnp.max(jnp.where(own == lane, down, 0), axis=0, keepdims=True)
    slot_of_place = jnp.max(jnp.where(places[0] == down, lane, 0), axis=1, keepdims=True)
    order_ref[2:3, :] = jnp.max(jnp.where(places[1] == down, slot_of_place, 0), axis=0, keepdims=True)
    fetch_order = pltpu.make_async_copy(order_ref, slot_ref, local_sem.at[4])
    fetch_order.start()
    fetch_order.wait()
    fetch_vectors.wait()

    def take_group(panel, group, begin_tile):
        first, count = GROUPS[panel][group]
        size = count * 8
        start = first * 8
        begin = first == 0
        values = panel_refs[panel]
        kept = first if panel == 0 else 0

        await_bytes(
            blocks_refs[panel].at[pl.ds(max(first, 1), first + count - max(first, 1))], block_recv_sem.at[panel, group]
        )

        def take_block(step, carry):
            slot = first + step
            place = slot_ref[panel, slot]
            near = pl.ds(pl.multiple_of(step * 8, 8), 8)
            row_index = me * 1024 + place * 8 + lax.broadcasted_iota(jnp.int32, (8, 256), 0)
            limit = offsets_ref[panel] + lax.broadcasted_iota(jnp.int32, (8, 256), 1)
            below = row_index > limit
            diagonal = jnp.where(row_index == limit, 1.0, 0.0)
            values[0, kept + step] = jnp.where(below, blocks_refs[panel][slot, 0], diagonal)
            values[1, kept + step] = jnp.where(below, blocks_refs[panel][slot, 1], 0.0)
            for part in range(2):
                wanted = z_ref[part, place]
                for chunk in range(4):
                    at = pl.ds(pl.multiple_of(chunk % 2 * 512 + step * 8, 8), 8)
                    rows_ref[chunk // 2, part, at, :] = wanted[:, chunk * 256 : (chunk + 1) * 256]
            if panel == 1:
                matching = slot_ref[2, slot]
                match_ref[0, near, :] = first_panel_ref[0, matching]
                match_ref[1, near, :] = first_panel_ref[1, matching]
            return carry

        lax.fori_loop(0, count, take_block, 0, unroll=4)

        own = [values[part, kept : kept + count].reshape(size, 256) for part in range(2)]
        forms = left_forms(own[0].T, -own[1].T)
        for form in range(3):
            adjoint_ref[form, :, 0 : 3 * size] = forms[form]

        def adjoint_products(right):
            return complex_dot([adjoint_ref[form, :, 0 : 3 * size] for form in range(3)], right)

        def add_tile(tile, parts):
            for part in range(2):
                for side in range(2):
                    value = parts[part][:, side * 128 : (side + 1) * 128]
                    start = side * 512 + part * 256
                    target = part_ref.at[tile, start : start + 256, :]
                    if begin:
                        target[...] = value
                    else:
                        target[...] += value

        if panel == 1:
            matched = (match_ref[0, 0:size, :], match_ref[1, 0:size, :])
            add_tile(TILES - 1, adjoint_products(right_forms(*matched)))
            if begin_tile is not None:
                begin_tile(TILES - 1)

        def take_columns(chunk, carry):
            at = pl.ds(pl.multiple_of(chunk % 2 * 512, 512), size)
            right = right_forms(rows_ref[chunk // 2, 0, at, :], rows_ref[chunk // 2, 1, at, :])
            add_tile(2 * chunk + panel, adjoint_products(right))
            return carry

        if begin_tile is None:
            lax.fori_loop(0, 4, take_columns, 0)
        else:
            for chunk in range(4):
                take_columns(chunk, 0)
                begin_tile(2 * chunk + panel)

        if panel == 1:
            for which, source in enumerate((matched, own)):
                scaled = complex_dot(left_forms(*source), [factor_ref[which, form] for form in range(3)])
                for part in range(2):
                    x_ref[part, start : start + size, which * 256 : (which + 1) * 256] = scaled[part]

    def device(place, core):
        strip = strip_of(*place, core)
        return (strip // 4, strip % 4)

    sibling = device(here, 1 - core)
    other = [place + 1 - 2 * (place % 2) for place in here] + [3 - place for place in here]
    bits = [((place + 1) // 2) % 2 for place in here] + [place // 2 for place in here]

    def across(links):
        place = list(here)
        for link in links:
            place[link % 3] = other[link]
        return device(place, core)

    def rows_at(first, count):
        return pl.ds(pl.multiple_of(first, 8), count)

    def send(tile, stage, source, target, peer):
        remote(source, target, send_sem.at[tile, stage], recv_sem.at[tile, stage], peer).start()

    def wait(tile, stage, sem):
        some = landed_ref.at[tile, pl.ds(0, COUNTS[level_of(stage)]), :]
        pltpu.make_async_copy(some, some, sem.at[tile, stage]).wait()

    def links_of(tile, level):
        return [(FIRST_LINKS[tile] + link) % 6 for link in LINKS[level]]

    def share(tile, level, flips=0):
        index = 0
        for place, link in enumerate(links_of(tile, level)):
            index = index * 2 + (1 - bits[link] if flips >> place & 1 else bits[link])
        return index

    def flipped(tile, level, flips):
        return across([link for place, link in enumerate(links_of(tile, level)) if flips >> place & 1])

    lows = [0] * TILES

    def split_rows(tile, level):
        held = held_ref.at[tile]
        size = SIZES[level + 1]
        for flips in range(1, 2 ** len(LINKS[level])):
            send(
                tile,
                level,
                held.at[rows_at(lows[tile] + share(tile, level, flips) * size, size), :],
                landed_ref.at[tile, pl.ds(BASES[level] + (flips - 1) * size, size), :],
                flipped(tile, level, flips),
            )
        lows[tile] = lows[tile] + share(tile, level) * size

    def return_rows(tile, level):
        size = SIZES[level + 1]
        place = total_ref.at[tile, rows_at(core * 512 + lows[tile], size), :]
        for flips in range(1, 2 ** len(LINKS[level])):
            send(tile, STAGES - 1 - level, place, place, flipped(tile, level, flips))

    def advance(tile, stage):
        level = level_of(stage)
        held = held_ref.at[tile]
        wait(tile, stage, recv_sem)
        if stage == 0:
            held[...] = part_ref[tile, rows_at(core * 512, 512), :] + landed_ref[tile, 0:512, :]
            split_rows(tile, 1)
        elif stage < HALF_STAGES:
            size = SIZES[level + 1]
            value = held[rows_at(lows[tile], size), :]
            for piece in range(2 ** len(LINKS[level]) - 1):
                start = BASES[level] + piece * size
                value += landed_ref[tile, start : start + size, :]
            if stage < HALF_STAGES - 1:
                held[rows_at(lows[tile], size), :] = value
                split_rows(tile, level + 1)
            else:
                total_ref[tile, rows_at(core * 512 + lows[tile], size), :] = value
                return_rows(tile, level)
        elif stage < STAGES - 1:
            lows[tile] = lows[tile] - share(tile, level) * SIZES[level + 1]
            if level > 1:
                return_rows(tile, level - 1)
            else:
                place = total_ref.at[tile, rows_at(core * 512, 512), :]
                send(tile, STAGES - 1, place, place, sibling)

    def parts(tile):
        values = total_ref[tile]
        real_part = jnp.concatenate([values[0:256], values[512:768]], axis=1)
        imag_part = jnp.concatenate([values[256:512], values[768:1024]], axis=1)
        return real_part, imag_part

    def correct(piece):
        if piece == 0:
            cross = complex_dot(left_forms(*parts(TILES - 1)), right_forms(*adjoint_upper(tri_ref, 0)))
            cross = right_forms(*cross)
            for form in range(3):
                factor_ref[0, form] = cross[form]
        rows = slice(piece * 256, (piece + 1) * 256)
        second = left_forms(x_ref[0, rows, 256:512], x_ref[1, rows, 256:512])
        real_part, imag_part = complex_dot(second, [factor_ref[0, form] for form in range(3)])
        first = left_forms(x_ref[0, rows, 0:256] - real_part, x_ref[1, rows, 0:256] - imag_part)
        for form in range(3):
            for part in range(2):
                source = slice((part + 1) * 256, (part + 2) * 256)
                start = part * 512
                left_ref[form, rows, start : start + 256] = first[form][:, source]
                left_ref[form, rows, start + 256 : start + 512] = second[form][:, source]

    written = []

    def apply(chunk, piece):
        if piece == 0:
            first = parts(2 * chunk)
            second = parts(2 * chunk + 1)
            forms = right_forms(*[jnp.concatenate([first[part], second[part]], axis=0) for part in range(2)])
            for form in range(3):
                right_ref[form, 0:512, :] = forms[form][512:1024]
                right_ref[form, 512:1024, :] = forms[form][0:512]
                right_ref[form, 1024:1536, :] = forms[form][0:512]
        rows = slice(piece * 256, (piece + 1) * 256)
        sums = [
            dot(left_ref[form, rows, 0:512], right_ref[form, 0:512, :])
            + dot(left_ref[form, rows, :], right_ref[form, 512:1536, :])
            for form in range(3)
        ]
        change = (sums[0] - sums[2], sums[0] + sums[1])
        for part in range(2):
            first_blocks_ref[piece * 32 : (piece + 1) * 32, part] = change[part].reshape(32, 8, 256)
        if piece < 3:
            return
        if len(written) > 1:
            written[-2].wait()
        columns = slice(chunk * 256, (chunk + 1) * 256)
        result = rows_ref.at[len(written) % 2]

        def put_block(block, carry):
            slot = slot_ref[4, block]
            rows = pl.ds(pl.multiple_of(block * 8, 8), 8)
            for part in range(2):
                result[part, rows, :] = z_ref[part, block, :, columns] - first_blocks_ref[slot, part]
            return carry

        lax.fori_loop(0, 128, put_block, 0, unroll=8)
        copy = pltpu.make_async_copy(result, out_ref.at[:, :, columns], local_sem.at[5 + len(written)])
        copy.start()
        written.append(copy)

    def begin(tile):
        send(
            tile,
            0,
            part_ref.at[tile, rows_at((1 - core) * 512, 512), :],
            landed_ref.at[tile, pl.ds(0, 512), :],
            sibling,
        )

    for panel in range(2):
        for group in range(len(GROUPS[panel])):
            take_group(panel, group, begin if group == len(GROUPS[panel]) - 1 else None)
    for tile, step in step_order():
        if tile is None:
            correct(step)
        elif tile < 0:
            apply(-1 - tile, step)
        else:
            advance(tile, step)
    await_bytes(all_ids_ref.at[pl.ds(0, 127)], id_sem.at[0])
    for panel in range(2):
        await_bytes(blocks_refs[panel].at[pl.ds(0, 127)], block_send_sem.at[panel])
    for tile in range(TILES):
        for stage in range(STAGES):
            wait(tile, stage, send_sem)
    for copy in written[-2:]:
        copy.wait()


def move_kernel(source_ref, target_ref, held_ref, in_sem, out_sem):
    into = []
    out_of = []
    for piece in range(16):
        place = (piece // 8, pl.ds(piece % 8 * 128, 128))
        into.append(pltpu.make_async_copy(source_ref.at[place], held_ref.at[place], in_sem.at[piece]))
        out_of.append(pltpu.make_async_copy(held_ref.at[place], target_ref.at[place], out_sem.at[piece]))
    for copy in into:
        copy.start()
    for arriving, leaving in zip(into, out_of):
        arriving.wait()
        leaving.start()
    for copy in out_of:
        copy.wait()


def per_device(vectors, panel_store, block_ids, offsets, tri_factors):
    f32 = jnp.float32
    bf16 = jnp.bfloat16
    whole = pl.BlockSpec(memory_space=pltpu.VMEM)
    anywhere = pl.BlockSpec(memory_space=pl.ANY)
    dma = pltpu.SemaphoreType.DMA
    result = pl.pallas_call(
        main_kernel,
        out_shape=jax.ShapeDtypeStruct(vectors.shape, f32),
        in_specs=[pl.BlockSpec(memory_space=pltpu.SMEM), whole, anywhere, whole, anywhere],
        out_specs=anywhere,
        scratch_shapes=[
            pltpu.VMEM((2, 2, 1024, 256), f32),
            pltpu.VMEM((2, 128, 8, 1024), f32),
            pltpu.VMEM((128, 2, 8, 256), f32),
            pltpu.VMEM((128, 2, 8, 256), f32),
            pltpu.VMEM((128, 2, 128), jnp.int32),
            pltpu.VMEM((8, 128), jnp.int32),
            pltpu.SMEM((8, 128), jnp.int32),
            pltpu.VMEM((2, 128, 8, 256), f32),
            pltpu.VMEM((2, 32, 8, 256), f32),
            pltpu.VMEM((2, 2, 1024, 256), f32),
            pltpu.VMEM((2, 256, 256), f32),
            pltpu.VMEM((3, 256, 1536), bf16),
            pltpu.VMEM((2, 3, 768, 256), bf16),
            pltpu.VMEM((TILES, 1024, 128), f32),
            pltpu.VMEM((2, 1024, 512), f32),
            pltpu.VMEM((TILES, 1024, 128), f32),
            pltpu.VMEM((TILES, 512, 128), f32),
            pltpu.VMEM((TILES, 1024, 128), f32),
            pltpu.VMEM((3, 1024, 1024), bf16),
            pltpu.VMEM((3, 1536, 256), bf16),
            dma((2,)),
            dma((2, 5)),
            dma((2,)),
            dma((TILES, STAGES)),
            dma((TILES, STAGES)),
            dma((11,)),
        ],
        compiler_params=pltpu.CompilerParams(
            vmem_limit_bytes=VMEM_LIMIT, collective_id=0, has_side_effects=True
        ),
        name="main",
    )(offsets, block_ids, panel_store, tri_factors, vectors.reshape(2, 128, 8, 1024))
    return pl.pallas_call(
        move_kernel,
        out_shape=jax.ShapeDtypeStruct(vectors.shape, f32),
        in_specs=[anywhere],
        out_specs=anywhere,
        scratch_shapes=[pltpu.VMEM(vectors.shape, f32), dma((16,)), dma((16,))],
        compiler_params=pltpu.CompilerParams(vmem_limit_bytes=VMEM_LIMIT),
        name="move",
    )(result)


def solution(mesh):
    placed = (
        P(None, ("row", "col"), None),
        P(None, None, ("row", "col"), None),
        P(None, ("row", "col")),
        P(),
        P(),
    )
    return jax.shard_map(
        per_device,
        mesh=mesh,
        in_specs=placed,
        out_specs=P(None, ("row", "col"), None),
        check_vma=False,
    )
```

```python
import jax
import jax.numpy as jnp
from jax import lax
from jax.experimental import pallas as pl
from jax.experimental.pallas import tpu as pltpu
from jax.sharding import PartitionSpec as P


MESH = pl.DeviceIdType.MESH


def strip_of(x, y, z, core):
    return ((x * 2 + z % 2) * 4 + y) * 4 + (z // 2) * 2 + core


VMEM_LIMIT = 60 * 1024 * 1024


def split(value):
    high = value.astype(jnp.bfloat16)
    return high, (value - high.astype(jnp.float32)).astype(jnp.bfloat16)


def dot(first_op, second_op):
    return jnp.dot(first_op, second_op, preferred_element_type=jnp.float32)


def left_pieces(value):
    high, low = split(value)
    return jnp.concatenate([high, high, low], axis=1)


def right_pieces(value):
    high, low = split(value)
    return jnp.concatenate([high, low, high], axis=0)


def left_forms(real_part, imag_part):
    return left_pieces(real_part + imag_part), left_pieces(real_part), left_pieces(imag_part)


def right_forms(real_part, imag_part):
    return right_pieces(real_part), right_pieces(imag_part - real_part), right_pieces(real_part + imag_part)


def complex_dot(left, right):
    shared = dot(left[0], right[0])
    return shared - dot(left[2], right[2]), shared + dot(left[1], right[1])


def adjoint_upper(tri_ref, panel):
    shape = tri_ref.shape[2:]
    upper = lax.broadcasted_iota(jnp.int32, shape, 0) <= lax.broadcasted_iota(jnp.int32, shape, 1)
    return jnp.where(upper, tri_ref[panel, 0], 0.0).T, -jnp.where(upper, tri_ref[panel, 1], 0.0).T


GROUPS = (
    ((0, 64), (64, 64)),
    ((0, 32), (32, 32), (64, 32), (96, 16), (112, 16)),
)


TILES = 9
LINKS = ((), (0, 1), (2, 3), (4, 5))
FIRST_LINKS = (3, 4, 2, 2, 5, 0, 4, 3, 0)
APART = 2.5
HALF_STAGES = len(LINKS)
STAGES = 2 * HALF_STAGES
SIZES = [1024, 512, 128, 32, 8]
COUNTS = [SIZES[stage] - SIZES[stage + 1] for stage in range(HALF_STAGES)]
BASES = [sum(COUNTS[:stage]) for stage in range(HALF_STAGES)]


def level_of(stage):
    return stage if stage < HALF_STAGES else STAGES - 1 - stage


def step_order():
    free = [0.0] * 7
    now = 0.0
    ready = []
    order = []
    work = []
    finished = set()
    queued = set()

    def send(tile, stage):
        nonlocal now
        level = level_of(stage)
        now += 0.06 * (2 ** len(LINKS[level]) - 1 if level else 1)
        if level == 0:
            free[6] = max(free[6], now) + 512 * 0.512 / 600
            arrival = free[6]
        else:
            arrival = now
            for link in LINKS[level]:
                link = (FIRST_LINKS[tile] + link) % 6
                free[link] = max(free[link], now) + SIZES[level] / 2 * 0.512 / 50
                arrival = max(arrival, free[link])
        if stage == 0 and tile < TILES - 1:
            arrival = max(arrival, tile // 2 * APART + 0.5)
        ready.append((arrival + 2.5, tile, stage))

    for tile in range(0, TILES - 1, 2):
        ready.append((tile // 2 * APART, tile, 0))
    for tile in [TILES - 1] + list(range(1, TILES - 1, 2)):
        now += 0.5
        send(tile, 0)
    while ready or work:
        ready.sort()
        if ready and (ready[0][0] <= now or not work):
            arrival, tile, stage = ready.pop(0)
            order.append((tile, stage))
            now = max(now, arrival) + (0.05 + COUNTS[stage] * 0.0006 if stage < HALF_STAGES else 0.03)
            if stage < STAGES - 1:
                send(tile, stage + 1)
            else:
                finished.add(tile)
            if TILES - 1 in finished:
                if None not in queued:
                    queued.add(None)
                    work += [(None, piece) for piece in range(4)]
                for chunk in range(4):
                    if chunk not in queued and {2 * chunk, 2 * chunk + 1} <= finished:
                        queued.add(chunk)
                        work += [(-1 - chunk, piece) for piece in range(4)]
        else:
            order.append(work.pop(0))
            now += 0.8
    return order


def main_kernel(
    offsets_ref,
    ids_ref,
    store_ref,
    tri_ref,
    vectors_ref,
    out_ref,
    listed_ref,
    z_ref,
    first_blocks_ref,
    second_blocks_ref,
    all_ids_ref,
    order_ref,
    slot_ref,
    first_panel_ref,
    second_panel_ref,
    rows_ref,
    match_ref,
    adjoint_ref,
    factor_ref,
    part_ref,
    x_ref,
    total_ref,
    held_ref,
    landed_ref,
    left_ref,
    right_ref,
    block_send_sem,
    block_recv_sem,
    id_sem,
    send_sem,
    recv_sem,
    local_sem,
):
    blocks_refs = (first_blocks_ref, second_blocks_ref)
    panel_refs = (first_panel_ref, second_panel_ref)
    row = lax.axis_index("row")
    col = lax.axis_index("col")
    me = row * 4 + col
    x = row // 8
    y = row % 4
    z = (col // 2) * 2 + (row // 4) % 2
    here = (x, y, z)
    core = col % 2

    barrier = pltpu.get_barrier_semaphore()

    def greet(step, carry):
        peer = (me + step) % 128
        pl.semaphore_signal(barrier, inc=1, device_id=(peer // 4, peer % 4), device_id_type=MESH)
        return carry

    lax.fori_loop(1, 128, greet, 0)

    def listed(strip):
        return pl.ds(pl.multiple_of(strip * 8, 8), 8)

    own_copies = [
        pltpu.make_async_copy(store_ref.at[panel, :, listed(me), :], blocks_refs[panel].at[0], local_sem.at[panel])
        for panel in range(2)
    ]
    own_copies.append(pltpu.make_async_copy(ids_ref, all_ids_ref.at[0], local_sem.at[2]))
    fetch_store = [
        pltpu.make_async_copy(store_ref.at[panel], listed_ref.at[panel], local_sem.at[9 + panel]) for panel in range(2)
    ]
    fetch_store[0].start()
    fetch_store[1].start()
    for copy in own_copies:
        copy.start()
    fetch_vectors = pltpu.make_async_copy(vectors_ref, z_ref, local_sem.at[3])
    fetch_vectors.start()

    for panel in range(2):
        forms = right_forms(*adjoint_upper(tri_ref, panel))
        for form in range(3):
            factor_ref[panel, form] = forms[form]

    pl.semaphore_wait(barrier, 127)

    def remote(source, target, sent, received, device):
        return pltpu.make_async_remote_copy(
            source,
            target,
            sent,
            received,
            device_id=device,
            device_id_type=MESH,
        )

    def strip_at(step):
        spread = (step // 2 * 27) % 64
        sign = 1 - 2 * core
        return strip_of(
            (x + 4 + sign * (spread % 4)) % 4,
            (y + 4 + sign * ((spread // 4) % 4)) % 4,
            (z + 4 + sign * (spread // 16)) % 4,
            (core + step) % 2,
        )

    def send_blocks(panel, group, first, last):
        def body(step, carry):
            strip = strip_at(step)
            remote(
                listed_ref.at[panel, :, listed(strip), :],
                blocks_refs[panel].at[step],
                block_send_sem.at[panel],
                block_recv_sem.at[panel, group],
                (strip // 4, strip % 4),
            ).start()
            return carry

        lax.fori_loop(first, last, body, 0)

    def send_ids(step, carry):
        strip = strip_at(step)
        remote(ids_ref, all_ids_ref.at[step], id_sem.at[0], id_sem.at[1], (strip // 4, strip % 4)).start()
        return carry

    def await_bytes(some, sem):
        pltpu.make_async_copy(some, some, sem).wait()

    fetch_store[0].wait()
    send_blocks(0, 0, 1, 24)
    lax.fori_loop(1, 128, send_ids, 0)
    send_blocks(0, 0, 24, 64)
    fetch_store[1].wait()
    for panel in range(2):
        for group, (first, count) in enumerate(GROUPS[panel]):
            if panel + group > 0:
                send_blocks(panel, group, max(first, 1), first + count)

    for copy in own_copies:
        copy.wait()
    await_bytes(all_ids_ref.at[pl.ds(1, 127)], id_sem.at[1])
    down = lax.broadcasted_iota(jnp.int32, (128, 128), 0)
    lane = lax.broadcasted_iota(jnp.int32, (128, 128), 1)
    order_ref[...] = jnp.zeros_like(order_ref)
    places = []
    for panel in range(2):
        own = jnp.sum(jnp.where(lane == me, all_ids_ref[:, panel, :], 0), axis=1, keepdims=True) % 128
        places.append(jnp.sum(jnp.where(down == lane, own, 0), axis=0, keepdims=True))
        order_ref[panel : panel + 1, :] = places[panel]
        order_ref[panel + 3 : panel + 4, :] = jnp.max(jnp.where(own == lane, down, 0), axis=0, keepdims=True)
    slot_of_place = jnp.max(jnp.where(places[0] == down, lane, 0), axis=1, keepdims=True)
    order_ref[2:3, :] = jnp.max(jnp.where(places[1] == down, slot_of_place, 0), axis=0, keepdims=True)
    fetch_order = pltpu.make_async_copy(order_ref, slot_ref, local_sem.at[4])
    fetch_order.start()
    fetch_order.wait()
    fetch_vectors.wait()

    def take_group(panel, group, begin_tile):
        first, count = GROUPS[panel][group]
        size = count * 8
        start = first * 8
        begin = first == 0
        values = panel_refs[panel]
        kept = first if panel == 0 else 0

        await_bytes(
            blocks_refs[panel].at[pl.ds(max(first, 1), first + count - max(first, 1))], block_recv_sem.at[panel, group]
        )

        def take_block(step, carry):
            slot = first + step
            place = slot_ref[panel, slot]
            near = pl.ds(pl.multiple_of(step * 8, 8), 8)
            row_index = me * 1024 + place * 8 + lax.broadcasted_iota(jnp.int32, (8, 256), 0)
            limit = offsets_ref[panel] + lax.broadcasted_iota(jnp.int32, (8, 256), 1)
            below = row_index > limit
            diagonal = jnp.where(row_index == limit, 1.0, 0.0)
            values[0, kept + step] = jnp.where(below, blocks_refs[panel][slot, 0], diagonal)
            values[1, kept + step] = jnp.where(below, blocks_refs[panel][slot, 1], 0.0)
            for part in range(2):
                wanted = z_ref[part, place]
                for chunk in range(4):
                    at = pl.ds(pl.multiple_of(chunk % 2 * 512 + step * 8, 8), 8)
                    rows_ref[chunk // 2, part, at, :] = wanted[:, chunk * 256 : (chunk + 1) * 256]
            if panel == 1:
                matching = slot_ref[2, slot]
                match_ref[0, near, :] = first_panel_ref[0, matching]
                match_ref[1, near, :] = first_panel_ref[1, matching]
            return carry

        lax.fori_loop(0, count, take_block, 0, unroll=4)

        own = [values[part, kept : kept + count].reshape(size, 256) for part in range(2)]
        forms = left_forms(own[0].T, -own[1].T)
        for form in range(3):
            adjoint_ref[form, :, 0 : 3 * size] = forms[form]

        def adjoint_products(right):
            return complex_dot([adjoint_ref[form, :, 0 : 3 * size] for form in range(3)], right)

        def add_tile(tile, parts):
            for part in range(2):
                for side in range(2):
                    value = parts[part][:, side * 128 : (side + 1) * 128]
                    start = side * 512 + part * 256
                    target = part_ref.at[tile, start : start + 256, :]
                    if begin:
                        target[...] = value
                    else:
                        target[...] += value

        if panel == 1:
            matched = (match_ref[0, 0:size, :], match_ref[1, 0:size, :])
            add_tile(TILES - 1, adjoint_products(right_forms(*matched)))
            if begin_tile is not None:
                begin_tile(TILES - 1)

        def take_columns(chunk, carry):
            at = pl.ds(pl.multiple_of(chunk % 2 * 512, 512), size)
            right = right_forms(rows_ref[chunk // 2, 0, at, :], rows_ref[chunk // 2, 1, at, :])
            add_tile(2 * chunk + panel, adjoint_products(right))
            return carry

        if begin_tile is None:
            lax.fori_loop(0, 4, take_columns, 0)
        else:
            for chunk in range(4):
                take_columns(chunk, 0)
                begin_tile(2 * chunk + panel)

        if panel == 1:
            for which, source in enumerate((matched, own)):
                scaled = complex_dot(left_forms(*source), [factor_ref[which, form] for form in range(3)])
                for part in range(2):
                    x_ref[part, start : start + size, which * 256 : (which + 1) * 256] = scaled[part]

    def device(place, core):
        strip = strip_of(*place, core)
        return (strip // 4, strip % 4)

    sibling = device(here, 1 - core)
    other = [place + 1 - 2 * (place % 2) for place in here] + [3 - place for place in here]
    bits = [((place + 1) // 2) % 2 for place in here] + [place // 2 for place in here]

    def across(links):
        place = list(here)
        for link in links:
            place[link % 3] = other[link]
        return device(place, core)

    def rows_at(first, count):
        return pl.ds(pl.multiple_of(first, 8), count)

    def send(tile, stage, source, target, peer):
        remote(source, target, send_sem.at[tile, stage], recv_sem.at[tile, stage], peer).start()

    def wait(tile, stage, sem):
        some = landed_ref.at[tile, pl.ds(0, COUNTS[level_of(stage)]), :]
        pltpu.make_async_copy(some, some, sem.at[tile, stage]).wait()

    def links_of(tile, level):
        return [(FIRST_LINKS[tile] + link) % 6 for link in LINKS[level]]

    def share(tile, level, flips=0):
        index = 0
        for place, link in enumerate(links_of(tile, level)):
            index = index * 2 + (1 - bits[link] if flips >> place & 1 else bits[link])
        return index

    def flipped(tile, level, flips):
        return across([link for place, link in enumerate(links_of(tile, level)) if flips >> place & 1])

    lows = [0] * TILES

    def split_rows(tile, level):
        held = held_ref.at[tile]
        size = SIZES[level + 1]
        for flips in range(1, 2 ** len(LINKS[level])):
            send(
                tile,
                level,
                held.at[rows_at(lows[tile] + share(tile, level, flips) * size, size), :],
                landed_ref.at[tile, pl.ds(BASES[level] + (flips - 1) * size, size), :],
                flipped(tile, level, flips),
            )
        lows[tile] = lows[tile] + share(tile, level) * size

    def return_rows(tile, level):
        size = SIZES[level + 1]
        place = total_ref.at[tile, rows_at(core * 512 + lows[tile], size), :]
        for flips in range(1, 2 ** len(LINKS[level])):
            send(tile, STAGES - 1 - level, place, place, flipped(tile, level, flips))

    def advance(tile, stage):
        level = level_of(stage)
        held = held_ref.at[tile]
        wait(tile, stage, recv_sem)
        if stage == 0:
            held[...] = part_ref[tile, rows_at(core * 512, 512), :] + landed_ref[tile, 0:512, :]
            split_rows(tile, 1)
        elif stage < HALF_STAGES:
            size = SIZES[level + 1]
            value = held[rows_at(lows[tile], size), :]
            for piece in range(2 ** len(LINKS[level]) - 1):
                start = BASES[level] + piece * size
                value += landed_ref[tile, start : start + size, :]
            if stage < HALF_STAGES - 1:
                held[rows_at(lows[tile], size), :] = value
                split_rows(tile, level + 1)
            else:
                total_ref[tile, rows_at(core * 512 + lows[tile], size), :] = value
                return_rows(tile, level)
        elif stage < STAGES - 1:
            lows[tile] = lows[tile] - share(tile, level) * SIZES[level + 1]
            if level > 1:
                return_rows(tile, level - 1)
            else:
                place = total_ref.at[tile, rows_at(core * 512, 512), :]
                send(tile, STAGES - 1, place, place, sibling)

    def parts(tile):
        values = total_ref[tile]
        real_part = jnp.concatenate([values[0:256], values[512:768]], axis=1)
        imag_part = jnp.concatenate([values[256:512], values[768:1024]], axis=1)
        return real_part, imag_part

    def correct(piece):
        if piece == 0:
            cross = complex_dot(left_forms(*parts(TILES - 1)), right_forms(*adjoint_upper(tri_ref, 0)))
            cross = right_forms(*cross)
            for form in range(3):
                factor_ref[0, form] = cross[form]
        rows = slice(piece * 256, (piece + 1) * 256)
        second = left_forms(x_ref[0, rows, 256:512], x_ref[1, rows, 256:512])
        real_part, imag_part = complex_dot(second, [factor_ref[0, form] for form in range(3)])
        first = left_forms(x_ref[0, rows, 0:256] - real_part, x_ref[1, rows, 0:256] - imag_part)
        for form in range(3):
            for part in range(2):
                source = slice((part + 1) * 256, (part + 2) * 256)
                start = part * 512
                left_ref[form, rows, start : start + 256] = first[form][:, source]
                left_ref[form, rows, start + 256 : start + 512] = second[form][:, source]

    written = []

    def apply(chunk, piece):
        if piece == 0:
            first = parts(2 * chunk)
            second = parts(2 * chunk + 1)
            forms = right_forms(*[jnp.concatenate([first[part], second[part]], axis=0) for part in range(2)])
            for form in range(3):
                right_ref[form, 0:512, :] = forms[form][512:1024]
                right_ref[form, 512:1024, :] = forms[form][0:512]
                right_ref[form, 1024:1536, :] = forms[form][0:512]
        rows = slice(piece * 256, (piece + 1) * 256)
        sums = [
            dot(left_ref[form, rows, 0:512], right_ref[form, 0:512, :])
            + dot(left_ref[form, rows, :], right_ref[form, 512:1536, :])
            for form in range(3)
        ]
        change = (sums[0] - sums[2], sums[0] + sums[1])
        for part in range(2):
            first_blocks_ref[piece * 32 : (piece + 1) * 32, part] = change[part].reshape(32, 8, 256)
        if piece < 3:
            return
        if len(written) > 1:
            written[-2].wait()
        columns = slice(chunk * 256, (chunk + 1) * 256)
        result = rows_ref.at[len(written) % 2]

        def put_block(block, carry):
            slot = slot_ref[4, block]
            rows = pl.ds(pl.multiple_of(block * 8, 8), 8)
            for part in range(2):
                result[part, rows, :] = z_ref[part, block, :, columns] - first_blocks_ref[slot, part]
            return carry

        lax.fori_loop(0, 128, put_block, 0, unroll=8)
        copy = pltpu.make_async_copy(result, out_ref.at[:, :, columns], local_sem.at[5 + len(written)])
        copy.start()
        written.append(copy)

    def begin(tile):
        send(
            tile,
            0,
            part_ref.at[tile, rows_at((1 - core) * 512, 512), :],
            landed_ref.at[tile, pl.ds(0, 512), :],
            sibling,
        )

    for panel in range(2):
        for group in range(len(GROUPS[panel])):
            take_group(panel, group, begin if group == len(GROUPS[panel]) - 1 else None)
    for tile, step in step_order():
        if tile is None:
            correct(step)
        elif tile < 0:
            apply(-1 - tile, step)
        else:
            advance(tile, step)
    await_bytes(all_ids_ref.at[pl.ds(0, 127)], id_sem.at[0])
    for panel in range(2):
        await_bytes(blocks_refs[panel].at[pl.ds(0, 127)], block_send_sem.at[panel])
    for tile in range(TILES):
        for stage in range(STAGES):
            wait(tile, stage, send_sem)
    for copy in written[-2:]:
        copy.wait()


def move_kernel(source_ref, target_ref, held_ref, in_sem, out_sem):
    into = []
    out_of = []
    for piece in range(16):
        place = (piece // 8, pl.ds(piece % 8 * 128, 128))
        into.append(pltpu.make_async_copy(source_ref.at[place], held_ref.at[place], in_sem.at[piece]))
        out_of.append(pltpu.make_async_copy(held_ref.at[place], target_ref.at[place], out_sem.at[piece]))
    for copy in into:
        copy.start()
    for arriving, leaving in zip(into, out_of):
        arriving.wait()
        leaving.start()
    for copy in out_of:
        copy.wait()


def per_device(vectors, panel_store, block_ids, offsets, tri_factors):
    f32 = jnp.float32
    bf16 = jnp.bfloat16
    whole = pl.BlockSpec(memory_space=pltpu.VMEM)
    anywhere = pl.BlockSpec(memory_space=pl.ANY)
    dma = pltpu.SemaphoreType.DMA
    result = pl.pallas_call(
        main_kernel,
        out_shape=jax.ShapeDtypeStruct(vectors.shape, f32),
        in_specs=[pl.BlockSpec(memory_space=pltpu.SMEM), whole, anywhere, whole, anywhere],
        out_specs=anywhere,
        scratch_shapes=[
            pltpu.VMEM((2, 2, 1024, 256), f32),
            pltpu.VMEM((2, 128, 8, 1024), f32),
            pltpu.VMEM((128, 2, 8, 256), f32),
            pltpu.VMEM((128, 2, 8, 256), f32),
            pltpu.VMEM((128, 2, 128), jnp.int32),
            pltpu.VMEM((8, 128), jnp.int32),
            pltpu.SMEM((8, 128), jnp.int32),
            pltpu.VMEM((2, 128, 8, 256), f32),
            pltpu.VMEM((2, 32, 8, 256), f32),
            pltpu.VMEM((2, 2, 1024, 256), f32),
            pltpu.VMEM((2, 256, 256), f32),
            pltpu.VMEM((3, 256, 1536), bf16),
            pltpu.VMEM((2, 3, 768, 256), bf16),
            pltpu.VMEM((TILES, 1024, 128), f32),
            pltpu.VMEM((2, 1024, 512), f32),
            pltpu.VMEM((TILES, 1024, 128), f32),
            pltpu.VMEM((TILES, 512, 128), f32),
            pltpu.VMEM((TILES, 1024, 128), f32),
            pltpu.VMEM((3, 1024, 1024), bf16),
            pltpu.VMEM((3, 1536, 256), bf16),
            dma((2,)),
            dma((2, 5)),
            dma((2,)),
            dma((TILES, STAGES)),
            dma((TILES, STAGES)),
            dma((11,)),
        ],
        compiler_params=pltpu.CompilerParams(
            vmem_limit_bytes=VMEM_LIMIT, collective_id=0, has_side_effects=True
        ),
        name="main",
    )(offsets, block_ids, panel_store, tri_factors, vectors.reshape(2, 128, 8, 1024))
    return pl.pallas_call(
        move_kernel,
        out_shape=jax.ShapeDtypeStruct(vectors.shape, f32),
        in_specs=[anywhere],
        out_specs=anywhere,
        scratch_shapes=[pltpu.VMEM(vectors.shape, f32), dma((16,)), dma((16,))],
        compiler_params=pltpu.CompilerParams(vmem_limit_bytes=VMEM_LIMIT),
        name="move",
    )(result)


def solution(mesh):
    placed = (
        P(None, ("row", "col"), None),
        P(None, None, ("row", "col"), None),
        P(None, ("row", "col")),
        P(),
        P(),
    )
    return jax.shard_map(
        per_device,
        mesh=mesh,
        in_specs=placed,
        out_specs=P(None, ("row", "col"), None),
        check_vma=False,
    )
```

```python
import jax
import jax.numpy as jnp
from jax import lax
from jax.experimental import pallas as pl
from jax.experimental.pallas import tpu as pltpu
from jax.sharding import PartitionSpec as P


MESH = pl.DeviceIdType.MESH


def strip_of(x, y, z, core):
    return ((x * 2 + z % 2) * 4 + y) * 4 + (z // 2) * 2 + core


VMEM_LIMIT = 60 * 1024 * 1024


def split(value):
    high = value.astype(jnp.bfloat16)
    return high, (value - high.astype(jnp.float32)).astype(jnp.bfloat16)


def dot(first_op, second_op):
    return jnp.dot(first_op, second_op, preferred_element_type=jnp.float32)


def left_pieces(value):
    high, low = split(value)
    return jnp.concatenate([high, high, low], axis=1)


def right_pieces(value):
    high, low = split(value)
    return jnp.concatenate([high, low, high], axis=0)


def left_forms(real_part, imag_part):
    return left_pieces(real_part + imag_part), left_pieces(real_part), left_pieces(imag_part)


def right_forms(real_part, imag_part):
    return right_pieces(real_part), right_pieces(imag_part - real_part), right_pieces(real_part + imag_part)


def complex_dot(left, right):
    shared = dot(left[0], right[0])
    return shared - dot(left[2], right[2]), shared + dot(left[1], right[1])


def adjoint_upper(tri_ref, panel):
    shape = tri_ref.shape[2:]
    upper = lax.broadcasted_iota(jnp.int32, shape, 0) <= lax.broadcasted_iota(jnp.int32, shape, 1)
    return jnp.where(upper, tri_ref[panel, 0], 0.0).T, -jnp.where(upper, tri_ref[panel, 1], 0.0).T


GROUPS = (
    ((0, 64), (64, 64)),
    ((0, 32), (32, 32), (64, 32), (96, 16), (112, 16)),
)


TILES = 9
LINKS = ((), (0, 1), (2, 3), (4, 5))
FIRST_LINKS = (3, 4, 2, 2, 5, 0, 4, 3, 0)
APART = 2.5
HALF_STAGES = len(LINKS)
STAGES = 2 * HALF_STAGES
SIZES = [1024, 512, 128, 32, 8]
COUNTS = [SIZES[stage] - SIZES[stage + 1] for stage in range(HALF_STAGES)]
BASES = [sum(COUNTS[:stage]) for stage in range(HALF_STAGES)]


def level_of(stage):
    return stage if stage < HALF_STAGES else STAGES - 1 - stage


def step_order():
    free = [0.0] * 7
    now = 0.0
    ready = []
    order = []
    work = []
    finished = set()
    queued = set()

    def send(tile, stage):
        nonlocal now
        level = level_of(stage)
        now += 0.06 * (2 ** len(LINKS[level]) - 1 if level else 1)
        if level == 0:
            free[6] = max(free[6], now) + 512 * 0.512 / 600
            arrival = free[6]
        else:
            arrival = now
            for link in LINKS[level]:
                link = (FIRST_LINKS[tile] + link) % 6
                free[link] = max(free[link], now) + SIZES[level] / 2 * 0.512 / 50
                arrival = max(arrival, free[link])
        if stage == 0 and tile < TILES - 1:
            arrival = max(arrival, tile // 2 * APART + 0.5)
        ready.append((arrival + 2.5, tile, stage))

    for tile in range(0, TILES - 1, 2):
        ready.append((tile // 2 * APART, tile, 0))
    for tile in [TILES - 1] + list(range(1, TILES - 1, 2)):
        now += 0.5
        send(tile, 0)
    while ready or work:
        ready.sort()
        if ready and (ready[0][0] <= now or not work):
            arrival, tile, stage = ready.pop(0)
            order.append((tile, stage))
            now = max(now, arrival) + (0.05 + COUNTS[stage] * 0.0006 if stage < HALF_STAGES else 0.03)
            if stage < STAGES - 1:
                send(tile, stage + 1)
            else:
                finished.add(tile)
            if TILES - 1 in finished:
                if None not in queued:
                    queued.add(None)
                    work += [(None, piece) for piece in range(4)]
                for chunk in range(4):
                    if chunk not in queued and {2 * chunk, 2 * chunk + 1} <= finished:
                        queued.add(chunk)
                        work += [(-1 - chunk, piece) for piece in range(4)]
        else:
            order.append(work.pop(0))
            now += 0.8
    return order


def main_kernel(
    offsets_ref,
    ids_ref,
    store_ref,
    tri_ref,
    vectors_ref,
    out_ref,
    listed_ref,
    z_ref,
    first_blocks_ref,
    second_blocks_ref,
    all_ids_ref,
    order_ref,
    slot_ref,
    first_panel_ref,
    second_panel_ref,
    rows_ref,
    match_ref,
    adjoint_ref,
    factor_ref,
    part_ref,
    x_ref,
    total_ref,
    held_ref,
    landed_ref,
    left_ref,
    right_ref,
    block_send_sem,
    block_recv_sem,
    id_sem,
    send_sem,
    recv_sem,
    local_sem,
):
    blocks_refs = (first_blocks_ref, second_blocks_ref)
    panel_refs = (first_panel_ref, second_panel_ref)
    row = lax.axis_index("row")
    col = lax.axis_index("col")
    me = row * 4 + col
    x = row // 8
    y = row % 4
    z = (col // 2) * 2 + (row // 4) % 2
    here = (x, y, z)
    core = col % 2

    barrier = pltpu.get_barrier_semaphore()

    def greet(step, carry):
        peer = (me + step) % 128
        pl.semaphore_signal(barrier, inc=1, device_id=(peer // 4, peer % 4), device_id_type=MESH)
        return carry

    lax.fori_loop(1, 128, greet, 0)

    def listed(strip):
        return pl.ds(pl.multiple_of(strip * 8, 8), 8)

    own_copies = [
        pltpu.make_async_copy(store_ref.at[panel, :, listed(me), :], blocks_refs[panel].at[0], local_sem.at[panel])
        for panel in range(2)
    ]
    own_copies.append(pltpu.make_async_copy(ids_ref, all_ids_ref.at[0], local_sem.at[2]))
    fetch_store = [
        pltpu.make_async_copy(store_ref.at[panel], listed_ref.at[panel], local_sem.at[9 + panel]) for panel in range(2)
    ]
    fetch_store[0].start()
    fetch_store[1].start()
    for copy in own_copies:
        copy.start()
    fetch_vectors = pltpu.make_async_copy(vectors_ref, z_ref, local_sem.at[3])
    fetch_vectors.start()

    for panel in range(2):
        forms = right_forms(*adjoint_upper(tri_ref, panel))
        for form in range(3):
            factor_ref[panel, form] = forms[form]

    pl.semaphore_wait(barrier, 127)

    def remote(source, target, sent, received, device):
        return pltpu.make_async_remote_copy(
            source,
            target,
            sent,
            received,
            device_id=device,
            device_id_type=MESH,
        )

    def strip_at(step):
        spread = (step // 2 * 21) % 64
        return strip_of(
            (x + spread % 4) % 4, (y + (spread // 4) % 4) % 4, (z + spread // 16) % 4, (core + step) % 2
        )

    def send_blocks(panel, group, first, last):
        def body(step, carry):
            strip = strip_at(step)
            remote(
                listed_ref.at[panel, :, listed(strip), :],
                blocks_refs[panel].at[step],
                block_send_sem.at[panel],
                block_recv_sem.at[panel, group],
                (strip // 4, strip % 4),
            ).start()
            return carry

        lax.fori_loop(first, last, body, 0)

    def send_ids(step, carry):
        strip = strip_at(step)
        remote(ids_ref, all_ids_ref.at[step], id_sem.at[0], id_sem.at[1], (strip // 4, strip % 4)).start()
        return carry

    def await_bytes(some, sem):
        pltpu.make_async_copy(some, some, sem).wait()

    fetch_store[0].wait()
    send_blocks(0, 0, 1, 24)
    lax.fori_loop(1, 128, send_ids, 0)
    send_blocks(0, 0, 24, 64)
    fetch_store[1].wait()
    for panel in range(2):
        for group, (first, count) in enumerate(GROUPS[panel]):
            if panel + group > 0:
                send_blocks(panel, group, max(first, 1), first + count)

    for copy in own_copies:
        copy.wait()
    await_bytes(all_ids_ref.at[pl.ds(1, 127)], id_sem.at[1])
    down = lax.broadcasted_iota(jnp.int32, (128, 128), 0)
    lane = lax.broadcasted_iota(jnp.int32, (128, 128), 1)
    order_ref[...] = jnp.zeros_like(order_ref)
    places = []
    for panel in range(2):
        own = jnp.sum(jnp.where(lane == me, all_ids_ref[:, panel, :], 0), axis=1, keepdims=True) % 128
        places.append(jnp.sum(jnp.where(down == lane, own, 0), axis=0, keepdims=True))
        order_ref[panel : panel + 1, :] = places[panel]
        order_ref[panel + 3 : panel + 4, :] = jnp.max(jnp.where(own == lane, down, 0), axis=0, keepdims=True)
    slot_of_place = jnp.max(jnp.where(places[0] == down, lane, 0), axis=1, keepdims=True)
    order_ref[2:3, :] = jnp.max(jnp.where(places[1] == down, slot_of_place, 0), axis=0, keepdims=True)
    fetch_order = pltpu.make_async_copy(order_ref, slot_ref, local_sem.at[4])
    fetch_order.start()
    fetch_order.wait()
    fetch_vectors.wait()

    def take_group(panel, group, begin_tile):
        first, count = GROUPS[panel][group]
        size = count * 8
        start = first * 8
        begin = first == 0
        values = panel_refs[panel]
        kept = first if panel == 0 else 0

        await_bytes(
            blocks_refs[panel].at[pl.ds(max(first, 1), first + count - max(first, 1))], block_recv_sem.at[panel, group]
        )

        def take_block(step, carry):
            slot = first + step
            place = slot_ref[panel, slot]
            near = pl.ds(pl.multiple_of(step * 8, 8), 8)
            row_index = me * 1024 + place * 8 + lax.broadcasted_iota(jnp.int32, (8, 256), 0)
            limit = offsets_ref[panel] + lax.broadcasted_iota(jnp.int32, (8, 256), 1)
            below = row_index > limit
            diagonal = jnp.where(row_index == limit, 1.0, 0.0)
            values[0, kept + step] = jnp.where(below, blocks_refs[panel][slot, 0], diagonal)
            values[1, kept + step] = jnp.where(below, blocks_refs[panel][slot, 1], 0.0)
            for part in range(2):
                wanted = z_ref[part, place]
                for chunk in range(4):
                    at = pl.ds(pl.multiple_of(chunk % 2 * 512 + step * 8, 8), 8)
                    rows_ref[chunk // 2, part, at, :] = wanted[:, chunk * 256 : (chunk + 1) * 256]
            if panel == 1:
                matching = slot_ref[2, slot]
                match_ref[0, near, :] = first_panel_ref[0, matching]
                match_ref[1, near, :] = first_panel_ref[1, matching]
            return carry

        lax.fori_loop(0, count, take_block, 0, unroll=4)

        own = [values[part, kept : kept + count].reshape(size, 256) for part in range(2)]
        forms = left_forms(own[0].T, -own[1].T)
        for form in range(3):
            adjoint_ref[form, :, 0 : 3 * size] = forms[form]

        def adjoint_products(right):
            return complex_dot([adjoint_ref[form, :, 0 : 3 * size] for form in range(3)], right)

        def add_tile(tile, parts):
            for part in range(2):
                for side in range(2):
                    value = parts[part][:, side * 128 : (side + 1) * 128]
                    start = side * 512 + part * 256
                    target = part_ref.at[tile, start : start + 256, :]
                    if begin:
                        target[...] = value
                    else:
                        target[...] += value

        if panel == 1:
            matched = (match_ref[0, 0:size, :], match_ref[1, 0:size, :])
            add_tile(TILES - 1, adjoint_products(right_forms(*matched)))
            if begin_tile is not None:
                begin_tile(TILES - 1)

        def take_columns(chunk, carry):
            at = pl.ds(pl.multiple_of(chunk % 2 * 512, 512), size)
            right = right_forms(rows_ref[chunk // 2, 0, at, :], rows_ref[chunk // 2, 1, at, :])
            add_tile(2 * chunk + panel, adjoint_products(right))
            return carry

        if begin_tile is None:
            lax.fori_loop(0, 4, take_columns, 0)
        else:
            for chunk in range(4):
                take_columns(chunk, 0)
                begin_tile(2 * chunk + panel)

        if panel == 1:
            for which, source in enumerate((matched, own)):
                scaled = complex_dot(left_forms(*source), [factor_ref[which, form] for form in range(3)])
                for part in range(2):
                    x_ref[part, start : start + size, which * 256 : (which + 1) * 256] = scaled[part]

    def device(place, core):
        strip = strip_of(*place, core)
        return (strip // 4, strip % 4)

    sibling = device(here, 1 - core)
    other = [place + 1 - 2 * (place % 2) for place in here] + [3 - place for place in here]
    bits = [((place + 1) // 2) % 2 for place in here] + [place // 2 for place in here]

    def across(links):
        place = list(here)
        for link in links:
            place[link % 3] = other[link]
        return device(place, core)

    def rows_at(first, count):
        return pl.ds(pl.multiple_of(first, 8), count)

    def send(tile, stage, source, target, peer):
        remote(source, target, send_sem.at[tile, stage], recv_sem.at[tile, stage], peer).start()

    def wait(tile, stage, sem):
        some = landed_ref.at[tile, pl.ds(0, COUNTS[level_of(stage)]), :]
        pltpu.make_async_copy(some, some, sem.at[tile, stage]).wait()

    def links_of(tile, level):
        return [(FIRST_LINKS[tile] + link) % 6 for link in LINKS[level]]

    def share(tile, level, flips=0):
        index = 0
        for place, link in enumerate(links_of(tile, level)):
            index = index * 2 + (1 - bits[link] if flips >> place & 1 else bits[link])
        return index

    def flipped(tile, level, flips):
        return across([link for place, link in enumerate(links_of(tile, level)) if flips >> place & 1])

    lows = [0] * TILES

    def split_rows(tile, level):
        held = held_ref.at[tile]
        size = SIZES[level + 1]
        for flips in range(1, 2 ** len(LINKS[level])):
            send(
                tile,
                level,
                held.at[rows_at(lows[tile] + share(tile, level, flips) * size, size), :],
                landed_ref.at[tile, pl.ds(BASES[level] + (flips - 1) * size, size), :],
                flipped(tile, level, flips),
            )
        lows[tile] = lows[tile] + share(tile, level) * size

    def return_rows(tile, level):
        size = SIZES[level + 1]
        place = total_ref.at[tile, rows_at(core * 512 + lows[tile], size), :]
        for flips in range(1, 2 ** len(LINKS[level])):
            send(tile, STAGES - 1 - level, place, place, flipped(tile, level, flips))

    def advance(tile, stage):
        level = level_of(stage)
        held = held_ref.at[tile]
        wait(tile, stage, recv_sem)
        if stage == 0:
            held[...] = part_ref[tile, rows_at(core * 512, 512), :] + landed_ref[tile, 0:512, :]
            split_rows(tile, 1)
        elif stage < HALF_STAGES:
            size = SIZES[level + 1]
            value = held[rows_at(lows[tile], size), :]
            for piece in range(2 ** len(LINKS[level]) - 1):
                start = BASES[level] + piece * size
                value += landed_ref[tile, start : start + size, :]
            if stage < HALF_STAGES - 1:
                held[rows_at(lows[tile], size), :] = value
                split_rows(tile, level + 1)
            else:
                total_ref[tile, rows_at(core * 512 + lows[tile], size), :] = value
                return_rows(tile, level)
        elif stage < STAGES - 1:
            lows[tile] = lows[tile] - share(tile, level) * SIZES[level + 1]
            if level > 1:
                return_rows(tile, level - 1)
            else:
                place = total_ref.at[tile, rows_at(core * 512, 512), :]
                send(tile, STAGES - 1, place, place, sibling)

    def parts(tile):
        values = total_ref[tile]
        real_part = jnp.concatenate([values[0:256], values[512:768]], axis=1)
        imag_part = jnp.concatenate([values[256:512], values[768:1024]], axis=1)
        return real_part, imag_part

    def correct(piece):
        if piece == 0:
            cross = complex_dot(left_forms(*parts(TILES - 1)), right_forms(*adjoint_upper(tri_ref, 0)))
            cross = right_forms(*cross)
            for form in range(3):
                factor_ref[0, form] = cross[form]
        rows = slice(piece * 256, (piece + 1) * 256)
        second = left_forms(x_ref[0, rows, 256:512], x_ref[1, rows, 256:512])
        real_part, imag_part = complex_dot(second, [factor_ref[0, form] for form in range(3)])
        first = left_forms(x_ref[0, rows, 0:256] - real_part, x_ref[1, rows, 0:256] - imag_part)
        for form in range(3):
            for part in range(2):
                source = slice((part + 1) * 256, (part + 2) * 256)
                start = part * 512
                left_ref[form, rows, start : start + 256] = first[form][:, source]
                left_ref[form, rows, start + 256 : start + 512] = second[form][:, source]

    written = []

    def apply(chunk, piece):
        if piece == 0:
            first = parts(2 * chunk)
            second = parts(2 * chunk + 1)
            forms = right_forms(*[jnp.concatenate([first[part], second[part]], axis=0) for part in range(2)])
            for form in range(3):
                right_ref[form, 0:512, :] = forms[form][512:1024]
                right_ref[form, 512:1024, :] = forms[form][0:512]
                right_ref[form, 1024:1536, :] = forms[form][0:512]
        rows = slice(piece * 256, (piece + 1) * 256)
        sums = [
            dot(left_ref[form, rows, 0:512], right_ref[form, 0:512, :])
            + dot(left_ref[form, rows, :], right_ref[form, 512:1536, :])
            for form in range(3)
        ]
        change = (sums[0] - sums[2], sums[0] + sums[1])
        for part in range(2):
            first_blocks_ref[piece * 32 : (piece + 1) * 32, part] = change[part].reshape(32, 8, 256)
        if piece < 3:
            return
        if len(written) > 1:
            written[-2].wait()
        columns = slice(chunk * 256, (chunk + 1) * 256)
        result = rows_ref.at[len(written) % 2]

        def put_block(block, carry):
            slot = slot_ref[4, block]
            rows = pl.ds(pl.multiple_of(block * 8, 8), 8)
            for part in range(2):
                result[part, rows, :] = z_ref[part, block, :, columns] - first_blocks_ref[slot, part]
            return carry

        lax.fori_loop(0, 128, put_block, 0, unroll=8)
        copy = pltpu.make_async_copy(result, out_ref.at[:, :, columns], local_sem.at[5 + len(written)])
        copy.start()
        written.append(copy)

    def begin(tile):
        send(
            tile,
            0,
            part_ref.at[tile, rows_at((1 - core) * 512, 512), :],
            landed_ref.at[tile, pl.ds(0, 512), :],
            sibling,
        )

    for panel in range(2):
        for group in range(len(GROUPS[panel])):
            take_group(panel, group, begin if group == len(GROUPS[panel]) - 1 else None)
    for tile, step in step_order():
        if tile is None:
            correct(step)
        elif tile < 0:
            apply(-1 - tile, step)
        else:
            advance(tile, step)
    await_bytes(all_ids_ref.at[pl.ds(0, 127)], id_sem.at[0])
    for panel in range(2):
        await_bytes(blocks_refs[panel].at[pl.ds(0, 127)], block_send_sem.at[panel])
    for tile in range(TILES):
        for stage in range(STAGES):
            wait(tile, stage, send_sem)
    for copy in written[-2:]:
        copy.wait()


def move_kernel(source_ref, target_ref, held_ref, in_sem, out_sem):
    into = []
    out_of = []
    for piece in range(16):
        place = (piece // 8, pl.ds(piece % 8 * 128, 128))
        into.append(pltpu.make_async_copy(source_ref.at[place], held_ref.at[place], in_sem.at[piece]))
        out_of.append(pltpu.make_async_copy(held_ref.at[place], target_ref.at[place], out_sem.at[piece]))
    for copy in into:
        copy.start()
    for arriving, leaving in zip(into, out_of):
        arriving.wait()
        leaving.start()
    for copy in out_of:
        copy.wait()


def per_device(vectors, panel_store, block_ids, offsets, tri_factors):
    f32 = jnp.float32
    bf16 = jnp.bfloat16
    whole = pl.BlockSpec(memory_space=pltpu.VMEM)
    anywhere = pl.BlockSpec(memory_space=pl.ANY)
    dma = pltpu.SemaphoreType.DMA
    result = pl.pallas_call(
        main_kernel,
        out_shape=jax.ShapeDtypeStruct(vectors.shape, f32),
        in_specs=[pl.BlockSpec(memory_space=pltpu.SMEM), whole, anywhere, whole, anywhere],
        out_specs=anywhere,
        scratch_shapes=[
            pltpu.VMEM((2, 2, 1024, 256), f32),
            pltpu.VMEM((2, 128, 8, 1024), f32),
            pltpu.VMEM((128, 2, 8, 256), f32),
            pltpu.VMEM((128, 2, 8, 256), f32),
            pltpu.VMEM((128, 2, 128), jnp.int32),
            pltpu.VMEM((8, 128), jnp.int32),
            pltpu.SMEM((8, 128), jnp.int32),
            pltpu.VMEM((2, 128, 8, 256), f32),
            pltpu.VMEM((2, 32, 8, 256), f32),
            pltpu.VMEM((2, 2, 1024, 256), f32),
            pltpu.VMEM((2, 256, 256), f32),
            pltpu.VMEM((3, 256, 1536), bf16),
            pltpu.VMEM((2, 3, 768, 256), bf16),
            pltpu.VMEM((TILES, 1024, 128), f32),
            pltpu.VMEM((2, 1024, 512), f32),
            pltpu.VMEM((TILES, 1024, 128), f32),
            pltpu.VMEM((TILES, 512, 128), f32),
            pltpu.VMEM((TILES, 1024, 128), f32),
            pltpu.VMEM((3, 1024, 1024), bf16),
            pltpu.VMEM((3, 1536, 256), bf16),
            dma((2,)),
            dma((2, 5)),
            dma((2,)),
            dma((TILES, STAGES)),
            dma((TILES, STAGES)),
            dma((11,)),
        ],
        compiler_params=pltpu.CompilerParams(
            vmem_limit_bytes=VMEM_LIMIT, collective_id=0, has_side_effects=True
        ),
        name="main",
    )(offsets, block_ids, panel_store, tri_factors, vectors.reshape(2, 128, 8, 1024))
    return pl.pallas_call(
        move_kernel,
        out_shape=jax.ShapeDtypeStruct(vectors.shape, f32),
        in_specs=[anywhere],
        out_specs=anywhere,
        scratch_shapes=[pltpu.VMEM(vectors.shape, f32), dma((16,)), dma((16,))],
        compiler_params=pltpu.CompilerParams(vmem_limit_bytes=VMEM_LIMIT),
        name="move",
    )(result)


def solution(mesh):
    placed = (
        P(None, ("row", "col"), None),
        P(None, None, ("row", "col"), None),
        P(None, ("row", "col")),
        P(),
        P(),
    )
    return jax.shard_map(
        per_device,
        mesh=mesh,
        in_specs=placed,
        out_specs=P(None, ("row", "col"), None),
        check_vma=False,
    )
```
